128 devices in a mesh: pipe: 2 (over z_lo), dp: 32 (over x, y, core), tensor: 2 (over z_hi).
Axes of the slice: x: 4, y: 4, z: 4 (z_hi: 2, z_lo: 2; z = z_hi * 2 + z_lo), core: 2. Of those that a mesh axis runs over, the one named last changes fastest.
Arguments:
- tokens: bfloat16 [64, 256, 768], P('dp', 'tensor'), may hold values from -6 to 6
- cotangent: bfloat16 [64, 256, 768], P('dp', 'tensor'), may hold values from -6 to 6
- routes: int32 [2, 64, 256, 1], P('pipe', 'dp', 'tensor'), may hold values from 0 to 3; in each aligned block of 256 rows (0 to 255, 256 to 511, ..., all dimensions but the last counted through in order) at most 88 rows name the same one
- g_attn: bfloat16 [2, 768], P('pipe', 'dp'), may hold values from 0.099609375 to 1.8984375
- w_qkv: bfloat16 [2, 768, 3, 768], P('pipe', 'dp', None, 'tensor'), may hold values from -0.21875 to 0.21875
- w_out: bfloat16 [2, 768, 768], P('pipe', 'dp', 'tensor'), may hold values from -1.75 to 1.75
- g_moe: bfloat16 [2, 768], P('pipe', 'dp'), may hold values from 0.099609375 to 1.8984375
- w_router: bfloat16 [2, 768, 4], P('pipe', 'dp'), may hold values from -0.15625 to 0.15625
- w_in: bfloat16 [2, 4, 768, 3072], P('pipe', None, 'dp', 'tensor'), may hold values from -0.21875 to 0.21875
- w_down: bfloat16 [2, 4, 768, 3072], P('pipe', None, 'dp', 'tensor'), may hold values from -0.4375 to 0.4375
Outputs:
- hidden_states: bfloat16 [2, 64, 256, 768], P('pipe', 'dp', 'tensor')
- grad_inputs: float32 [2, 64, 256, 768], P('pipe', 'dp', 'tensor')
- grad_g_attn: float32 [2, 768], P('pipe', 'dp')
- grad_w_qkv: float32 [2, 768, 3, 768], P('pipe', 'dp', None, 'tensor')
- grad_w_out: float32 [2, 768, 768], P('pipe', 'dp', 'tensor')
- grad_g_moe: float32 [2, 768], P('pipe', 'dp')
- grad_w_router: float32 [2, 768, 4], P('pipe', 'dp')
- grad_w_in: float32 [2, 4, 768, 3072], P('pipe', None, 'dp', 'tensor')
- grad_w_down: float32 [2, 4, 768, 3072], P('pipe', None, 'dp', 'tensor')
The draws below stay inside these ranges and needn't reach their ends.
Inputs may be any that keep to these rules, and one draw needn't show every extreme that they name: `routes`: within the 256 tokens of one sequence of a layer no expert is named more than 88 times; in some sequences one expert is named exactly 88 times.
All inputs are finite; a program needn't handle non-finite values.
Results may differ from the reference program's by a relative error of at most 0.033.
Values may be sent and summed in bfloat16 or wider, within the bound.
No kernel may reach another device: no remote copies, remote signals or barrier semaphores. Data moves between devices by JAX's collectives and lax.ppermute only.
A program may use at most 256 MiB of HBM per device.

```python
import math
import jax
import jax.numpy as jnp
import numpy as np
from jax import lax

D = 768
H = 12
DH = 64
FF = 3072
E = 4
LEN = 256
CAP = 88
SEQS = 64


def block_levels(own_key, shape, cuts, least, largest):
    factor_of = 1.0
    for axis_at, shards_of in cuts:
        steps = jax.random.uniform(jax.random.fold_in(jax.random.fold_in(own_key, 6), axis_at), (shards_of,), jnp.float32, least / len(cuts), largest / len(cuts))
        factor_of = factor_of * jnp.repeat(jnp.exp(steps), shape[axis_at] // shards_of).reshape((-1,) + (1,) * (len(shape) - 1 - axis_at))
    return factor_of


def assign_block(rng, own, number, rows, count, top, reach, skew):
    sequence = jax.random.permutation(rng, count)
    heavy_load, common = shares(count, rows * top, reach, skew, True), shares(count, rows * top, reach, skew, False)
    places = jnp.arange(count)

    def named(sizes, offset_by):
        used = int((sizes > 0).sum())
        fixed = max(1, used // 4)
        moved = fixed + (places - fixed + offset_by * (used - fixed)) % max(1, count - fixed)
        return jnp.zeros((count,), jnp.int32).at[sequence[jnp.where(places < fixed, places, moved)]].set(jnp.asarray(sizes, jnp.int32))

    sizes = jnp.where(number % 4 == 0, named(heavy_load, number // 4), named(common, number - number // 4 - 1))
    mixed = jax.random.permutation(jax.random.fold_in(own, 3), count)
    giver, receiver = mixed[0:count // 2 * 2:2], mixed[1:count // 2 * 2:2]
    slack = jnp.minimum(sizes[giver] - 1, reach - sizes[receiver]) // 2
    slack = jnp.where((giver == sequence[0]) | (receiver == sequence[0]) | (sizes[receiver] == 0), 0, jnp.maximum(slack, 0))
    moved = jax.random.randint(jax.random.fold_in(own, 4), (count // 2,), 0, 1 << 20) % (slack + 1)
    sizes = sizes.at[giver].add(-moved).at[receiver].add(moved)
    labels = jnp.searchsorted(jnp.cumsum(sizes), jnp.arange(rows * top), side="right").astype(jnp.int32)
    listing = labels.reshape(top, rows).T
    listing = listing[jax.random.permutation(jax.random.fold_in(own, 1), rows)]
    offset_by = jax.random.randint(jax.random.fold_in(own, 2), (rows, 1), 0, top)
    return jnp.take_along_axis(listing, (jnp.arange(top)[None, :] + offset_by) % top, axis=1)


def shares(count, total, most, lean, full):
    loads = [(1 << 20) // math.isqrt(standing ** lean) + 1 for standing in range(1, count + 1)]
    largest = most if full else min(most, max(-(-total // count), total * loads[0] // sum(loads)))
    least = 1 if total - largest >= count - 1 else 0
    holding, rest = [largest] + [least] * (count - 1), total - largest - least * (count - 1)
    while rest > 0:
        free = [i for i in range(1, count) if holding[i] < largest] or [i for i in range(1, count) if holding[i] < most]
        pool, budget = sum([loads[i] for i in free]), rest
        for i in free:
            more = min(most - holding[i], max(1, budget * loads[i] // pool), rest)
            holding[i] = holding[i] + more
            rest = rest - more
    return np.array(holding)


def gaussian(rng, shape, deviation, reach, pieces=(), kind=jnp.bfloat16):
    values = jax.random.normal(rng, shape, jnp.float32) * deviation
    if len(pieces) > 0:
        values = block_levels(rng, shape, pieces, -0.22, 0.18) * values
    return jnp.clip(values, min=-reach, max=reach).astype(kind)


def setup_inputs(seed: int = 0) -> dict:
    key_list = jax.random.split(jax.random.key(seed), 11)
    tokens = gaussian(key_list[0], (SEQS, LEN, D), 1.0, 6.0, ((0, 32), (1, 2)))
    cotangent = gaussian(key_list[1], (SEQS, LEN, D), 1.0, 6.0, ((0, 32), (1, 2)))
    routes_keys = jax.random.split(jax.random.fold_in(key_list[2], 1), 2 * SEQS * LEN // LEN)
    routes_turns = jax.random.permutation(jax.random.fold_in(key_list[2], 3), 2 * SEQS * LEN // LEN)
    routes = jax.vmap(lambda own, number: assign_block(jax.random.fold_in(key_list[2], 2), own, number, LEN, E, 1, CAP, 1))(routes_keys, routes_turns).reshape((2, SEQS, LEN, 1))
    g_attn = jnp.clip(1.0 + 0.18 * jax.random.normal(key_list[3], (2, D), jnp.float32), 0.099609375, 1.8984375).astype(jnp.bfloat16)
    w_qkv = gaussian(key_list[4], (2, D, 3, H * DH), D ** -0.5, 0.21875, ((0, 2), (1, 32), (3, 2)))
    w_out = gaussian(key_list[5], (2, D, H * DH), (max(H * DH // 64, 1)) ** -0.5, 1.75, ((0, 2), (1, 32), (2, 2)))
    g_moe = jnp.clip(1.0 + 0.18 * jax.random.normal(key_list[6], (2, D), jnp.float32), 0.099609375, 1.8984375).astype(jnp.bfloat16)
    w_router = gaussian(key_list[7], (2, D, E), (D * 16 // 9) ** -0.5, 0.15625, ((0, 2), (1, 32)))
    w_in = gaussian(key_list[8], (2, E, D, FF), D ** -0.5, 0.21875, ((0, 2), (2, 32), (3, 2)))
    w_down = gaussian(key_list[9], (2, E, D, FF), (FF // 16) ** -0.5, 0.4375, ((0, 2), (2, 32), (3, 2)))
    return dict(tokens=tokens, cotangent=cotangent, routes=routes, g_attn=g_attn, w_qkv=w_qkv, w_out=w_out, g_moe=g_moe, w_router=w_router, w_in=w_in, w_down=w_down)


@jax.custom_vjp
def low(v):
    return lax.optimization_barrier(v.astype(jnp.bfloat16)).astype(jnp.float32)

@jax.custom_vjp
def low_back(v):
    return v

def low_keep(v):
    return (low(v), None)

def low_pass(kept, grad):
    return (grad,)

def back_keep(v):
    return (v, None)

def back_low(kept, grad):
    return (low(grad),)
low.defvjp(low_keep, low_pass)
low_back.defvjp(back_keep, back_low)
highest = lax.Precision.HIGHEST
norm_eps = 1e-06

def matmul(left, right):
    return jnp.dot(left, right, precision=highest, preferred_element_type=jnp.float32)

def rms_norm(values, gain):
    scale_rows = lax.rsqrt(lax.optimization_barrier(jnp.mean(values * values, axis=-1, keepdims=True)) + norm_eps)
    return values * scale_rows * gain

def softmax_rows(scores):
    shifted = scores - lax.optimization_barrier(jnp.max(scores, axis=-1, keepdims=True))
    exponent = jnp.exp(shifted)
    return exponent / lax.optimization_barrier(jnp.sum(exponent, axis=-1, keepdims=True))

def slot_index(route_ids):
    onehot = (route_ids[:, None] == jnp.arange(E, dtype=jnp.int32)[None, :]).astype(jnp.int32)
    before = jnp.cumsum(onehot, axis=0) - onehot
    return (route_ids * CAP + lax.optimization_barrier(jnp.sum(before * onehot, axis=1))).astype(jnp.int32)

def encoder_layer(inputs, g_attn, w_qkv, w_out, g_moe, w_router, w_in, w_down, route_ids):
    head_width = H * DH
    normed = low(rms_norm(inputs, g_attn))
    packed = matmul(normed, w_qkv.reshape(D, 3 * head_width))
    query_rows = low_back(low(packed[:, :head_width])).reshape(LEN, H, DH)
    key_rows = low_back(low(packed[:, head_width:2 * head_width])).reshape(LEN, H, DH)
    value_rows = low_back(low(packed[:, 2 * head_width:])).reshape(LEN, H, DH)
    score_scale = 1.0 / math.sqrt(DH)
    scores = low_back(score_scale * jnp.einsum('qhd,khd->hqk', query_rows, key_rows, precision=highest))
    attn_probs = low(softmax_rows(scores))
    context = jnp.einsum('hqk,khd->qhd', attn_probs, value_rows, precision=highest)
    context = low_back(low(context)).reshape(LEN, head_width)
    projected = low_back(jnp.dot(context, w_out.T, precision=highest))
    middle = inputs + projected
    mixed_rows = low(rms_norm(middle, g_moe))
    router_probs = softmax_rows(matmul(mixed_rows, w_router))
    onehot = route_ids[:, None] == jnp.arange(E, dtype=jnp.int32)[None, :]
    gate_prob = lax.optimization_barrier(jnp.sum(jnp.where(onehot, router_probs, jnp.zeros_like(router_probs)), axis=-1))
    slot_ids = slot_index(route_ids)
    filled = jnp.zeros((E * CAP, D), jnp.float32).at[slot_ids].set(mixed_rows).reshape(E, CAP, D)
    hidden = low_back(jnp.einsum('ecd,edf->ecf', filled, w_in, precision=highest))
    activated = low(jax.nn.gelu(hidden, approximate=False))
    expert_out = jnp.einsum('ecf,edf->ecd', activated, w_down, precision=highest).reshape(E * CAP, D)
    combined = low_back(jnp.take(expert_out, slot_ids, axis=0))
    return middle + gate_prob[:, None] * combined

def reference(tokens, cotangent, routes, g_attn, w_qkv, w_out, g_moe, w_router, w_in, w_down):
    weights = [tuple((weight_arg[layer_index].astype(jnp.float32) for weight_arg in (g_attn, w_qkv, w_out, g_moe, w_router, w_in, w_down))) for layer_index in range(2)]

    def sequence_step(totals, item):
        seq_tokens, seq_cot, route_first, route_second = item
        out_first, pull_first = jax.vjp(lambda inputs, *params: encoder_layer(inputs, *params, route_first), seq_tokens.astype(jnp.float32), *weights[0])
        handoff = low(out_first)
        out_second, pull_second = jax.vjp(lambda inputs, *params: encoder_layer(inputs, *params, route_second), handoff, *weights[1])
        grads_second = pull_second(seq_cot.astype(jnp.float32))
        back_middle = low(grads_second[0])
        grads_first = pull_first(back_middle)
        totals = tuple((total + jnp.stack([grad_one, grad_two]) for total, grad_one, grad_two in zip(totals, grads_first[1:], grads_second[1:])))
        return (totals, (handoff, out_second, grads_first[0], back_middle))
    initial = tuple((jnp.zeros((2,) + weight.shape, jnp.float32) for weight in weights[0]))
    items = (tokens, cotangent, routes[0, :, :, 0], routes[1, :, :, 0])
    totals, stacked = lax.scan(sequence_step, initial, items)
    first_out, second_out, first_grad, second_grad = stacked
    hidden_states = jnp.stack([first_out, second_out]).astype(jnp.bfloat16)
    grad_inputs = jnp.stack([first_grad, second_grad])
    return (hidden_states, grad_inputs, totals[0], totals[1], totals[2], totals[3], totals[4], totals[5], totals[6])
```

```python
import math

import jax
import jax.numpy as jnp
from jax import lax
from jax.sharding import Mesh
from jax.sharding import PartitionSpec as P

D = 768
DH = 64
E = 4
LEN = 256
HALF = 128
PAD = 96
QKV = 1152
OUT = 384
SMALL = 256
ATTN = QKV + OUT + SMALL
FFH = 1536

norm_eps = 1e-06
f32 = jnp.float32
bf16 = jnp.bfloat16
COLUMN = ("pipe", "core", "tensor")


def column_pairs(target):
    pairs = []
    for p in range(2):
        for c in range(2):
            for t in range(2):
                p2, c2, t2 = target(p, c, t)
                pairs.append((p * 4 + c * 2 + t, p2 * 4 + c2 * 2 + t2))
    return pairs


def column_send(array, target):
    return lax.ppermute(array, COLUMN, column_pairs(target))


def core_swap(array):
    return lax.ppermute(array, "core", [(0, 1), (1, 0)])


def chip_swap(array, k):
    return lax.ppermute(array, ("pipe", "tensor"), [(i, i ^ k) for i in range(4)])


def axis_swap(array, axis, k):
    return lax.ppermute(array, axis, [(i, i ^ k) for i in range(4)])


def gather_axis(block, axis, dim):
    me = lax.axis_index(axis)
    whole = jnp.zeros(block.shape[:dim] + (4,) + block.shape[dim:], block.dtype)
    parts = [block] + [axis_swap(block, axis, k) for k in (1, 2, 3)]
    for k, part in enumerate(parts):
        whole = lax.dynamic_update_index_in_dim(whole, part, me ^ k, dim)
    return whole


def gather_plane(block, first):
    rows, width = block.shape
    if first == "x":
        whole = gather_axis(gather_axis(block, "x", 0), "y", 1)
    else:
        whole = gather_axis(gather_axis(block, "y", 0), "x", 0)
    return whole.reshape(16 * rows, width)


def scatter_axis(whole, axis, dim):
    me = lax.axis_index(axis)
    parts = [lax.dynamic_index_in_dim(whole, me ^ k, dim, keepdims=False) for k in range(4)]
    got = [parts[0]] + [axis_swap(parts[k], axis, k) for k in (1, 2, 3)]
    return sum(part.astype(f32) for part in got).astype(bf16)


def scatter_plane(whole, first):
    whole = whole.reshape(4, 4, -1, whole.shape[1])
    if first == "x":
        return scatter_axis(scatter_axis(whole, "x", 0), "y", 0)
    return scatter_axis(scatter_axis(whole, "y", 1), "x", 0)


def rms_scale(values):
    return lax.rsqrt(jnp.mean(values * values, axis=-1, keepdims=True) + norm_eps)


def norm_back(grad_normed, values, scale_rows, gain):
    normal = values * scale_rows
    weighted = grad_normed * gain
    grad_values = scale_rows * (
        weighted - normal * jnp.mean(weighted * normal, axis=-1, keepdims=True)
    )
    return grad_values, jnp.sum(grad_normed * normal, axis=0)


def matmul(left, right, dims):
    return lax.dot_general(left, right, ((dims[:1], dims[1:]), ((), ())), preferred_element_type=f32)


def pair_sum(partial):
    mine = partial.astype(bf16)
    return mine.astype(f32) + core_swap(mine).astype(f32)


def to_experts(rows):
    parts = [rows[k * PAD : (k + 1) * PAD] for k in range(4)]
    return jnp.concatenate([parts[0]] + [chip_swap(parts[k], k) for k in (1, 2, 3)], axis=0)


def unpack(packed):
    return [
        packed[:, i * OUT : (i + 1) * OUT].astype(bf16).reshape(LEN, OUT // DH, DH)
        for i in range(3)
    ]


def forward(inputs, table, onehot, weights):
    w_qkv, w_out, g_attn, g_moe, w_router, w_in, w_down = weights
    score_scale = 1.0 / math.sqrt(DH)
    scale_in = rms_scale(inputs)
    normed = (inputs * scale_in * g_attn).astype(bf16)
    query, key, value = unpack(matmul(normed, w_qkv, (1, 0)))
    scores = jnp.einsum("qhd,khd->hqk", query, key, preferred_element_type=f32) * score_scale
    top = jnp.max(scores, axis=-1, keepdims=True)
    exponent = jnp.exp(scores - top)
    probs = exponent / jnp.sum(exponent, axis=-1, keepdims=True)
    context = jnp.einsum("hqk,khd->qhd", probs.astype(bf16), value, preferred_element_type=f32)
    context = context.astype(bf16).reshape(LEN, OUT)
    middle = inputs + pair_sum(matmul(context, w_out, (1, 1)))
    scale_mid = rms_scale(middle)
    mixed = (middle * scale_mid * g_moe).astype(bf16)
    logits = matmul(mixed, w_router, (1, 0))
    exponent = jnp.exp(logits - jnp.max(logits, axis=-1, keepdims=True))
    router_probs = exponent / jnp.sum(exponent, axis=-1, keepdims=True)
    gate = jnp.sum(onehot * router_probs, axis=-1, keepdims=True)
    filled = to_experts(matmul(table, mixed, (1, 0)).astype(bf16))
    hidden = matmul(filled, w_in, (1, 0))
    cdf = 0.5 * (1.0 + lax.erf(hidden * (1.0 / math.sqrt(2.0))))
    activated = (hidden * cdf).astype(bf16)
    slope = cdf + hidden * jnp.exp(-0.5 * hidden * hidden) * (1.0 / math.sqrt(2.0 * math.pi))
    expert_out = to_experts(matmul(activated, w_down, (1, 1)).astype(bf16))
    combined = pair_sum(matmul(table, expert_out, (0, 0)))
    output = (middle + gate * combined).astype(bf16)
    kept = (
        inputs, scale_in, normed, query, key, value, probs, context, middle, scale_mid,
        mixed, router_probs, gate, filled, activated, slope, combined,
    )
    return output, kept


def backward_moe(grad_out, kept, table, onehot, weights):
    w_qkv, w_out, g_attn, g_moe, w_router, w_in, w_down = weights
    (
        inputs, scale_in, normed, query, key, value, probs, context, middle, scale_mid,
        mixed, router_probs, gate, filled, activated, slope, combined,
    ) = kept
    grad_gate = jnp.sum(grad_out * combined, axis=-1, keepdims=True)
    grad_branch = (gate * grad_out).astype(bf16)
    grad_slots = to_experts(matmul(table, grad_branch, (1, 0)).astype(bf16))
    grad_act = matmul(grad_slots, w_down, (1, 0))
    grad_hidden = (grad_act * slope).astype(bf16)
    grad_filled = to_experts(matmul(grad_hidden, w_in, (1, 1)).astype(bf16))
    grad_w_down = matmul(grad_slots, activated, (0, 0)).astype(bf16)
    grad_w_in = matmul(filled, grad_hidden, (0, 0)).astype(bf16)
    grad_mixed = pair_sum(matmul(table, grad_filled, (0, 0)))
    grad_logits = router_probs * (onehot - gate) * grad_gate
    grad_w_router = lax.dot_general(
        mixed.astype(f32), grad_logits, (((0,), (0,)), ((), ())), precision=lax.Precision.HIGHEST
    )
    back_rows = sum(grad_logits[:, e : e + 1] * w_router[:, e].astype(f32)[None, :] for e in range(E))
    grad_norm, grad_g_moe = norm_back(grad_mixed + back_rows, middle, scale_mid, g_moe)
    return grad_out + grad_norm, grad_w_in, grad_w_down, grad_w_router, grad_g_moe


def backward_attn(grad_middle, kept, weights):
    w_qkv, w_out, g_attn, g_moe, w_router, w_in, w_down = weights
    (
        inputs, scale_in, normed, query, key, value, probs, context, middle, scale_mid,
        mixed, router_probs, gate, filled, activated, slope, combined,
    ) = kept
    score_scale = 1.0 / math.sqrt(DH)
    proj = grad_middle.astype(bf16)
    grad_heads = matmul(proj, w_out, (1, 0)).astype(bf16).reshape(LEN, OUT // DH, DH)
    grad_value = jnp.einsum(
        "hqk,qhd->khd", probs.astype(bf16), grad_heads, preferred_element_type=f32
    ).astype(bf16)
    grad_probs = jnp.einsum("qhd,khd->hqk", grad_heads, value, preferred_element_type=f32)
    grad_scores = (
        probs * (grad_probs - jnp.sum(grad_probs * probs, axis=-1, keepdims=True))
    ).astype(bf16)
    grad_query = (
        jnp.einsum("hqk,khd->qhd", grad_scores, key, preferred_element_type=f32) * score_scale
    ).astype(bf16)
    grad_key = (
        jnp.einsum("hqk,qhd->khd", grad_scores, query, preferred_element_type=f32) * score_scale
    ).astype(bf16)
    packed = jnp.concatenate(
        [grad_query.reshape(LEN, OUT), grad_key.reshape(LEN, OUT), grad_value.reshape(LEN, OUT)],
        axis=1,
    )
    grad_normed = pair_sum(matmul(packed, w_qkv, (1, 1)))
    grad_w_out = matmul(proj, context, (0, 0)).astype(bf16)
    grad_w_qkv = matmul(normed, packed, (0, 0)).astype(bf16)
    grad_norm, grad_g_attn = norm_back(grad_normed, inputs, scale_in, g_attn)
    return grad_middle + grad_norm, grad_w_qkv, grad_w_out, grad_g_attn


def by_layer(p, near, far):
    return jnp.where(p == 0, near, far), jnp.where(p == 0, far, near)


def on_device(tokens, cotangent, routes, g_attn, w_qkv, w_out, g_moe, w_router, w_in, w_down):
    p, c, t = lax.axis_index("pipe"), lax.axis_index("core"), lax.axis_index("tensor")
    chip = p * 2 + t

    def spread(chunk_of):
        got = []
        for k in range(4):
            k1, k0 = k >> 1, k & 1
            got.append(column_send(chunk_of(k), lambda p, c, t: (p ^ k1, t, c ^ k0)))
        layers = []
        for first, second in ((by_layer(p, got[0], got[2])), (by_layer(p, got[1], got[3]))):
            layers.append((first, second))
        return [
            jnp.concatenate(
                [
                    jnp.where(t == 0, layers[0][l], layers[1][l]),
                    jnp.where(t == 0, layers[1][l], layers[0][l]),
                ],
                axis=0,
            )
            for l in range(2)
        ]

    def expert_chunk(k):
        expert = (p * 2 + c) ^ k
        return jnp.concatenate(
            [
                lax.dynamic_index_in_dim(w_in[0], expert, 0, keepdims=False),
                lax.dynamic_index_in_dim(w_down[0], expert, 0, keepdims=False),
            ],
            axis=1,
        )

    moe_blocks = spread(expert_chunk)
    small = jnp.concatenate([g_attn[0][:, None], g_moe[0][:, None], w_router[0]], axis=1)
    small = jnp.pad(small, ((0, 0), (0, SMALL - small.shape[1])))
    attn_chunk = jnp.concatenate([w_qkv[0].reshape(-1, QKV), w_out[0], small], axis=1)
    attn_blocks = spread(lambda k: attn_chunk)

    def to_owner(rows):
        got = [column_send(rows, lambda p, c, t, j=j: (p, t ^ j, c)) for j in range(2)]
        return jnp.where(c == 0, got[0], got[1]), jnp.where(c == 0, got[1], got[0])

    own_routes = routes[0, :, :, 0].astype(bf16)
    far_routes = lax.ppermute(own_routes, "pipe", [(0, 1), (1, 0)])
    route_pair = jnp.stack(by_layer(p, own_routes, far_routes))
    route_rows = lax.dynamic_index_in_dim(route_pair, p, 1, keepdims=False)
    own_tokens = lax.dynamic_index_in_dim(tokens, p, 0, keepdims=False)
    extra = jnp.pad(route_rows.reshape(1, 2 * HALF), ((0, 15), (0, D - 2 * HALF)))
    low_rows, high_rows = to_owner(jnp.concatenate([own_tokens, extra], axis=0))
    inputs = jnp.concatenate([low_rows[:HALF], high_rows[:HALF]], axis=0).astype(f32)
    tables, onehots = [], []
    earlier = (
        lax.broadcasted_iota(jnp.int32, (LEN, LEN), 0)
        < lax.broadcasted_iota(jnp.int32, (LEN, LEN), 1)
    ).astype(bf16)
    for l in range(2):
        cut = slice(l * HALF, (l + 1) * HALF)
        ids = jnp.concatenate([low_rows[HALF, cut], high_rows[HALF, cut]]).astype(jnp.int32)
        picks = (ids[None, :] == jnp.arange(E, dtype=jnp.int32)[:, None]).astype(f32)
        before = matmul(picks.astype(bf16), earlier, (1, 0))
        rank = jnp.sum(before * picks, axis=0).astype(jnp.int32)
        place = (ids ^ chip) * PAD + rank
        tables.append(
            (place[None, :] == jnp.arange(E * PAD, dtype=jnp.int32)[:, None]).astype(bf16)
        )
        onehots.append(picks.T)

    moe_full = lax.all_gather(
        jnp.concatenate(moe_blocks, axis=1), ("x", "y"), axis=0, tiled=True
    )
    attn_full = [gather_plane(attn_blocks[0], "x"), gather_plane(attn_blocks[1], "y")]

    def weights_of(attn, w_in_full, w_down_full):
        small = attn[:, QKV + OUT :]
        return (
            attn[:, :QKV],
            attn[:, QKV : QKV + OUT],
            small[:, 0].astype(f32)[None, :],
            small[:, 1].astype(f32)[None, :],
            small[:, 2 : 2 + E],
            w_in_full,
            w_down_full,
        )

    weights = [
        weights_of(
            attn_full[l],
            moe_full[:, 2 * l * FFH : (2 * l + 1) * FFH],
            moe_full[:, (2 * l + 1) * FFH : (2 * l + 2) * FFH],
        )
        for l in range(2)
    ]

    cot_rows = lax.dynamic_index_in_dim(cotangent, p, 0, keepdims=False)
    grad_out = jnp.concatenate(to_owner(cot_rows), axis=0).astype(f32)

    first_out, kept_first = forward(inputs, tables[0], onehots[0], weights[0])
    second_out, kept_second = forward(first_out.astype(f32), tables[1], onehots[1], weights[1])

    def to_home(first, second):
        cut = lambda rows: lax.dynamic_slice_in_dim(rows, c * HALF, HALF, 0)
        near, far = by_layer(p, cut(first), cut(second))
        near = column_send(near, lambda p, c, t: (p, t, c))
        far = column_send(far, lambda p, c, t: (1 - p, t, c))
        return jnp.stack(by_layer(p, near, far))

    hidden_states = to_home(first_out, second_out)

    def small_grads(grad_g_attn, grad_g_moe, grad_w_router):
        rows = jnp.concatenate([grad_g_attn[:, None], grad_g_moe[:, None], grad_w_router], axis=1)
        return jnp.pad(rows, ((0, 0), (0, SMALL - rows.shape[1]))).astype(bf16)

    grad_mid, g_in, g_down, g_router, gg_moe = backward_moe(
        grad_out, kept_second, tables[1], onehots[1], weights[1]
    )
    grad_x, g_qkv, g_out, gg_attn = backward_attn(grad_mid, kept_second, weights[1])
    second_grad = grad_x.astype(bf16)
    second_parts = [g_qkv, g_out, small_grads(gg_attn, gg_moe, g_router), g_in, g_down]
    grad_mid, g_in, g_down, g_router, gg_moe = backward_moe(
        second_grad.astype(f32), kept_first, tables[0], onehots[0], weights[0]
    )
    reduced = lax.psum_scatter(
        jnp.concatenate(second_parts + [g_in, g_down], axis=1),
        ("x", "y"), scatter_dimension=0, tiled=True,
    )
    reduced = lax.optimization_barrier(reduced)
    grad_x, g_qkv, g_out, gg_attn = backward_attn(grad_mid, kept_first, weights[0])
    attn_first = jnp.concatenate(
        [
            scatter_plane(g_qkv[:, : 2 * OUT], "x"),
            scatter_plane(
                jnp.concatenate(
                    [g_qkv[:, 2 * OUT :], g_out, small_grads(gg_attn, gg_moe, g_router)], axis=1
                ),
                "y",
            ),
        ],
        axis=1,
    )
    grad_inputs = to_home(grad_x.astype(bf16), second_grad).astype(f32)

    near, far = by_layer(
        p,
        jnp.concatenate([attn_first, reduced[:, ATTN + 2 * FFH :]], axis=1),
        reduced[:, : ATTN + 2 * FFH],
    )
    attn_sum = jnp.zeros((24, ATTN), f32)
    moe_all = jnp.zeros((E, 24, 2 * FFH), bf16)
    for k in range(4):
        k1, k0 = k >> 1, k & 1
        layer_rows = far if k1 else near
        piece = lax.dynamic_slice_in_dim(layer_rows, (t ^ k0) * 24, 24, 0)
        got = column_send(piece, lambda p, c, t: (p ^ k1, t ^ k0, c))
        attn_sum = attn_sum + got[:, :ATTN].astype(f32)
        moe_all = lax.dynamic_update_index_in_dim(moe_all, got[:, ATTN:], (p * 2 + c) ^ k, 0)
    small = attn_sum[:, QKV + OUT :]
    return (
        hidden_states[None],
        grad_inputs[None],
        small[:, 0][None],
        attn_sum[:, :QKV].reshape(24, 3, OUT)[None],
        attn_sum[:, QKV : QKV + OUT][None],
        small[:, 1][None],
        small[:, 2 : 2 + E][None],
        moe_all[:, :, :FFH].astype(f32)[None],
        moe_all[:, :, FFH:].astype(f32)[None],
    )


def solution(mesh):
    grid = Mesh(mesh.devices.reshape(2, 4, 4, 2, 2), ("pipe", "x", "y", "core", "tensor"))
    dp = ("x", "y", "core")
    return jax.shard_map(
        on_device,
        mesh=grid,
        in_specs=(
            P(dp, "tensor", None),
            P(dp, "tensor", None),
            P("pipe", dp, "tensor", None),
            P("pipe", dp),
            P("pipe", dp, None, "tensor"),
            P("pipe", dp, "tensor"),
            P("pipe", dp),
            P("pipe", dp, None),
            P("pipe", None, dp, "tensor"),
            P("pipe", None, dp, "tensor"),
        ),
        out_specs=(
            P("pipe", dp, "tensor", None),
            P("pipe", dp, "tensor", None),
            P("pipe", dp),
            P("pipe", dp, None, "tensor"),
            P("pipe", dp, "tensor"),
            P("pipe", dp),
            P("pipe", dp, None),
            P("pipe", None, dp, "tensor"),
            P("pipe", None, dp, "tensor"),
        ),
        check_vma=False,
    )
```

```python
import math

import jax
import jax.numpy as jnp
from jax import lax
from jax.experimental import pallas as pl
from jax.experimental.pallas import tpu as pltpu
from jax.sharding import Mesh
from jax.sharding import PartitionSpec as P

D = 768
DH = 64
E = 4
LEN = 256
HALF = 128
PAD = 96
QKV = 1152
OUT = 384
SMALL = 256
ATTN = QKV + OUT + SMALL
FFH = 1536
BOTH = ATTN + 2 * FFH

norm_eps = 1e-06
f32 = jnp.float32
bf16 = jnp.bfloat16
COLUMN = ("pipe", "core", "tensor")


def column_pairs(target):
    pairs = []
    for p in range(2):
        for c in range(2):
            for t in range(2):
                p2, c2, t2 = target(p, c, t)
                pairs.append((p * 4 + c * 2 + t, p2 * 4 + c2 * 2 + t2))
    return pairs


def column_send(array, target):
    return lax.ppermute(array, COLUMN, column_pairs(target))


def core_swap(array):
    return lax.ppermute(array, "core", [(0, 1), (1, 0)])


def chip_swap(array, k):
    return lax.ppermute(array, ("pipe", "tensor"), [(i, i ^ k) for i in range(4)])


def axis_swap(array, axis, k):
    return lax.ppermute(array, axis, [(i, i ^ k) for i in range(4)])


def scatter_axis(whole, axis, dim):
    me = lax.axis_index(axis)
    parts = [lax.dynamic_index_in_dim(whole, me ^ k, dim, keepdims=False) for k in range(4)]
    got = [parts[0]] + [axis_swap(parts[k], axis, k) for k in (1, 2, 3)]
    return sum(part.astype(f32) for part in got).astype(bf16)


def scatter_first(whole, axis):
    return scatter_axis(whole.reshape(4, 4, -1, whole.shape[1]), axis, "xy".index(axis))


def rms_scale(values):
    return lax.rsqrt(jnp.mean(values * values, axis=-1, keepdims=True) + norm_eps)


def norm_back(grad_normed, values, scale_rows, gain):
    normal = values * scale_rows
    weighted = grad_normed * gain
    grad_values = scale_rows * (
        weighted - normal * jnp.mean(weighted * normal, axis=-1, keepdims=True)
    )
    return grad_values, jnp.sum(grad_normed * normal, axis=0)


def matmul(left, right, dims):
    return lax.dot_general(left, right, ((dims[:1], dims[1:]), ((), ())), preferred_element_type=f32)


def pair_sum(partial):
    mine = partial.astype(bf16)
    return mine.astype(f32) + core_swap(mine).astype(f32)


def to_experts(rows):
    parts = [rows[k * PAD : (k + 1) * PAD] for k in range(4)]
    return jnp.concatenate([parts[0]] + [chip_swap(parts[k], k) for k in (1, 2, 3)], axis=0)


PAIR = 2 * DH
SCALE = 1.0 / math.sqrt(DH)


def dot(left, right, dims):
    return lax.dot_general(left, right, ((dims[:1], dims[1:]), ((), ())), preferred_element_type=f32)


def first_head():
    return lax.broadcasted_iota(jnp.int32, (LEN, PAIR), 1) < DH


def head_probs(query, key):
    scores = dot(query, key, (1, 1)) * SCALE
    exponent = jnp.exp(scores - jnp.max(scores, axis=-1, keepdims=True))
    return exponent / jnp.sum(exponent, axis=-1, keepdims=True)


def attend_kernel(x_ref, gain_ref, attn_ref, part_ref, normed_ref, packed_ref, context_ref):
    values = x_ref[...]
    scale = lax.rsqrt(jnp.mean(values * values, axis=-1, keepdims=True) + norm_eps)
    normed = (values * scale * gain_ref[...]).astype(bf16)
    normed_ref[...] = normed
    packed_ref[...] = dot(normed, attn_ref[:, :QKV], (1, 0)).astype(bf16)
    low = first_head()
    for pair in range(OUT // PAIR):
        at = pair * PAIR
        query = packed_ref[:, at : at + PAIR]
        key = packed_ref[:, OUT + at : OUT + at + PAIR]
        value = packed_ref[:, 2 * OUT + at : 2 * OUT + at + PAIR]
        none = jnp.zeros_like(query)
        parts = []
        for head in range(2):
            mine = low if head == 0 else ~low
            probs = head_probs(jnp.where(mine, query, none), key).astype(bf16)
            parts.append(dot(probs, value, (1, 0)))
        context_ref[:, at : at + PAIR] = jnp.where(low, parts[0], parts[1]).astype(bf16)
    part_ref[...] = dot(context_ref[...], attn_ref[:, QKV : QKV + OUT], (1, 1)).astype(bf16)


def attend(inputs, gain, attn):
    shape = jax.ShapeDtypeStruct
    return pl.pallas_call(
        attend_kernel,
        out_shape=(
            shape((LEN, D), bf16),
            shape((LEN, D), bf16),
            shape((LEN, QKV), bf16),
            shape((LEN, OUT), bf16),
        ),
        compiler_params=pltpu.CompilerParams(vmem_limit_bytes=24 * 2**20),
        cost_estimate=pl.CostEstimate(
            flops=2 * LEN * D * (QKV + OUT), bytes_accessed=6 * 2**20, transcendentals=6 * LEN * LEN
        ),
        name="attend",
    )(inputs, gain, attn)


def attend_back_kernel(grad_ref, attn_ref, packed_ref, part_ref, grads_ref, heads_ref):
    heads_ref[...] = dot(grad_ref[...], attn_ref[:, QKV : QKV + OUT], (1, 0)).astype(bf16)
    low = first_head()
    for pair in range(OUT // PAIR):
        at = pair * PAIR
        query = packed_ref[:, at : at + PAIR]
        key = packed_ref[:, OUT + at : OUT + at + PAIR]
        value = packed_ref[:, 2 * OUT + at : 2 * OUT + at + PAIR]
        grad = heads_ref[:, at : at + PAIR]
        none = jnp.zeros_like(query)
        found = []
        for head in range(2):
            mine = low if head == 0 else ~low
            probs = head_probs(jnp.where(mine, query, none), key)
            grad_probs = dot(jnp.where(mine, grad, none), value, (1, 1))
            inner = jnp.sum(grad_probs * probs, axis=-1, keepdims=True)
            grad_scores = (probs * (grad_probs - inner)).astype(bf16)
            found.append(
                (
                    dot(grad_scores, key, (1, 0)) * SCALE,
                    dot(grad_scores, query, (0, 0)) * SCALE,
                    dot(probs.astype(bf16), grad, (0, 0)),
                )
            )
        for j in range(3):
            both = jnp.where(low, found[0][j], found[1][j]).astype(bf16)
            grads_ref[:, j * OUT + at : j * OUT + at + PAIR] = both
    part_ref[...] = dot(grads_ref[...], attn_ref[:, :QKV], (1, 1)).astype(bf16)


def attend_back(grad, attn, packed):
    shape = jax.ShapeDtypeStruct
    return pl.pallas_call(
        attend_back_kernel,
        out_shape=(shape((LEN, D), bf16), shape((LEN, QKV), bf16)),
        scratch_shapes=[pltpu.VMEM((LEN, OUT), bf16)],
        compiler_params=pltpu.CompilerParams(vmem_limit_bytes=24 * 2**20),
        cost_estimate=pl.CostEstimate(
            flops=2 * LEN * D * (QKV + OUT), bytes_accessed=6 * 2**20, transcendentals=6 * LEN * LEN
        ),
        name="attend_back",
    )(grad, attn, packed)


def forward(inputs, table, onehot, weights):
    attn, g_attn, g_moe, w_router, w_in, w_down = weights
    part, normed, packed, context = attend(inputs, g_attn, attn)
    middle = inputs + pair_sum(part)
    scale_mid = rms_scale(middle)
    mixed = (middle * scale_mid * g_moe).astype(bf16)
    logits = matmul(mixed, w_router, (1, 0))
    exponent = jnp.exp(logits - jnp.max(logits, axis=-1, keepdims=True))
    router_probs = exponent / jnp.sum(exponent, axis=-1, keepdims=True)
    gate = jnp.sum(onehot * router_probs, axis=-1, keepdims=True)
    filled = to_experts(matmul(table, mixed, (1, 0)).astype(bf16))
    hidden = matmul(filled, w_in, (1, 0))
    cdf = 0.5 * (1.0 + lax.erf(hidden * (1.0 / math.sqrt(2.0))))
    activated = (hidden * cdf).astype(bf16)
    slope = cdf + hidden * jnp.exp(-0.5 * hidden * hidden) * (1.0 / math.sqrt(2.0 * math.pi))
    expert_out = to_experts(matmul(activated, w_down, (1, 1)).astype(bf16))
    combined = pair_sum(matmul(table, expert_out, (0, 0)))
    output = (middle + gate * combined).astype(bf16)
    kept = (
        inputs, normed, packed, context, middle, scale_mid,
        mixed, router_probs, gate, filled, activated, slope, combined,
    )
    return output, kept


def backward_moe(grad_out, kept, table, onehot, weights):
    attn, g_attn, g_moe, w_router, w_in, w_down = weights
    (
        inputs, normed, packed, context, middle, scale_mid,
        mixed, router_probs, gate, filled, activated, slope, combined,
    ) = kept
    grad_gate = jnp.sum(grad_out * combined, axis=-1, keepdims=True)
    grad_branch = (gate * grad_out).astype(bf16)
    grad_slots = to_experts(matmul(table, grad_branch, (1, 0)).astype(bf16))
    grad_act = matmul(grad_slots, w_down, (1, 0))
    grad_hidden = (grad_act * slope).astype(bf16)
    grad_filled = to_experts(matmul(grad_hidden, w_in, (1, 1)).astype(bf16))
    grad_w_down = matmul(grad_slots, activated, (0, 0)).astype(bf16)
    grad_w_in = matmul(filled, grad_hidden, (0, 0)).astype(bf16)
    grad_mixed = pair_sum(matmul(table, grad_filled, (0, 0)))
    grad_logits = router_probs * (onehot - gate) * grad_gate
    grad_w_router = lax.dot_general(
        mixed.astype(f32), grad_logits, (((0,), (0,)), ((), ())), precision=lax.Precision.HIGHEST
    )
    back_rows = sum(grad_logits[:, e : e + 1] * w_router[:, e].astype(f32)[None, :] for e in range(E))
    grad_norm, grad_g_moe = norm_back(grad_mixed + back_rows, middle, scale_mid, g_moe)
    return grad_out + grad_norm, grad_w_in, grad_w_down, grad_w_router, grad_g_moe


def backward_attn(grad_middle, kept, weights):
    attn, g_attn, g_moe, w_router, w_in, w_down = weights
    (
        inputs, normed, packed, context, middle, scale_mid,
        mixed, router_probs, gate, filled, activated, slope, combined,
    ) = kept
    proj = grad_middle.astype(bf16)
    part, grads = attend_back(proj, attn, packed)
    grad_normed = pair_sum(part)
    grad_w_out = matmul(proj, context, (0, 0)).astype(bf16)
    grad_w_qkv = matmul(normed, grads, (0, 0)).astype(bf16)
    grad_norm, grad_g_attn = norm_back(grad_normed, inputs, rms_scale(inputs), g_attn)
    return grad_middle + grad_norm, grad_w_qkv, grad_w_out, grad_g_attn


def by_layer(p, near, far):
    return jnp.where(p == 0, near, far), jnp.where(p == 0, far, near)


def on_device(tokens, cotangent, routes, g_attn, w_qkv, w_out, g_moe, w_router, w_in, w_down):
    p, c, t = lax.axis_index("pipe"), lax.axis_index("core"), lax.axis_index("tensor")
    chip = p * 2 + t

    def spread(chunk_of):
        got = []
        for k in range(4):
            k1, k0 = k >> 1, k & 1
            got.append(column_send(chunk_of(k), lambda p, c, t: (p ^ k1, t, c ^ k0)))
        layers = []
        for first, second in ((by_layer(p, got[0], got[2])), (by_layer(p, got[1], got[3]))):
            layers.append((first, second))
        return [
            jnp.concatenate(
                [
                    jnp.where(t == 0, layers[0][l], layers[1][l]),
                    jnp.where(t == 0, layers[1][l], layers[0][l]),
                ],
                axis=0,
            )
            for l in range(2)
        ]

    small = jnp.concatenate([g_attn[0][:, None], g_moe[0][:, None], w_router[0]], axis=1)
    small = jnp.pad(small, ((0, 0), (0, SMALL - small.shape[1])))

    def chunk_of(k):
        expert = (p * 2 + c) ^ k
        return jnp.concatenate(
            [
                w_qkv[0].reshape(-1, QKV),
                w_out[0],
                small,
                lax.dynamic_index_in_dim(w_in[0], expert, 0, keepdims=False),
                lax.dynamic_index_in_dim(w_down[0], expert, 0, keepdims=False),
            ],
            axis=1,
        )

    blocks = spread(chunk_of)
    early = lax.all_gather(
        jnp.concatenate([blocks[0], blocks[1][:, :ATTN]], axis=1), ("x", "y"), axis=0, tiled=True
    )
    late = lax.all_gather(blocks[1][:, ATTN:], ("x", "y"), axis=0, tiled=True)

    def to_owner(rows):
        got = [column_send(rows, lambda p, c, t, j=j: (p, t ^ j, c)) for j in range(2)]
        return jnp.where(c == 0, got[0], got[1]), jnp.where(c == 0, got[1], got[0])

    own_routes = routes[0, :, :, 0].astype(bf16)
    far_routes = lax.ppermute(own_routes, "pipe", [(0, 1), (1, 0)])
    route_pair = jnp.stack(by_layer(p, own_routes, far_routes))
    route_rows = lax.dynamic_index_in_dim(route_pair, p, 1, keepdims=False)
    own_tokens = lax.dynamic_index_in_dim(tokens, p, 0, keepdims=False)
    extra = jnp.pad(route_rows.reshape(1, 2 * HALF), ((0, 15), (0, D - 2 * HALF)))
    low_rows, high_rows = to_owner(jnp.concatenate([own_tokens, extra], axis=0))
    inputs = jnp.concatenate([low_rows[:HALF], high_rows[:HALF]], axis=0).astype(f32)
    tables, onehots = [], []
    earlier = (
        lax.broadcasted_iota(jnp.int32, (LEN, LEN), 0)
        < lax.broadcasted_iota(jnp.int32, (LEN, LEN), 1)
    ).astype(bf16)
    for l in range(2):
        cut = slice(l * HALF, (l + 1) * HALF)
        ids = jnp.concatenate([low_rows[HALF, cut], high_rows[HALF, cut]]).astype(jnp.int32)
        picks = (ids[None, :] == jnp.arange(E, dtype=jnp.int32)[:, None]).astype(f32)
        before = matmul(picks.astype(bf16), earlier, (1, 0))
        rank = jnp.sum(before * picks, axis=0).astype(jnp.int32)
        place = (ids ^ chip) * PAD + rank
        tables.append(
            (place[None, :] == jnp.arange(E * PAD, dtype=jnp.int32)[:, None]).astype(bf16)
        )
        onehots.append(picks.T)

    def weights_of(attn, w_in_full, w_down_full):
        small = attn[:, QKV + OUT :]
        return (
            attn,
            small[:, 0].astype(f32)[None, :],
            small[:, 1].astype(f32)[None, :],
            small[:, 2 : 2 + E],
            w_in_full,
            w_down_full,
        )

    weights = [
        weights_of(early[:, :ATTN], early[:, ATTN : ATTN + FFH], early[:, ATTN + FFH : BOTH]),
        weights_of(early[:, BOTH:], late[:, :FFH], late[:, FFH:]),
    ]

    cot_rows = lax.dynamic_index_in_dim(cotangent, p, 0, keepdims=False)
    grad_out = jnp.concatenate(to_owner(cot_rows), axis=0).astype(f32)

    first_out, kept_first = forward(inputs, tables[0], onehots[0], weights[0])
    second_out, kept_second = forward(first_out.astype(f32), tables[1], onehots[1], weights[1])

    def to_home(first, second):
        cut = lambda rows: lax.dynamic_slice_in_dim(rows, c * HALF, HALF, 0)
        near, far = by_layer(p, cut(first), cut(second))
        near = column_send(near, lambda p, c, t: (p, t, c))
        far = column_send(far, lambda p, c, t: (1 - p, t, c))
        return jnp.stack(by_layer(p, near, far))

    hidden_states = to_home(first_out, second_out)

    def small_grads(grad_g_attn, grad_g_moe, grad_w_router):
        rows = jnp.concatenate([grad_g_attn[:, None], grad_g_moe[:, None], grad_w_router], axis=1)
        return jnp.pad(rows, ((0, 0), (0, SMALL - rows.shape[1]))).astype(bf16)

    grad_mid, g_in, g_down, g_router, gg_moe = backward_moe(
        grad_out, kept_second, tables[1], onehots[1], weights[1]
    )
    grad_x, g_qkv, g_out, gg_attn = backward_attn(grad_mid, kept_second, weights[1])
    second_grad = grad_x.astype(bf16)
    second_all = lax.psum_scatter(
        jnp.concatenate(
            [g_qkv, g_out, small_grads(gg_attn, gg_moe, g_router), g_in, g_down], axis=1
        ),
        ("x", "y"), scatter_dimension=0, tiled=True,
    )
    second_all = lax.optimization_barrier(second_all)
    grad_mid, g_in, g_down, g_router, gg_moe = backward_moe(
        second_grad.astype(f32), kept_first, tables[0], onehots[0], weights[0]
    )
    in_part, down_part = scatter_first(g_in, "x"), scatter_first(g_down, "y")
    grad_x, g_qkv, g_out, gg_attn = backward_attn(grad_mid, kept_first, weights[0])
    qk_part = scatter_first(g_qkv[:, : 2 * OUT], "x")
    rest_part = scatter_first(
        jnp.concatenate(
            [g_qkv[:, 2 * OUT :], g_out, small_grads(gg_attn, gg_moe, g_router)], axis=1
        ),
        "y",
    )
    over_x = scatter_axis(jnp.concatenate([qk_part, in_part], axis=2), "y", 0)
    over_y = scatter_axis(jnp.concatenate([rest_part, down_part], axis=2), "x", 0)
    cut = 2 * OUT
    first_all = jnp.concatenate(
        [over_x[:, :cut], over_y[:, : ATTN - cut], over_x[:, cut:], over_y[:, ATTN - cut :]], axis=1
    )
    grad_inputs = to_home(grad_x.astype(bf16), second_grad).astype(f32)

    attn_sum = jnp.zeros((24, ATTN), f32)
    moe_all = jnp.zeros((E, 24, 2 * FFH), bf16)
    for k in range(4):
        k1, k0 = k >> 1, k & 1
        got = None
        for l, layer_rows in ((1, second_all), (0, first_all)):
            piece = lax.dynamic_slice_in_dim(layer_rows, (t ^ k0) * 24, 24, 0)
            pairs = [
                pair
                for pair in column_pairs(lambda p, c, t: (p ^ k1, t ^ k0, c))
                if pair[1] // 4 == l
            ]
            piece = lax.ppermute(piece, COLUMN, pairs)
            got = piece if got is None else jnp.where(p == 1, got, piece)
        attn_sum = attn_sum + got[:, :ATTN].astype(f32)
        moe_all = lax.dynamic_update_index_in_dim(moe_all, got[:, ATTN:], (p * 2 + c) ^ k, 0)
    small = attn_sum[:, QKV + OUT :]
    return (
        hidden_states[None],
        grad_inputs[None],
        small[:, 0][None],
        attn_sum[:, :QKV].reshape(24, 3, OUT)[None],
        attn_sum[:, QKV : QKV + OUT][None],
        small[:, 1][None],
        small[:, 2 : 2 + E][None],
        moe_all[:, :, :FFH].astype(f32)[None],
        moe_all[:, :, FFH:].astype(f32)[None],
    )


def solution(mesh):
    grid = Mesh(mesh.devices.reshape(2, 4, 4, 2, 2), ("pipe", "x", "y", "core", "tensor"))
    dp = ("x", "y", "core")
    return jax.shard_map(
        on_device,
        mesh=grid,
        in_specs=(
            P(dp, "tensor", None),
            P(dp, "tensor", None),
            P("pipe", dp, "tensor", None),
            P("pipe", dp),
            P("pipe", dp, None, "tensor"),
            P("pipe", dp, "tensor"),
            P("pipe", dp),
            P("pipe", dp, None),
            P("pipe", None, dp, "tensor"),
            P("pipe", None, dp, "tensor"),
        ),
        out_specs=(
            P("pipe", dp, "tensor", None),
            P("pipe", dp, "tensor", None),
            P("pipe", dp),
            P("pipe", dp, None, "tensor"),
            P("pipe", dp, "tensor"),
            P("pipe", dp),
            P("pipe", dp, None),
            P("pipe", None, dp, "tensor"),
            P("pipe", None, dp, "tensor"),
        ),
        check_vma=False,
    )
```

```python
import functools
import math

import jax
import jax.numpy as jnp
from jax import lax
from jax.experimental import pallas as pl
from jax.experimental.pallas import tpu as pltpu
from jax.sharding import Mesh
from jax.sharding import PartitionSpec as P

D = 768
DH = 64
E = 4
LEN = 256
HALF = 128
PAD = 96
QKV = 1152
OUT = 384
SMALL = 256
ATTN = QKV + OUT + SMALL
FFH = 1536
MOE = 2 * FFH

norm_eps = 1e-06
f32 = jnp.float32
bf16 = jnp.bfloat16
COLUMN = ("pipe", "core", "tensor")


def column_pairs(target):
    pairs = []
    for p in range(2):
        for c in range(2):
            for t in range(2):
                p2, c2, t2 = target(p, c, t)
                pairs.append((p * 4 + c * 2 + t, p2 * 4 + c2 * 2 + t2))
    return pairs


def column_send(array, target):
    return lax.ppermute(array, COLUMN, column_pairs(target))


def core_swap(array):
    return lax.ppermute(array, "core", [(0, 1), (1, 0)])


def chip_swap(array, k):
    return lax.ppermute(array, ("pipe", "tensor"), [(i, i ^ k) for i in range(4)])


def axis_swap(array, axis, k):
    return lax.ppermute(array, axis, [(i, i ^ k) for i in range(4)])


def scatter_axis(whole, axis, dim):
    me = lax.axis_index(axis)
    parts = [lax.dynamic_index_in_dim(whole, me ^ k, dim, keepdims=False) for k in range(4)]
    got = [parts[0]] + [axis_swap(parts[k], axis, k) for k in (1, 2, 3)]
    return sum(part.astype(f32) for part in got).astype(bf16)


def scatter_first(whole, axis):
    return scatter_axis(whole.reshape(4, 4, -1, whole.shape[1]), axis, "xy".index(axis))


def rms_scale(values):
    return lax.rsqrt(jnp.mean(values * values, axis=-1, keepdims=True) + norm_eps)


def norm_back(grad_normed, values, scale_rows, gain):
    normal = values * scale_rows
    weighted = grad_normed * gain
    grad_values = scale_rows * (
        weighted - normal * jnp.mean(weighted * normal, axis=-1, keepdims=True)
    )
    return grad_values, jnp.sum(grad_normed * normal, axis=0)


def matmul(left, right, dims):
    return lax.dot_general(left, right, ((dims[:1], dims[1:]), ((), ())), preferred_element_type=f32)


def pair_sum(partial):
    mine = partial.astype(bf16)
    return mine.astype(f32) + core_swap(mine).astype(f32)


def to_experts(rows):
    parts = [rows[k * PAD : (k + 1) * PAD] for k in range(4)]
    return jnp.concatenate([parts[0]] + [chip_swap(parts[k], k) for k in (1, 2, 3)], axis=0)


PAIR = 2 * DH
SCALE = 1.0 / math.sqrt(DH)


def dot(left, right, dims):
    return lax.dot_general(left, right, ((dims[:1], dims[1:]), ((), ())), preferred_element_type=f32)


def first_head():
    return lax.broadcasted_iota(jnp.int32, (LEN, PAIR), 1) < DH


def head_probs(query, key):
    scores = dot(query, key, (1, 1)) * SCALE
    exponent = jnp.exp(scores - jnp.max(scores, axis=-1, keepdims=True))
    return exponent / jnp.sum(exponent, axis=-1, keepdims=True)


def fetch(weights_ref, attn_ref, sem, layer):
    copy = pltpu.make_async_copy(weights_ref.at[:, pl.ds(layer * ATTN, ATTN)], attn_ref, sem)
    copy.start()
    return copy


def attend_kernel(
    layer, x_ref, weights_ref, part_ref, normed_ref, packed_ref, context_ref, small_ref, attn_ref, sem
):
    copy = fetch(weights_ref, attn_ref, sem, layer)
    values = x_ref[...]
    scale = lax.rsqrt(jnp.mean(values * values, axis=-1, keepdims=True) + norm_eps)
    copy.wait()
    small = jnp.transpose(attn_ref[:, QKV + OUT : QKV + OUT + 128].astype(f32))[:8]
    small_ref[...] = small
    normed = (values * scale * small[:1]).astype(bf16)
    normed_ref[...] = normed
    packed_ref[...] = dot(normed, attn_ref[:, :QKV], (1, 0)).astype(bf16)
    low = first_head()
    for pair in range(OUT // PAIR):
        at = pair * PAIR
        query = packed_ref[:, at : at + PAIR]
        key = packed_ref[:, OUT + at : OUT + at + PAIR]
        value = packed_ref[:, 2 * OUT + at : 2 * OUT + at + PAIR]
        none = jnp.zeros_like(query)
        parts = []
        for head in range(2):
            mine = low if head == 0 else ~low
            probs = head_probs(jnp.where(mine, query, none), key).astype(bf16)
            parts.append(dot(probs, value, (1, 0)))
        context_ref[:, at : at + PAIR] = jnp.where(low, parts[0], parts[1]).astype(bf16)
    part_ref[...] = dot(context_ref[...], attn_ref[:, QKV : QKV + OUT], (1, 1)).astype(bf16)


VMEM = pl.BlockSpec(memory_space=pltpu.VMEM)
HBM = pl.BlockSpec(memory_space=pltpu.HBM)


def attend(inputs, weights, layer):
    shape = jax.ShapeDtypeStruct
    return pl.pallas_call(
        functools.partial(attend_kernel, layer),
        in_specs=[VMEM, HBM],
        out_specs=(VMEM,) * 5,
        out_shape=(
            shape((LEN, D), bf16),
            shape((LEN, D), bf16),
            shape((LEN, QKV), bf16),
            shape((LEN, OUT), bf16),
            shape((8, D), f32),
        ),
        scratch_shapes=[pltpu.VMEM((D, ATTN), bf16), pltpu.SemaphoreType.DMA],
        compiler_params=pltpu.CompilerParams(vmem_limit_bytes=24 * 2**20),
        cost_estimate=pl.CostEstimate(
            flops=2 * LEN * D * (QKV + OUT), bytes_accessed=6 * 2**20, transcendentals=6 * LEN * LEN
        ),
        name="attend",
    )(inputs, weights)


def attend_back_kernel(
    layer, grad_ref, weights_ref, packed_ref, part_ref, grads_ref, heads_ref, attn_ref, sem
):
    fetch(weights_ref, attn_ref, sem, layer).wait()
    heads_ref[...] = dot(grad_ref[...], attn_ref[:, QKV : QKV + OUT], (1, 0)).astype(bf16)
    low = first_head()
    for pair in range(OUT // PAIR):
        at = pair * PAIR
        query = packed_ref[:, at : at + PAIR]
        key = packed_ref[:, OUT + at : OUT + at + PAIR]
        value = packed_ref[:, 2 * OUT + at : 2 * OUT + at + PAIR]
        grad = heads_ref[:, at : at + PAIR]
        none = jnp.zeros_like(query)
        found = []
        for head in range(2):
            mine = low if head == 0 else ~low
            probs = head_probs(jnp.where(mine, query, none), key)
            grad_probs = dot(jnp.where(mine, grad, none), value, (1, 1))
            inner = jnp.sum(grad_probs * probs, axis=-1, keepdims=True)
            grad_scores = (probs * (grad_probs - inner)).astype(bf16)
            found.append(
                (
                    dot(grad_scores, key, (1, 0)) * SCALE,
                    dot(grad_scores, query, (0, 0)) * SCALE,
                    dot(probs.astype(bf16), grad, (0, 0)),
                )
            )
        for j in range(3):
            both = jnp.where(low, found[0][j], found[1][j]).astype(bf16)
            grads_ref[:, j * OUT + at : j * OUT + at + PAIR] = both
    part_ref[...] = dot(grads_ref[...], attn_ref[:, :QKV], (1, 1)).astype(bf16)


def attend_back(grad, weights, packed, layer):
    shape = jax.ShapeDtypeStruct
    return pl.pallas_call(
        functools.partial(attend_back_kernel, layer),
        in_specs=[VMEM, HBM, VMEM],
        out_specs=(VMEM, VMEM),
        out_shape=(shape((LEN, D), bf16), shape((LEN, QKV), bf16)),
        scratch_shapes=[
            pltpu.VMEM((LEN, OUT), bf16),
            pltpu.VMEM((D, ATTN), bf16),
            pltpu.SemaphoreType.DMA,
        ],
        compiler_params=pltpu.CompilerParams(vmem_limit_bytes=24 * 2**20),
        cost_estimate=pl.CostEstimate(
            flops=2 * LEN * D * (QKV + OUT), bytes_accessed=6 * 2**20, transcendentals=6 * LEN * LEN
        ),
        name="attend_back",
    )(grad, weights, packed)


TILE = 256


def expert_grads_kernel(at, filled_ref, hidden_ref, slots_ref, active_ref, *rest):
    out_ref, tiles, sems = rest[-3:]
    copies = []
    for i in range(D // TILE):
        rows = slice(i * TILE, (i + 1) * TILE)
        tiles[rows, :FFH] = dot(filled_ref[:, rows], hidden_ref[...], (0, 0)).astype(bf16)
        tiles[rows, FFH:] = dot(slots_ref[:, rows], active_ref[...], (0, 0)).astype(bf16)
        copy = pltpu.make_async_copy(
            tiles.at[pl.ds(i * TILE, TILE)],
            out_ref.at[pl.ds(i * TILE, TILE), pl.ds(at, MOE)],
            sems.at[i],
        )
        copy.start()
        copies.append(copy)
    for copy in copies:
        copy.wait()


def expert_grads(filled, grad_hidden, grad_slots, activated, buffer=None):
    operands = [filled, grad_hidden, grad_slots, activated]
    width = MOE
    if buffer is not None:
        operands.append(buffer)
        width = buffer.shape[1]
    return pl.pallas_call(
        functools.partial(expert_grads_kernel, width - MOE),
        in_specs=[VMEM] * 4 + [HBM] * (len(operands) - 4),
        out_specs=HBM,
        out_shape=jax.ShapeDtypeStruct((D, width), bf16),
        scratch_shapes=[
            pltpu.VMEM((D, MOE), bf16),
            pltpu.SemaphoreType.DMA((D // TILE,)),
        ],
        input_output_aliases={} if buffer is None else {4: 0},
        compiler_params=pltpu.CompilerParams(vmem_limit_bytes=32 * 2**20),
        cost_estimate=pl.CostEstimate(
            flops=4 * E * PAD * D * FFH, bytes_accessed=9 * 2**20, transcendentals=0
        ),
        name="expert_grads",
    )(*operands)


def attend_grads_kernel(normed_ref, grads_ref, proj_ref, context_ref, small_ref, out_ref, tiles, sem):
    tiles[:, :QKV] = dot(normed_ref[...], grads_ref[...], (0, 0)).astype(bf16)
    tiles[:, QKV : QKV + OUT] = dot(proj_ref[...], context_ref[...], (0, 0)).astype(bf16)
    rows = jnp.concatenate([small_ref[...], jnp.zeros((120, D), f32)], axis=0)
    tiles[:, QKV + OUT : QKV + OUT + 128] = jnp.transpose(rows).astype(bf16)
    tiles[:, QKV + OUT + 128 :] = jnp.zeros((D, SMALL - 128), bf16)
    copy = pltpu.make_async_copy(tiles, out_ref.at[:, pl.ds(0, ATTN)], sem)
    copy.start()
    copy.wait()


def attend_grads(normed, grads, proj, context, small, width):
    return pl.pallas_call(
        attend_grads_kernel,
        in_specs=[VMEM] * 5,
        out_specs=HBM,
        out_shape=jax.ShapeDtypeStruct((D, width), bf16),
        scratch_shapes=[pltpu.VMEM((D, ATTN), bf16), pltpu.SemaphoreType.DMA],
        compiler_params=pltpu.CompilerParams(vmem_limit_bytes=24 * 2**20),
        cost_estimate=pl.CostEstimate(
            flops=2 * LEN * D * (QKV + OUT), bytes_accessed=5 * 2**20, transcendentals=0
        ),
        name="attend_grads",
    )(normed, grads, proj, context, small)


def expert_weights(weights, layer):
    at = 2 * ATTN + layer * MOE
    return weights[:, at : at + FFH], weights[:, at + FFH : at + MOE]


def forward(inputs, table, onehot, weights, layer):
    w_in, w_down = expert_weights(weights, layer)
    part, normed, packed, context, small = attend(inputs, weights, layer)
    g_moe, w_router = small[1:2], small[2 : 2 + E].astype(bf16)
    middle = inputs + pair_sum(part)
    scale_mid = rms_scale(middle)
    mixed = (middle * scale_mid * g_moe).astype(bf16)
    logits = matmul(mixed, w_router, (1, 1))
    exponent = jnp.exp(logits - jnp.max(logits, axis=-1, keepdims=True))
    router_probs = exponent / jnp.sum(exponent, axis=-1, keepdims=True)
    gate = jnp.sum(onehot * router_probs, axis=-1, keepdims=True)
    filled = to_experts(matmul(table, mixed, (1, 0)).astype(bf16))
    hidden = matmul(filled, w_in, (1, 0))
    cdf = 0.5 * (1.0 + lax.erf(hidden * (1.0 / math.sqrt(2.0))))
    activated = (hidden * cdf).astype(bf16)
    slope = cdf + hidden * jnp.exp(-0.5 * hidden * hidden) * (1.0 / math.sqrt(2.0 * math.pi))
    expert_out = to_experts(matmul(activated, w_down, (1, 1)).astype(bf16))
    combined = pair_sum(matmul(table, expert_out, (0, 0)))
    output = (middle + gate * combined).astype(bf16)
    kept = (
        inputs, small, normed, packed, context, middle, scale_mid,
        mixed, router_probs, gate, filled, activated, slope, combined,
    )
    return output, kept


def backward_moe(grad_out, kept, table, onehot, weights, layer, buffer=None):
    w_in, w_down = expert_weights(weights, layer)
    (
        inputs, small, normed, packed, context, middle, scale_mid,
        mixed, router_probs, gate, filled, activated, slope, combined,
    ) = kept
    grad_gate = jnp.sum(grad_out * combined, axis=-1, keepdims=True)
    grad_branch = (gate * grad_out).astype(bf16)
    grad_slots = to_experts(matmul(table, grad_branch, (1, 0)).astype(bf16))
    grad_act = matmul(grad_slots, w_down, (1, 0))
    grad_hidden = (grad_act * slope).astype(bf16)
    grad_filled = to_experts(matmul(grad_hidden, w_in, (1, 1)).astype(bf16))
    expert = expert_grads(filled, grad_hidden, grad_slots, activated, buffer)
    grad_filled, expert = lax.optimization_barrier((grad_filled, expert))
    grad_mixed = pair_sum(matmul(table, grad_filled, (0, 0)))
    grad_logits = router_probs * (onehot - gate) * grad_gate
    grad_w_router = lax.dot_general(
        grad_logits, mixed.astype(f32), (((0,), (0,)), ((), ())), precision=lax.Precision.HIGHEST
    )
    g_moe, w_router = small[1:2], small[2 : 2 + E]
    back_rows = sum(grad_logits[:, e : e + 1] * w_router[e][None, :] for e in range(E))
    grad_norm, grad_g_moe = norm_back(grad_mixed + back_rows, middle, scale_mid, g_moe)
    return grad_out + grad_norm, expert, grad_w_router, grad_g_moe


def backward_attn(grad_middle, kept, weights, layer, grad_w_router, grad_g_moe, width):
    (
        inputs, small, normed, packed, context, middle, scale_mid,
        mixed, router_probs, gate, filled, activated, slope, combined,
    ) = kept
    proj = grad_middle.astype(bf16)
    part, grads = attend_back(proj, weights, packed, layer)
    grad_normed = pair_sum(part)
    grad_norm, grad_g_attn = norm_back(grad_normed, inputs, rms_scale(inputs), small[:1])
    rows = jnp.concatenate(
        [grad_g_attn[None], grad_g_moe[None], grad_w_router, jnp.zeros((6 - E, D), f32)], axis=0
    )
    return grad_middle + grad_norm, attend_grads(normed, grads, proj, context, rows, width)


def by_layer(p, near, far):
    return jnp.where(p == 0, near, far), jnp.where(p == 0, far, near)


def on_device(tokens, cotangent, routes, g_attn, w_qkv, w_out, g_moe, w_router, w_in, w_down):
    p, c, t = lax.axis_index("pipe"), lax.axis_index("core"), lax.axis_index("tensor")
    chip = p * 2 + t

    def spread(chunk_of):
        got = []
        for k in range(4):
            k1, k0 = k >> 1, k & 1
            got.append(column_send(chunk_of(k), lambda p, c, t: (p ^ k1, t, c ^ k0)))
        layers = []
        for first, second in ((by_layer(p, got[0], got[2])), (by_layer(p, got[1], got[3]))):
            layers.append((first, second))
        return [
            jnp.concatenate(
                [
                    jnp.where(t == 0, layers[0][l], layers[1][l]),
                    jnp.where(t == 0, layers[1][l], layers[0][l]),
                ],
                axis=0,
            )
            for l in range(2)
        ]

    small = jnp.concatenate([g_attn[0][:, None], g_moe[0][:, None], w_router[0]], axis=1)
    small = jnp.pad(small, ((0, 0), (0, SMALL - small.shape[1])))

    def chunk_of(k):
        expert = (p * 2 + c) ^ k
        return jnp.concatenate(
            [
                w_qkv[0].reshape(-1, QKV),
                w_out[0],
                small,
                lax.dynamic_index_in_dim(w_in[0], expert, 0, keepdims=False),
                lax.dynamic_index_in_dim(w_down[0], expert, 0, keepdims=False),
            ],
            axis=1,
        )

    blocks = spread(chunk_of)
    cut = lambda l, at, end: blocks[l][:, at:end]
    weights = lax.all_gather(
        jnp.concatenate(
            [cut(0, 0, ATTN), cut(1, 0, ATTN), cut(0, ATTN, ATTN + MOE), cut(1, ATTN, ATTN + MOE)],
            axis=1,
        ),
        ("x", "y"), axis=0, tiled=True,
    )

    def to_owner(rows):
        got = [column_send(rows, lambda p, c, t, j=j: (p, t ^ j, c)) for j in range(2)]
        return jnp.where(c == 0, got[0], got[1]), jnp.where(c == 0, got[1], got[0])

    own_routes = routes[0, :, :, 0].astype(bf16)
    far_routes = lax.ppermute(own_routes, "pipe", [(0, 1), (1, 0)])
    route_pair = jnp.stack(by_layer(p, own_routes, far_routes))
    route_rows = lax.dynamic_index_in_dim(route_pair, p, 1, keepdims=False)
    own_tokens = lax.dynamic_index_in_dim(tokens, p, 0, keepdims=False)
    extra = jnp.pad(route_rows.reshape(1, 2 * HALF), ((0, 15), (0, D - 2 * HALF)))
    low_rows, high_rows = to_owner(jnp.concatenate([own_tokens, extra], axis=0))
    inputs = jnp.concatenate([low_rows[:HALF], high_rows[:HALF]], axis=0).astype(f32)
    tables, onehots = [], []
    earlier = (
        lax.broadcasted_iota(jnp.int32, (LEN, LEN), 0)
        < lax.broadcasted_iota(jnp.int32, (LEN, LEN), 1)
    ).astype(bf16)
    for l in range(2):
        cut = slice(l * HALF, (l + 1) * HALF)
        ids = jnp.concatenate([low_rows[HALF, cut], high_rows[HALF, cut]]).astype(jnp.int32)
        picks = (ids[None, :] == jnp.arange(E, dtype=jnp.int32)[:, None]).astype(f32)
        before = matmul(picks.astype(bf16), earlier, (1, 0))
        rank = jnp.sum(before * picks, axis=0).astype(jnp.int32)
        place = (ids ^ chip) * PAD + rank
        tables.append(
            (place[None, :] == jnp.arange(E * PAD, dtype=jnp.int32)[:, None]).astype(bf16)
        )
        onehots.append(picks.T)

    cot_rows = lax.dynamic_index_in_dim(cotangent, p, 0, keepdims=False)
    grad_out = jnp.concatenate(to_owner(cot_rows), axis=0).astype(f32)

    inputs, grad_out = lax.optimization_barrier((inputs, grad_out))
    first_out, kept_first = forward(inputs, tables[0], onehots[0], weights, 0)
    second_out, kept_second = forward(first_out.astype(f32), tables[1], onehots[1], weights, 1)

    def to_home(first, second):
        cut = lambda rows: lax.dynamic_slice_in_dim(rows, c * HALF, HALF, 0)
        near, far = by_layer(p, cut(first), cut(second))
        near = column_send(near, lambda p, c, t: (p, t, c))
        far = column_send(far, lambda p, c, t: (1 - p, t, c))
        return jnp.stack(by_layer(p, near, far))

    def reduce_plane(whole):
        return lax.optimization_barrier(
            lax.psum_scatter(whole, ("x", "y"), scatter_dimension=0, tiled=True)
        )

    grad_mid, expert, g_router, gg_moe = backward_moe(
        grad_out, kept_second, tables[1], onehots[1], weights, 1
    )
    moe_second = reduce_plane(expert)
    grad_x, buffer = backward_attn(
        grad_mid, kept_second, weights, 1, g_router, gg_moe, ATTN + MOE
    )
    second_grad = grad_x.astype(bf16)
    grad_mid, buffer, g_router, gg_moe = backward_moe(
        second_grad.astype(f32), kept_first, tables[0], onehots[0], weights, 0, buffer
    )
    mixed_all = reduce_plane(buffer)
    grad_x, attn_whole = backward_attn(grad_mid, kept_first, weights, 0, g_router, gg_moe, ATTN)
    over_x = scatter_axis(scatter_first(attn_whole[:, : ATTN // 2], "x"), "y", 0)
    over_y = scatter_axis(scatter_first(attn_whole[:, ATTN // 2 :], "y"), "x", 0)
    attn_first = jnp.concatenate([over_x, over_y], axis=1)
    first_out, second_out, grad_x = lax.optimization_barrier((first_out, second_out, grad_x))
    hidden_states = to_home(first_out, second_out)
    grad_inputs = to_home(grad_x.astype(bf16), second_grad).astype(f32)

    def send_back(first, second):
        got = []
        for k in range(4):
            k1, k0 = k >> 1, k & 1
            piece = jnp.where((p ^ k1) == 0, first, second)
            piece = lax.dynamic_slice_in_dim(piece, (t ^ k0) * 24, 24, 0)
            got.append(column_send(piece, lambda p, c, t: (p ^ k1, t ^ k0, c)))
        return got

    widen = lambda attn: jnp.pad(attn, ((0, 0), (0, MOE - ATTN)))
    one = send_back(widen(attn_first), moe_second)
    mixed_all, one = lax.optimization_barrier((mixed_all, one))
    two = send_back(mixed_all[:, ATTN:], widen(mixed_all[:, :ATTN]))
    attn_sum = jnp.zeros((24, ATTN), f32)
    moe_all = jnp.zeros((E, 24, MOE), bf16)
    for k in range(4):
        attn_sum = attn_sum + jnp.where(p == 0, one[k], two[k])[:, :ATTN].astype(f32)
        moe_all = lax.dynamic_update_index_in_dim(
            moe_all, jnp.where(p == 0, two[k], one[k]), (p * 2 + c) ^ k, 0
        )
    small = attn_sum[:, QKV + OUT :]
    return (
        hidden_states[None],
        grad_inputs[None],
        small[:, 0][None],
        attn_sum[:, :QKV].reshape(24, 3, OUT)[None],
        attn_sum[:, QKV : QKV + OUT][None],
        small[:, 1][None],
        small[:, 2 : 2 + E][None],
        moe_all[:, :, :FFH].astype(f32)[None],
        moe_all[:, :, FFH:].astype(f32)[None],
    )


def solution(mesh):
    grid = Mesh(mesh.devices.reshape(2, 4, 4, 2, 2), ("pipe", "x", "y", "core", "tensor"))
    dp = ("x", "y", "core")
    return jax.shard_map(
        on_device,
        mesh=grid,
        in_specs=(
            P(dp, "tensor", None),
            P(dp, "tensor", None),
            P("pipe", dp, "tensor", None),
            P("pipe", dp),
            P("pipe", dp, None, "tensor"),
            P("pipe", dp, "tensor"),
            P("pipe", dp),
            P("pipe", dp, None),
            P("pipe", None, dp, "tensor"),
            P("pipe", None, dp, "tensor"),
        ),
        out_specs=(
            P("pipe", dp, "tensor", None),
            P("pipe", dp, "tensor", None),
            P("pipe", dp),
            P("pipe", dp, None, "tensor"),
            P("pipe", dp, "tensor"),
            P("pipe", dp),
            P("pipe", dp, None),
            P("pipe", None, dp, "tensor"),
            P("pipe", None, dp, "tensor"),
        ),
        check_vma=False,
    )
```

```python
import functools
import math

import jax
import jax.numpy as jnp
from jax import lax
from jax.experimental import pallas as pl
from jax.experimental.pallas import tpu as pltpu
from jax.sharding import Mesh
from jax.sharding import PartitionSpec as P

D = 768
DH = 64
E = 4
LEN = 256
HALF = 128
PAD = 96
QKV = 1152
OUT = 384
SMALL = 256
ATTN = QKV + OUT + SMALL
FFH = 1536
MOE = 2 * FFH

norm_eps = 1e-06
f32 = jnp.float32
bf16 = jnp.bfloat16
COLUMN = ("pipe", "core", "tensor")


def column_pairs(target):
    pairs = []
    for p in range(2):
        for c in range(2):
            for t in range(2):
                p2, c2, t2 = target(p, c, t)
                pairs.append((p * 4 + c * 2 + t, p2 * 4 + c2 * 2 + t2))
    return pairs


def column_send(array, target):
    return lax.ppermute(array, COLUMN, column_pairs(target))


def core_swap(array):
    return lax.ppermute(array, "core", [(0, 1), (1, 0)])


def chip_swap(array, k):
    return lax.ppermute(array, ("pipe", "tensor"), [(i, i ^ k) for i in range(4)])


def axis_swap(array, axis, k):
    return lax.ppermute(array, axis, [(i, i ^ k) for i in range(4)])


def scatter_axis(whole, axis, dim):
    me = lax.axis_index(axis)
    parts = [lax.dynamic_index_in_dim(whole, me ^ k, dim, keepdims=False) for k in range(4)]
    got = [parts[0]] + [axis_swap(parts[k], axis, k) for k in (1, 2, 3)]
    return sum(part.astype(f32) for part in got).astype(bf16)


def scatter_first(whole, axis):
    return scatter_axis(whole.reshape(4, 4, -1, whole.shape[1]), axis, "xy".index(axis))


def rms_scale(values):
    return lax.rsqrt(jnp.mean(values * values, axis=-1, keepdims=True) + norm_eps)


def norm_back(grad_normed, values, scale_rows, gain):
    normal = values * scale_rows
    weighted = grad_normed * gain
    grad_values = scale_rows * (
        weighted - normal * jnp.mean(weighted * normal, axis=-1, keepdims=True)
    )
    return grad_values, jnp.sum(grad_normed * normal, axis=0)


def matmul(left, right, dims):
    return lax.dot_general(left, right, ((dims[:1], dims[1:]), ((), ())), preferred_element_type=f32)


def pair_sum(partial):
    mine = partial.astype(bf16)
    return mine.astype(f32) + core_swap(mine).astype(f32)


def to_experts(*arrays):
    parts = [
        jnp.stack([rows[k * PAD : (k + 1) * PAD] for rows in arrays]) for k in range(4)
    ]
    parts = [parts[0]] + [chip_swap(parts[k], k) for k in (1, 2, 3)]
    found = [
        jnp.concatenate([part[i] for part in parts], axis=0) for i in range(len(arrays))
    ]
    return found if len(arrays) > 1 else found[0]


PAIR = 2 * DH
SCALE = 1.0 / math.sqrt(DH)


def dot(left, right, dims):
    return lax.dot_general(left, right, ((dims[:1], dims[1:]), ((), ())), preferred_element_type=f32)


def first_head():
    return lax.broadcasted_iota(jnp.int32, (LEN, PAIR), 1) < DH


def head_probs(query, key):
    scores = dot(query, key, (1, 1)) * SCALE
    exponent = jnp.exp(scores - jnp.max(scores, axis=-1, keepdims=True))
    return exponent / jnp.sum(exponent, axis=-1, keepdims=True)


def fetch(weights_ref, attn_ref, sem, layer):
    copy = pltpu.make_async_copy(weights_ref.at[:, pl.ds(layer * ATTN, ATTN)], attn_ref, sem)
    copy.start()
    return copy


def attend_kernel(
    layer, x_ref, weights_ref, part_ref, normed_ref, packed_ref, context_ref, small_ref, attn_ref, sem
):
    copy = fetch(weights_ref, attn_ref, sem, layer)
    values = x_ref[...]
    scale = lax.rsqrt(jnp.mean(values * values, axis=-1, keepdims=True) + norm_eps)
    copy.wait()
    small = jnp.transpose(attn_ref[:, QKV + OUT : QKV + OUT + 128].astype(f32))[:8]
    small_ref[...] = small
    normed = (values * scale * small[:1]).astype(bf16)
    normed_ref[...] = normed
    packed_ref[...] = dot(normed, attn_ref[:, :QKV], (1, 0)).astype(bf16)
    low = first_head()
    for pair in range(OUT // PAIR):
        at = pair * PAIR
        query = packed_ref[:, at : at + PAIR]
        key = packed_ref[:, OUT + at : OUT + at + PAIR]
        value = packed_ref[:, 2 * OUT + at : 2 * OUT + at + PAIR]
        none = jnp.zeros_like(query)
        parts = []
        for head in range(2):
            mine = low if head == 0 else ~low
            probs = head_probs(jnp.where(mine, query, none), key).astype(bf16)
            parts.append(dot(probs, value, (1, 0)))
        context_ref[:, at : at + PAIR] = jnp.where(low, parts[0], parts[1]).astype(bf16)
    part_ref[...] = dot(context_ref[...], attn_ref[:, QKV : QKV + OUT], (1, 1)).astype(bf16)


VMEM = pl.BlockSpec(memory_space=pltpu.VMEM)
HBM = pl.BlockSpec(memory_space=pltpu.HBM)


def attend(inputs, weights, layer):
    shape = jax.ShapeDtypeStruct
    return pl.pallas_call(
        functools.partial(attend_kernel, layer),
        in_specs=[VMEM, HBM],
        out_specs=(VMEM,) * 5,
        out_shape=(
            shape((LEN, D), bf16),
            shape((LEN, D), bf16),
            shape((LEN, QKV), bf16),
            shape((LEN, OUT), bf16),
            shape((8, D), f32),
        ),
        scratch_shapes=[pltpu.VMEM((D, ATTN), bf16), pltpu.SemaphoreType.DMA],
        compiler_params=pltpu.CompilerParams(vmem_limit_bytes=54 * 2**20),
        cost_estimate=pl.CostEstimate(
            flops=2 * LEN * D * (QKV + OUT), bytes_accessed=6 * 2**20, transcendentals=6 * LEN * LEN
        ),
        name="attend",
    )(inputs, weights)


def attend_back_kernel(
    layer, grad_ref, weights_ref, packed_ref, part_ref, grads_ref, heads_ref, attn_ref, sem
):
    fetch(weights_ref, attn_ref, sem, layer).wait()
    heads_ref[...] = dot(grad_ref[...], attn_ref[:, QKV : QKV + OUT], (1, 0)).astype(bf16)
    low = first_head()
    for pair in range(OUT // PAIR):
        at = pair * PAIR
        query = packed_ref[:, at : at + PAIR]
        key = packed_ref[:, OUT + at : OUT + at + PAIR]
        value = packed_ref[:, 2 * OUT + at : 2 * OUT + at + PAIR]
        grad = heads_ref[:, at : at + PAIR]
        none = jnp.zeros_like(query)
        found = []
        for head in range(2):
            mine = low if head == 0 else ~low
            probs = head_probs(jnp.where(mine, query, none), key)
            grad_probs = dot(jnp.where(mine, grad, none), value, (1, 1))
            inner = jnp.sum(grad_probs * probs, axis=-1, keepdims=True)
            grad_scores = (probs * (grad_probs - inner)).astype(bf16)
            found.append(
                (
                    dot(grad_scores, key, (1, 0)) * SCALE,
                    dot(grad_scores, query, (0, 0)) * SCALE,
                    dot(probs.astype(bf16), grad, (0, 0)),
                )
            )
        for j in range(3):
            both = jnp.where(low, found[0][j], found[1][j]).astype(bf16)
            grads_ref[:, j * OUT + at : j * OUT + at + PAIR] = both
    part_ref[...] = dot(grads_ref[...], attn_ref[:, :QKV], (1, 1)).astype(bf16)


def attend_back(grad, weights, packed, layer):
    shape = jax.ShapeDtypeStruct
    return pl.pallas_call(
        functools.partial(attend_back_kernel, layer),
        in_specs=[VMEM, HBM, VMEM],
        out_specs=(VMEM, VMEM),
        out_shape=(shape((LEN, D), bf16), shape((LEN, QKV), bf16)),
        scratch_shapes=[
            pltpu.VMEM((LEN, OUT), bf16),
            pltpu.VMEM((D, ATTN), bf16),
            pltpu.SemaphoreType.DMA,
        ],
        compiler_params=pltpu.CompilerParams(vmem_limit_bytes=54 * 2**20),
        cost_estimate=pl.CostEstimate(
            flops=2 * LEN * D * (QKV + OUT), bytes_accessed=6 * 2**20, transcendentals=6 * LEN * LEN
        ),
        name="attend_back",
    )(grad, weights, packed)


TILE = 256


def expert_grads_kernel(at, filled_ref, hidden_ref, slots_ref, active_ref, *rest):
    out_ref, tiles, sems = rest[-3:]
    copies = []
    for i in range(D // TILE):
        rows = slice(i * TILE, (i + 1) * TILE)
        tiles[rows, :FFH] = dot(filled_ref[:, rows], hidden_ref[...], (0, 0)).astype(bf16)
        tiles[rows, FFH:] = dot(slots_ref[:, rows], active_ref[...], (0, 0)).astype(bf16)
        copy = pltpu.make_async_copy(
            tiles.at[pl.ds(i * TILE, TILE)],
            out_ref.at[pl.ds(i * TILE, TILE), pl.ds(at, MOE)],
            sems.at[i],
        )
        copy.start()
        copies.append(copy)
    for copy in copies:
        copy.wait()


def attend_grads_kernel(at, normed_ref, grads_ref, proj_ref, context_ref, small_ref, *rest):
    out_ref, tiles, sems = rest[-3:]
    tiles[:, :QKV] = dot(normed_ref[...], grads_ref[...], (0, 0)).astype(bf16)
    tiles[:, QKV : QKV + OUT] = dot(proj_ref[...], context_ref[...], (0, 0)).astype(bf16)
    rows = jnp.concatenate([small_ref[...], jnp.zeros((120, D), f32)], axis=0)
    tiles[:, QKV + OUT : QKV + OUT + 128] = jnp.transpose(rows).astype(bf16)
    tiles[:, QKV + OUT + 128 :] = jnp.zeros((D, SMALL - 128), bf16)
    copy = pltpu.make_async_copy(tiles, out_ref.at[:, pl.ds(at, ATTN)], sems.at[0])
    copy.start()
    copy.wait()


def grads_into(kernel, name, columns, operands, buffer, width, at):
    count = len(operands)
    if buffer is not None:
        operands = operands + [buffer]
    return pl.pallas_call(
        functools.partial(kernel, at),
        in_specs=[VMEM] * count + [HBM] * (len(operands) - count),
        out_specs=HBM,
        out_shape=jax.ShapeDtypeStruct((D, width), bf16),
        scratch_shapes=[
            pltpu.VMEM((D, columns), bf16),
            pltpu.SemaphoreType.DMA((D // TILE,)),
        ],
        input_output_aliases={} if buffer is None else {count: 0},
        compiler_params=pltpu.CompilerParams(vmem_limit_bytes=54 * 2**20),
        cost_estimate=pl.CostEstimate(
            flops=2 * E * PAD * D * columns, bytes_accessed=9 * 2**20, transcendentals=0
        ),
        name=name,
    )(*operands)


def expert_grads(operands, buffer, width, at):
    return grads_into(expert_grads_kernel, "expert_grads", MOE, operands, buffer, width, at)


def attend_grads(operands, buffer, width, at):
    return grads_into(attend_grads_kernel, "attend_grads", ATTN, operands, buffer, width, at)


def attention(inputs, weights, layer, onehot):
    part, normed, packed, context, small = attend(inputs, weights, layer)
    g_moe, w_router = small[1:2], small[2 : 2 + E].astype(bf16)
    middle = inputs + pair_sum(part)
    scale_mid = rms_scale(middle)
    mixed = (middle * scale_mid * g_moe).astype(bf16)
    logits = matmul(mixed, w_router, (1, 1))
    exponent = jnp.exp(logits - jnp.max(logits, axis=-1, keepdims=True))
    router_probs = exponent / jnp.sum(exponent, axis=-1, keepdims=True)
    gate = jnp.sum(onehot * router_probs, axis=-1, keepdims=True)
    return inputs, small, normed, packed, context, middle, scale_mid, mixed, router_probs, gate


def experts(filled, w_in, w_down):
    hidden = matmul(filled, w_in, (1, 0))
    cdf = 0.5 * (1.0 + lax.erf(hidden * (1.0 / math.sqrt(2.0))))
    activated = (hidden * cdf).astype(bf16)
    slope = cdf + hidden * jnp.exp(-0.5 * hidden * hidden) * (1.0 / math.sqrt(2.0 * math.pi))
    return activated, slope, matmul(activated, w_down, (1, 1)).astype(bf16)


def experts_back(grad_slots, slope, w_in, w_down):
    grad_hidden = (matmul(grad_slots, w_down, (1, 0)) * slope).astype(bf16)
    return grad_hidden, matmul(grad_hidden, w_in, (1, 1)).astype(bf16)


def to_slots(table, rows):
    return matmul(table, rows, (1, 0)).astype(bf16)


def from_slots(table, slots):
    return matmul(table, slots, (0, 0)).astype(bf16)


def mixed_back(grad_out, grad_mixed, combined, onehot, kept):
    inputs, small, normed, packed, context, middle, scale_mid, mixed, router_probs, gate = kept
    grad_gate = jnp.sum(grad_out * combined, axis=-1, keepdims=True)
    grad_logits = router_probs * (onehot - gate) * grad_gate
    grad_w_router = lax.dot_general(
        grad_logits, mixed.astype(f32), (((0,), (0,)), ((), ())), precision=lax.Precision.HIGHEST
    )
    g_moe, w_router = small[1:2], small[2 : 2 + E]
    back_rows = sum(grad_logits[:, e : e + 1] * w_router[e][None, :] for e in range(E))
    grad_norm, grad_g_moe = norm_back(grad_mixed + back_rows, middle, scale_mid, g_moe)
    return grad_out + grad_norm, grad_w_router, grad_g_moe


def attention_back(grad_middle, kept, weights, layer, grad_w_router, grad_g_moe, buffer, width, at):
    inputs, small, normed, packed, context, middle, scale_mid, mixed, router_probs, gate = kept
    proj = grad_middle.astype(bf16)
    part, grads = attend_back(proj, weights, packed, layer)
    grad_normed = pair_sum(part)
    grad_norm, grad_g_attn = norm_back(grad_normed, inputs, rms_scale(inputs), small[:1])
    rows = jnp.concatenate(
        [grad_g_attn[None], grad_g_moe[None], grad_w_router, jnp.zeros((6 - E, D), f32)], axis=0
    )
    buffer = attend_grads([normed, grads, proj, context, rows], buffer, width, at)
    return grad_middle + grad_norm, buffer


def by_layer(p, near, far):
    return jnp.where(p == 0, near, far), jnp.where(p == 0, far, near)


def on_device(tokens, cotangent, routes, g_attn, w_qkv, w_out, g_moe, w_router, w_in, w_down):
    p, c, t = lax.axis_index("pipe"), lax.axis_index("core"), lax.axis_index("tensor")
    chip = p * 2 + t

    def spread(chunk_of):
        got = []
        for k in range(4):
            k1, k0 = k >> 1, k & 1
            got.append(column_send(chunk_of(k), lambda p, c, t: (p ^ k1, t, c ^ k0)))
        layers = []
        for first, second in ((by_layer(p, got[0], got[2])), (by_layer(p, got[1], got[3]))):
            layers.append((first, second))
        return [
            jnp.concatenate(
                [
                    jnp.where(t == 0, layers[0][l], layers[1][l]),
                    jnp.where(t == 0, layers[1][l], layers[0][l]),
                ],
                axis=0,
            )
            for l in range(2)
        ]

    small = jnp.concatenate([g_attn[0][:, None], g_moe[0][:, None], w_router[0]], axis=1)
    small = jnp.pad(small, ((0, 0), (0, SMALL - small.shape[1])))

    def chunk_of(k):
        expert = (p * 2 + c) ^ k
        return jnp.concatenate(
            [
                w_qkv[0].reshape(-1, QKV),
                w_out[0],
                small,
                lax.dynamic_index_in_dim(w_in[0], expert, 0, keepdims=False),
                lax.dynamic_index_in_dim(w_down[0], expert, 0, keepdims=False),
            ],
            axis=1,
        )

    blocks = spread(chunk_of)
    cut = lambda l, at, end: blocks[l][:, at:end]
    weights = lax.all_gather(
        jnp.concatenate([cut(0, 0, ATTN), cut(1, 0, ATTN), cut(0, ATTN, ATTN + MOE)], axis=1),
        ("x", "y"), axis=0, tiled=True,
    )
    late = lax.all_gather(cut(1, ATTN, ATTN + MOE), ("x", "y"), axis=0, tiled=True)

    def to_owner(rows):
        got = [column_send(rows, lambda p, c, t, j=j: (p, t ^ j, c)) for j in range(2)]
        return jnp.where(c == 0, got[0], got[1]), jnp.where(c == 0, got[1], got[0])

    own_routes = routes[0, :, :, 0].astype(bf16)
    far_routes = lax.ppermute(own_routes, "pipe", [(0, 1), (1, 0)])
    route_pair = jnp.stack(by_layer(p, own_routes, far_routes))
    route_rows = lax.dynamic_index_in_dim(route_pair, p, 1, keepdims=False)
    own_tokens = lax.dynamic_index_in_dim(tokens, p, 0, keepdims=False)
    extra = jnp.pad(route_rows.reshape(1, 2 * HALF), ((0, 15), (0, D - 2 * HALF)))
    low_rows, high_rows = to_owner(jnp.concatenate([own_tokens, extra], axis=0))
    inputs = jnp.concatenate([low_rows[:HALF], high_rows[:HALF]], axis=0).astype(f32)
    tables, onehots = [], []
    earlier = (
        lax.broadcasted_iota(jnp.int32, (LEN, LEN), 0)
        < lax.broadcasted_iota(jnp.int32, (LEN, LEN), 1)
    ).astype(bf16)
    for l in range(2):
        cut = slice(l * HALF, (l + 1) * HALF)
        ids = jnp.concatenate([low_rows[HALF, cut], high_rows[HALF, cut]]).astype(jnp.int32)
        picks = (ids[None, :] == jnp.arange(E, dtype=jnp.int32)[:, None]).astype(f32)
        before = matmul(picks.astype(bf16), earlier, (1, 0))
        rank = jnp.sum(before * picks, axis=0).astype(jnp.int32)
        place = (ids ^ chip) * PAD + rank
        tables.append(
            (place[None, :] == jnp.arange(E * PAD, dtype=jnp.int32)[:, None]).astype(bf16)
        )
        onehots.append(picks.T)

    cot_rows = lax.dynamic_index_in_dim(cotangent, p, 0, keepdims=False)
    grad_out = jnp.concatenate(to_owner(cot_rows), axis=0).astype(f32)

    inputs, grad_out = lax.optimization_barrier((inputs, grad_out))
    in_first, down_first = weights[:, 2 * ATTN : 2 * ATTN + FFH], weights[:, 2 * ATTN + FFH :]
    in_second, down_second = late[:, :FFH], late[:, FFH:]

    first = attention(inputs, weights, 0, onehots[0])
    filled_first = to_experts(to_slots(tables[0], first[7]))
    active_first, slope_first, out_slots = experts(filled_first, in_first, down_first)
    combined_first = pair_sum(from_slots(tables[0], to_experts(out_slots)))
    first_out = (first[5] + first[9] * combined_first).astype(bf16)

    second = attention(first_out.astype(f32), weights, 1, onehots[1])
    filled, grad_slots = to_experts(
        to_slots(tables[1], second[7]),
        to_slots(tables[1], (second[9] * grad_out).astype(bf16)),
    )
    activated, slope, out_slots = experts(filled, in_second, down_second)
    grad_hidden, grad_filled = experts_back(grad_slots, slope, in_second, down_second)
    width = 2 * MOE + ATTN
    found = to_experts(out_slots, grad_filled)
    buffer = expert_grads([filled, grad_hidden, grad_slots, activated], None, width, 0)
    found, buffer = lax.optimization_barrier((found, buffer))
    sums = pair_sum(jnp.concatenate([from_slots(tables[1], rows) for rows in found], axis=1))
    combined, grad_mixed = sums[:, :D], sums[:, D:]
    second_out = (second[5] + second[9] * combined).astype(bf16)

    def to_home(first, second):
        cut = lambda rows: lax.dynamic_slice_in_dim(rows, c * HALF, HALF, 0)
        near, far = by_layer(p, cut(first), cut(second))
        near = column_send(near, lambda p, c, t: (p, t, c))
        far = column_send(far, lambda p, c, t: (1 - p, t, c))
        return jnp.stack(by_layer(p, near, far))

    def reduce_plane(whole):
        return lax.optimization_barrier(
            lax.psum_scatter(whole, ("x", "y"), scatter_dimension=0, tiled=True)
        )

    grad_mid, g_router, gg_moe = mixed_back(grad_out, grad_mixed, combined, onehots[1], second)
    grad_x, buffer = attention_back(
        grad_mid, second, weights, 1, g_router, gg_moe, buffer, width, MOE
    )
    second_grad = grad_x.astype(bf16)
    grad_out = second_grad.astype(f32)
    grad_slots = to_experts(to_slots(tables[0], (first[9] * grad_out).astype(bf16)))
    grad_hidden, grad_filled = experts_back(grad_slots, slope_first, in_first, down_first)
    grad_filled = to_experts(grad_filled)
    buffer = expert_grads(
        [filled_first, grad_hidden, grad_slots, active_first], buffer, width, MOE + ATTN
    )
    grad_filled, buffer = lax.optimization_barrier((grad_filled, buffer))
    reduced = reduce_plane(buffer)
    grad_mixed = pair_sum(from_slots(tables[0], grad_filled))
    grad_mid, g_router, gg_moe = mixed_back(
        grad_out, grad_mixed, combined_first, onehots[0], first
    )
    grad_x, attn_whole = attention_back(
        grad_mid, first, weights, 0, g_router, gg_moe, None, ATTN, 0
    )
    over_x = scatter_axis(scatter_first(attn_whole[:, : ATTN // 2], "x"), "y", 0)
    over_y = scatter_axis(scatter_first(attn_whole[:, ATTN // 2 :], "y"), "x", 0)
    attn_first = jnp.concatenate([over_x, over_y], axis=1)
    first_out, second_out, grad_x = lax.optimization_barrier((first_out, second_out, grad_x))
    hidden_states = to_home(first_out, second_out)
    grad_inputs = to_home(grad_x.astype(bf16), second_grad).astype(f32)

    layers = (jnp.concatenate([reduced[:, MOE + ATTN :], attn_first], axis=1), reduced[:, : MOE + ATTN])
    attn_sum = jnp.zeros((24, ATTN), f32)
    moe_all = jnp.zeros((E, 24, MOE), bf16)
    for k in range(4):
        k1, k0 = k >> 1, k & 1
        piece = jnp.where((p ^ k1) == 0, layers[0], layers[1])
        piece = lax.dynamic_slice_in_dim(piece, (t ^ k0) * 24, 24, 0)
        got = column_send(piece, lambda p, c, t: (p ^ k1, t ^ k0, c))
        attn_sum = attn_sum + got[:, MOE:].astype(f32)
        moe_all = lax.dynamic_update_index_in_dim(moe_all, got[:, :MOE], (p * 2 + c) ^ k, 0)
    small = attn_sum[:, QKV + OUT :]
    return (
        hidden_states[None],
        grad_inputs[None],
        small[:, 0][None],
        attn_sum[:, :QKV].reshape(24, 3, OUT)[None],
        attn_sum[:, QKV : QKV + OUT][None],
        small[:, 1][None],
        small[:, 2 : 2 + E][None],
        moe_all[:, :, :FFH].astype(f32)[None],
        moe_all[:, :, FFH:].astype(f32)[None],
    )


def solution(mesh):
    grid = Mesh(mesh.devices.reshape(2, 4, 4, 2, 2), ("pipe", "x", "y", "core", "tensor"))
    dp = ("x", "y", "core")
    return jax.shard_map(
        on_device,
        mesh=grid,
        in_specs=(
            P(dp, "tensor", None),
            P(dp, "tensor", None),
            P("pipe", dp, "tensor", None),
            P("pipe", dp),
            P("pipe", dp, None, "tensor"),
            P("pipe", dp, "tensor"),
            P("pipe", dp),
            P("pipe", dp, None),
            P("pipe", None, dp, "tensor"),
            P("pipe", None, dp, "tensor"),
        ),
        out_specs=(
            P("pipe", dp, "tensor", None),
            P("pipe", dp, "tensor", None),
            P("pipe", dp),
            P("pipe", dp, None, "tensor"),
            P("pipe", dp, "tensor"),
            P("pipe", dp),
            P("pipe", dp, None),
            P("pipe", None, dp, "tensor"),
            P("pipe", None, dp, "tensor"),
        ),
        check_vma=False,
    )
```

```python
import functools
import math

import jax
import jax.numpy as jnp
from jax import lax
from jax.experimental import pallas as pl
from jax.experimental.pallas import tpu as pltpu
from jax.sharding import Mesh
from jax.sharding import PartitionSpec as P

D = 768
DH = 64
E = 4
LEN = 256
HALF = 128
PAD = 96
QKV = 1152
OUT = 384
SMALL = 256
ATTN = QKV + OUT + SMALL
FFH = 1536
MOE = 2 * FFH
QUARTER = 512

norm_eps = 1e-06
f32 = jnp.float32
bf16 = jnp.bfloat16
COLUMN = ("pipe", "core", "tensor")


def column_pairs(target):
    pairs = []
    for p in range(2):
        for c in range(2):
            for t in range(2):
                p2, c2, t2 = target(p, c, t)
                pairs.append((p * 4 + c * 2 + t, p2 * 4 + c2 * 2 + t2))
    return pairs


def column_send(array, target):
    return lax.ppermute(array, COLUMN, column_pairs(target))


def core_swap(array):
    return lax.ppermute(array, "core", [(0, 1), (1, 0)])


def chip_swap(array, k):
    return lax.ppermute(array, ("pipe", "tensor"), [(i, i ^ k) for i in range(4)])


def axis_swap(array, axis, k):
    return lax.ppermute(array, axis, [(i, i ^ k) for i in range(4)])


def scatter_axis(whole, axis, dim):
    me = lax.axis_index(axis)
    parts = [lax.dynamic_index_in_dim(whole, me ^ k, dim, keepdims=False) for k in range(4)]
    got = [parts[0]] + [axis_swap(parts[k], axis, k) for k in (1, 2, 3)]
    return sum(part.astype(f32) for part in got).astype(bf16)


def scatter_first(whole, axis):
    return scatter_axis(whole.reshape(4, 4, -1, whole.shape[1]), axis, "xy".index(axis))


def rms_scale(values):
    return lax.rsqrt(jnp.mean(values * values, axis=-1, keepdims=True) + norm_eps)


def norm_back(grad_normed, values, scale_rows, gain):
    normal = values * scale_rows
    weighted = grad_normed * gain
    grad_values = scale_rows * (
        weighted - normal * jnp.mean(weighted * normal, axis=-1, keepdims=True)
    )
    return grad_values, jnp.sum(grad_normed * normal, axis=0)


def matmul(left, right, dims):
    return lax.dot_general(left, right, ((dims[:1], dims[1:]), ((), ())), preferred_element_type=f32)


def pair_sum(partial):
    mine = partial.astype(bf16)
    return mine.astype(f32) + core_swap(mine).astype(f32)


def to_experts(*arrays):
    parts = [
        jnp.stack([rows[k * PAD : (k + 1) * PAD] for rows in arrays]) for k in range(4)
    ]
    parts = [parts[0]] + [chip_swap(parts[k], k) for k in (1, 2, 3)]
    found = [
        jnp.concatenate([part[i] for part in parts], axis=0) for i in range(len(arrays))
    ]
    return found if len(arrays) > 1 else found[0]


PAIR = 2 * DH
SCALE = 1.0 / math.sqrt(DH)


def dot(left, right, dims):
    return lax.dot_general(left, right, ((dims[:1], dims[1:]), ((), ())), preferred_element_type=f32)


def first_head():
    return lax.broadcasted_iota(jnp.int32, (LEN, PAIR), 1) < DH


def head_probs(query, key):
    scores = dot(query, key, (1, 1)) * SCALE
    exponent = jnp.exp(scores - jnp.max(scores, axis=-1, keepdims=True))
    return exponent / jnp.sum(exponent, axis=-1, keepdims=True)


def attend_kernel(
    layer, x_ref, weights_ref, part_ref, normed_ref, packed_ref, context_ref, small_ref, attn_ref, sem
):
    copy = pltpu.make_async_copy(weights_ref.at[:, pl.ds(layer * ATTN, ATTN)], attn_ref, sem)
    copy.start()
    values = x_ref[...]
    scale = lax.rsqrt(jnp.mean(values * values, axis=-1, keepdims=True) + norm_eps)
    copy.wait()
    small = jnp.transpose(attn_ref[:, QKV + OUT : QKV + OUT + 128].astype(f32))[:8]
    small_ref[...] = small
    normed = (values * scale * small[:1]).astype(bf16)
    normed_ref[...] = normed
    packed_ref[...] = dot(normed, attn_ref[:, :QKV], (1, 0)).astype(bf16)
    low = first_head()
    for pair in range(OUT // PAIR):
        at = pair * PAIR
        query = packed_ref[:, at : at + PAIR]
        key = packed_ref[:, OUT + at : OUT + at + PAIR]
        value = packed_ref[:, 2 * OUT + at : 2 * OUT + at + PAIR]
        none = jnp.zeros_like(query)
        parts = []
        for head in range(2):
            mine = low if head == 0 else ~low
            probs = head_probs(jnp.where(mine, query, none), key).astype(bf16)
            parts.append(dot(probs, value, (1, 0)))
        context_ref[:, at : at + PAIR] = jnp.where(low, parts[0], parts[1]).astype(bf16)
    part_ref[...] = dot(context_ref[...], attn_ref[:, QKV : QKV + OUT], (1, 1)).astype(bf16)


VMEM = pl.BlockSpec(memory_space=pltpu.VMEM)
HBM = pl.BlockSpec(memory_space=pltpu.HBM)


def attend(inputs, weights, layer):
    shape = jax.ShapeDtypeStruct
    return pl.pallas_call(
        functools.partial(attend_kernel, layer),
        in_specs=[VMEM, HBM],
        out_specs=(VMEM,) * 6,
        out_shape=(
            shape((LEN, D), bf16),
            shape((LEN, D), bf16),
            shape((LEN, QKV), bf16),
            shape((LEN, OUT), bf16),
            shape((8, D), f32),
            shape((D, ATTN), bf16),
        ),
        scratch_shapes=[pltpu.SemaphoreType.DMA],
        compiler_params=pltpu.CompilerParams(vmem_limit_bytes=24 * 2**20),
        cost_estimate=pl.CostEstimate(
            flops=2 * LEN * D * (QKV + OUT), bytes_accessed=6 * 2**20, transcendentals=6 * LEN * LEN
        ),
        name="attend",
    )(inputs, pltpu.with_memory_space_constraint(weights, pltpu.HBM))


def attend_back_kernel(grad_ref, attn_ref, packed_ref, part_ref, grads_ref, heads_ref):
    heads_ref[...] = dot(grad_ref[...], attn_ref[:, QKV : QKV + OUT], (1, 0)).astype(bf16)
    low = first_head()
    for pair in range(OUT // PAIR):
        at = pair * PAIR
        query = packed_ref[:, at : at + PAIR]
        key = packed_ref[:, OUT + at : OUT + at + PAIR]
        value = packed_ref[:, 2 * OUT + at : 2 * OUT + at + PAIR]
        grad = heads_ref[:, at : at + PAIR]
        none = jnp.zeros_like(query)
        found = []
        for head in range(2):
            mine = low if head == 0 else ~low
            probs = head_probs(jnp.where(mine, query, none), key)
            grad_probs = dot(jnp.where(mine, grad, none), value, (1, 1))
            inner = jnp.sum(grad_probs * probs, axis=-1, keepdims=True)
            grad_scores = (probs * (grad_probs - inner)).astype(bf16)
            found.append(
                (
                    dot(grad_scores, key, (1, 0)) * SCALE,
                    dot(grad_scores, query, (0, 0)) * SCALE,
                    dot(probs.astype(bf16), grad, (0, 0)),
                )
            )
        for j in range(3):
            both = jnp.where(low, found[0][j], found[1][j]).astype(bf16)
            grads_ref[:, j * OUT + at : j * OUT + at + PAIR] = both
    part_ref[...] = dot(grads_ref[...], attn_ref[:, :QKV], (1, 1)).astype(bf16)


def attend_back(grad, attn, packed):
    shape = jax.ShapeDtypeStruct
    return pl.pallas_call(
        attend_back_kernel,
        out_shape=(shape((LEN, D), bf16), shape((LEN, QKV), bf16)),
        scratch_shapes=[pltpu.VMEM((LEN, OUT), bf16)],
        compiler_params=pltpu.CompilerParams(vmem_limit_bytes=24 * 2**20),
        cost_estimate=pl.CostEstimate(
            flops=2 * LEN * D * (QKV + OUT), bytes_accessed=6 * 2**20, transcendentals=6 * LEN * LEN
        ),
        name="attend_back",
    )(grad, attn, packed)


TILE = 256


def expert_grads_kernel(at, filled_ref, hidden_ref, slots_ref, active_ref, *rest):
    out_ref, tiles, sems = rest[-3:]
    copies = []
    for i in range(D // TILE):
        rows = slice(i * TILE, (i + 1) * TILE)
        tiles[rows, :FFH] = dot(filled_ref[:, rows], hidden_ref[...], (0, 0)).astype(bf16)
        tiles[rows, FFH:] = dot(slots_ref[:, rows], active_ref[...], (0, 0)).astype(bf16)
        copy = pltpu.make_async_copy(
            tiles.at[pl.ds(i * TILE, TILE)],
            out_ref.at[pl.ds(i * TILE, TILE), pl.ds(at, MOE)],
            sems.at[i],
        )
        copy.start()
        copies.append(copy)
    for copy in copies:
        copy.wait()


def attend_grads_kernel(at, normed_ref, grads_ref, proj_ref, context_ref, small_ref, *rest):
    out_ref, tiles, sems = rest[-3:]
    tiles[:, :QKV] = dot(normed_ref[...], grads_ref[...], (0, 0)).astype(bf16)
    tiles[:, QKV : QKV + OUT] = dot(proj_ref[...], context_ref[...], (0, 0)).astype(bf16)
    rows = jnp.concatenate([small_ref[...], jnp.zeros((120, D), f32)], axis=0)
    tiles[:, QKV + OUT : QKV + OUT + 128] = jnp.transpose(rows).astype(bf16)
    tiles[:, QKV + OUT + 128 :] = jnp.zeros((D, tiles.shape[1] - QKV - OUT - 128), bf16)
    copy = pltpu.make_async_copy(tiles, out_ref.at[:, pl.ds(at, tiles.shape[1])], sems.at[0])
    copy.start()
    copy.wait()


def grads_into(kernel, name, columns, operands, buffer, width, at):
    count = len(operands)
    if buffer is not None:
        operands = operands + [buffer]
    return pl.pallas_call(
        functools.partial(kernel, at),
        in_specs=[VMEM] * count + [HBM] * (len(operands) - count),
        out_specs=HBM,
        out_shape=pltpu.HBM((D, width), bf16),
        scratch_shapes=[
            pltpu.VMEM((D, columns), bf16),
            pltpu.SemaphoreType.DMA((D // TILE,)),
        ],
        input_output_aliases={} if buffer is None else {count: 0},
        compiler_params=pltpu.CompilerParams(vmem_limit_bytes=24 * 2**20),
        cost_estimate=pl.CostEstimate(
            flops=2 * E * PAD * D * columns, bytes_accessed=9 * 2**20, transcendentals=0
        ),
        name=name,
    )(*operands)


def expert_grads(operands, buffer, width, at):
    return grads_into(expert_grads_kernel, "expert_grads", MOE, operands, buffer, width, at)


def attend_grads(operands, buffer, width, at):
    columns = ATTN if buffer is not None else width
    return grads_into(attend_grads_kernel, "attend_grads", columns, operands, buffer, width, at)


def attention(inputs, weights, layer, onehot):
    part, normed, packed, context, small, attn = attend(inputs, weights, layer)
    g_moe, w_router = small[1:2], small[2 : 2 + E].astype(bf16)
    middle = inputs + pair_sum(part)
    scale_mid = rms_scale(middle)
    mixed = (middle * scale_mid * g_moe).astype(bf16)
    logits = matmul(mixed, w_router, (1, 1))
    exponent = jnp.exp(logits - jnp.max(logits, axis=-1, keepdims=True))
    router_probs = exponent / jnp.sum(exponent, axis=-1, keepdims=True)
    gate = jnp.sum(onehot * router_probs, axis=-1, keepdims=True)
    return (
        inputs, small, normed, packed, context, middle, scale_mid, mixed, router_probs, gate, attn,
    )


def experts(filled, w_in, w_down):
    hidden = matmul(filled, w_in, (1, 0))
    cdf = 0.5 * (1.0 + lax.erf(hidden * (1.0 / math.sqrt(2.0))))
    activated = (hidden * cdf).astype(bf16)
    slope = cdf + hidden * jnp.exp(-0.5 * hidden * hidden) * (1.0 / math.sqrt(2.0 * math.pi))
    return activated, slope, matmul(activated, w_down, (1, 1)).astype(bf16)


def experts_back(grad_slots, slope, w_in, w_down):
    grad_hidden = (matmul(grad_slots, w_down, (1, 0)) * slope).astype(bf16)
    return grad_hidden, matmul(grad_hidden, w_in, (1, 1)).astype(bf16)


def to_slots(table, rows):
    return matmul(table, rows, (1, 0)).astype(bf16)


def from_slots(table, slots):
    return matmul(table, slots, (0, 0)).astype(bf16)


def mixed_back(grad_out, grad_mixed, combined, onehot, kept):
    inputs, small, normed, packed, context, middle, scale_mid, mixed, router_probs, gate, attn = kept
    grad_gate = jnp.sum(grad_out * combined, axis=-1, keepdims=True)
    grad_logits = router_probs * (onehot - gate) * grad_gate
    grad_w_router = lax.dot_general(
        grad_logits, mixed.astype(f32), (((0,), (0,)), ((), ())), precision=lax.Precision.HIGHEST
    )
    g_moe, w_router = small[1:2], small[2 : 2 + E]
    back_rows = sum(grad_logits[:, e : e + 1] * w_router[e][None, :] for e in range(E))
    grad_norm, grad_g_moe = norm_back(grad_mixed + back_rows, middle, scale_mid, g_moe)
    return grad_out + grad_norm, grad_w_router, grad_g_moe


def attention_back(grad_middle, kept, grad_w_router, grad_g_moe, buffer, width, at):
    inputs, small, normed, packed, context, middle, scale_mid, mixed, router_probs, gate, attn = kept
    proj = grad_middle.astype(bf16)
    part, grads = attend_back(proj, attn, packed)
    grad_normed = pair_sum(part)
    grad_norm, grad_g_attn = norm_back(grad_normed, inputs, rms_scale(inputs), small[:1])
    rows = jnp.concatenate(
        [grad_g_attn[None], grad_g_moe[None], grad_w_router, jnp.zeros((6 - E, D), f32)], axis=0
    )
    buffer = attend_grads([normed, grads, proj, context, rows], buffer, width, at)
    return grad_middle + grad_norm, buffer


def by_layer(p, near, far):
    return jnp.where(p == 0, near, far), jnp.where(p == 0, far, near)


def on_device(tokens, cotangent, routes, g_attn, w_qkv, w_out, g_moe, w_router, w_in, w_down):
    p, c, t = lax.axis_index("pipe"), lax.axis_index("core"), lax.axis_index("tensor")
    chip = p * 2 + t

    def spread(chunk_of):
        got = []
        for k in range(4):
            k1, k0 = k >> 1, k & 1
            got.append(column_send(chunk_of(k), lambda p, c, t: (p ^ k1, t, c ^ k0)))
        layers = []
        for first, second in ((by_layer(p, got[0], got[2])), (by_layer(p, got[1], got[3]))):
            layers.append((first, second))
        return [
            jnp.concatenate(
                [
                    jnp.where(t == 0, layers[0][l], layers[1][l]),
                    jnp.where(t == 0, layers[1][l], layers[0][l]),
                ],
                axis=0,
            )
            for l in range(2)
        ]

    small = jnp.concatenate([g_attn[0][:, None], g_moe[0][:, None], w_router[0]], axis=1)
    small = jnp.pad(small, ((0, 0), (0, SMALL - small.shape[1])))

    def chunk_of(k):
        expert = (p * 2 + c) ^ k
        return jnp.concatenate(
            [
                w_qkv[0].reshape(-1, QKV),
                w_out[0],
                small,
                lax.dynamic_index_in_dim(w_in[0], expert, 0, keepdims=False),
                lax.dynamic_index_in_dim(w_down[0], expert, 0, keepdims=False),
            ],
            axis=1,
        )

    blocks = spread(chunk_of)
    cut = lambda l, at, end: blocks[l][:, at:end]
    weights = lax.all_gather(
        jnp.concatenate([cut(0, 0, ATTN), cut(1, 0, ATTN), cut(0, ATTN, ATTN + MOE)], axis=1),
        ("x", "y"), axis=0, tiled=True,
    )
    late = lax.all_gather(cut(1, ATTN, ATTN + MOE), ("x", "y"), axis=0, tiled=True)

    def to_owner(rows):
        got = [column_send(rows, lambda p, c, t, j=j: (p, t ^ j, c)) for j in range(2)]
        return jnp.where(c == 0, got[0], got[1]), jnp.where(c == 0, got[1], got[0])

    own_routes = routes[0, :, :, 0].astype(bf16)
    far_routes = lax.ppermute(own_routes, "pipe", [(0, 1), (1, 0)])
    route_pair = jnp.stack(by_layer(p, own_routes, far_routes))
    route_rows = lax.dynamic_index_in_dim(route_pair, p, 1, keepdims=False)
    own_tokens = lax.dynamic_index_in_dim(tokens, p, 0, keepdims=False)
    extra = jnp.pad(route_rows.reshape(1, 2 * HALF), ((0, 15), (0, D - 2 * HALF)))
    low_rows, high_rows = to_owner(jnp.concatenate([own_tokens, extra], axis=0))
    inputs = jnp.concatenate([low_rows[:HALF], high_rows[:HALF]], axis=0).astype(f32)
    tables, onehots = [], []
    earlier = (
        lax.broadcasted_iota(jnp.int32, (LEN, LEN), 0)
        < lax.broadcasted_iota(jnp.int32, (LEN, LEN), 1)
    ).astype(bf16)
    for l in range(2):
        cut = slice(l * HALF, (l + 1) * HALF)
        ids = jnp.concatenate([low_rows[HALF, cut], high_rows[HALF, cut]]).astype(jnp.int32)
        picks = (ids[None, :] == jnp.arange(E, dtype=jnp.int32)[:, None]).astype(f32)
        before = matmul(picks.astype(bf16), earlier, (1, 0))
        rank = jnp.sum(before * picks, axis=0).astype(jnp.int32)
        place = (ids ^ chip) * PAD + rank
        tables.append(
            (place[None, :] == jnp.arange(E * PAD, dtype=jnp.int32)[:, None]).astype(bf16)
        )
        onehots.append(picks.T)

    cot_rows = lax.dynamic_index_in_dim(cotangent, p, 0, keepdims=False)
    grad_out = jnp.concatenate(to_owner(cot_rows), axis=0).astype(f32)

    inputs, grad_out = lax.optimization_barrier((inputs, grad_out))
    in_first, down_first = weights[:, 2 * ATTN : 2 * ATTN + FFH], weights[:, 2 * ATTN + FFH :]
    in_second, down_second = late[:, :FFH], late[:, FFH:]

    first = attention(inputs, weights, 0, onehots[0])
    filled_first = to_experts(to_slots(tables[0], first[7]))
    active_first, slope_first, out_slots = experts(filled_first, in_first, down_first)
    combined_first = pair_sum(from_slots(tables[0], to_experts(out_slots)))
    first_out = (first[5] + first[9] * combined_first).astype(bf16)

    second = attention(first_out.astype(f32), weights, 1, onehots[1])
    filled, grad_slots = to_experts(
        to_slots(tables[1], second[7]),
        to_slots(tables[1], (second[9] * grad_out).astype(bf16)),
    )
    activated, slope, out_slots = experts(filled, in_second, down_second)
    grad_hidden, grad_filled = experts_back(grad_slots, slope, in_second, down_second)
    width = 2 * MOE + ATTN
    found = to_experts(out_slots, grad_filled)
    buffer = expert_grads([filled, grad_hidden, grad_slots, activated], None, width, 0)
    found, buffer = lax.optimization_barrier((found, buffer))
    sums = pair_sum(jnp.concatenate([from_slots(tables[1], rows) for rows in found], axis=1))
    combined, grad_mixed = sums[:, :D], sums[:, D:]
    second_out = (second[5] + second[9] * combined).astype(bf16)

    def to_home(first, second):
        cut = lambda rows: lax.dynamic_slice_in_dim(rows, c * HALF, HALF, 0)
        near, far = by_layer(p, cut(first), cut(second))
        near = column_send(near, lambda p, c, t: (p, t, c))
        far = column_send(far, lambda p, c, t: (1 - p, t, c))
        return jnp.stack(by_layer(p, near, far))

    def reduce_plane(whole):
        return lax.optimization_barrier(
            lax.psum_scatter(whole, ("x", "y"), scatter_dimension=0, tiled=True)
        )

    grad_mid, g_router, gg_moe = mixed_back(grad_out, grad_mixed, combined, onehots[1], second)
    grad_x, buffer = attention_back(
        grad_mid, second, g_router, gg_moe, buffer, width, MOE
    )
    second_grad = grad_x.astype(bf16)
    grad_out = second_grad.astype(f32)
    grad_slots = to_experts(to_slots(tables[0], (first[9] * grad_out).astype(bf16)))
    grad_hidden, grad_filled = experts_back(grad_slots, slope_first, in_first, down_first)
    grad_filled = to_experts(grad_filled)
    buffer = expert_grads(
        [filled_first, grad_hidden, grad_slots, active_first], buffer, width, MOE + ATTN
    )
    grad_filled, buffer = lax.optimization_barrier((grad_filled, buffer))
    reduced = reduce_plane(buffer)
    grad_mixed = pair_sum(from_slots(tables[0], grad_filled))
    grad_mid, g_router, gg_moe = mixed_back(
        grad_out, grad_mixed, combined_first, onehots[0], first
    )
    grad_x, attn_whole = attention_back(
        grad_mid, first, g_router, gg_moe, None, 4 * QUARTER, 0
    )
    quarters = [
        lax.dynamic_slice_in_dim(attn_whole, (chip ^ k) * QUARTER, QUARTER, 1) for k in range(4)
    ]
    quarters = [quarters[0]] + [chip_swap(quarters[k], k) for k in (1, 2, 3)]
    attn_whole = sum(part.astype(f32) for part in quarters).astype(bf16)
    over_x = scatter_axis(scatter_first(attn_whole[:, : QUARTER // 2], "x"), "y", 0)
    over_y = scatter_axis(scatter_first(attn_whole[:, QUARTER // 2 :], "y"), "x", 0)
    attn_first = jnp.concatenate([over_x, over_y], axis=1)
    first_out, second_out, grad_x = lax.optimization_barrier((first_out, second_out, grad_x))
    hidden_states = to_home(first_out, second_out)
    grad_inputs = to_home(grad_x.astype(bf16), second_grad).astype(f32)

    first_all = jnp.concatenate(
        [reduced[:, MOE + ATTN :], attn_first, jnp.zeros((48, ATTN - QUARTER), bf16)], axis=1
    )
    second_all = reduced[:, : MOE + ATTN]
    attn_sum = jnp.zeros((24, ATTN), f32)
    attn_all = jnp.zeros((24, 4 * QUARTER), bf16)
    moe_all = jnp.zeros((E, 24, MOE), bf16)
    for k in range(4):
        k1, k0 = k >> 1, k & 1
        piece = jnp.where((p ^ k1) == 0, first_all, second_all)
        piece = lax.dynamic_slice_in_dim(piece, (t ^ k0) * 24, 24, 0)
        got = column_send(piece, lambda p, c, t: (p ^ k1, t ^ k0, c))
        source = (p * 2 + c) ^ k
        moe_all = lax.dynamic_update_index_in_dim(moe_all, got[:, :MOE], source, 0)
        attn_sum = attn_sum + got[:, MOE:].astype(f32)
        attn_all = lax.dynamic_update_slice_in_dim(
            attn_all, got[:, MOE : MOE + QUARTER], source * QUARTER, 1
        )
    attn_sum = jnp.where(p == 0, attn_all[:, :ATTN].astype(f32), attn_sum)
    small = attn_sum[:, QKV + OUT :]
    return (
        hidden_states[None],
        grad_inputs[None],
        small[:, 0][None],
        attn_sum[:, :QKV].reshape(24, 3, OUT)[None],
        attn_sum[:, QKV : QKV + OUT][None],
        small[:, 1][None],
        small[:, 2 : 2 + E][None],
        moe_all[:, :, :FFH].astype(f32)[None],
        moe_all[:, :, FFH:].astype(f32)[None],
    )


def solution(mesh):
    grid = Mesh(mesh.devices.reshape(2, 4, 4, 2, 2), ("pipe", "x", "y", "core", "tensor"))
    dp = ("x", "y", "core")
    return jax.shard_map(
        on_device,
        mesh=grid,
        in_specs=(
            P(dp, "tensor", None),
            P(dp, "tensor", None),
            P("pipe", dp, "tensor", None),
            P("pipe", dp),
            P("pipe", dp, None, "tensor"),
            P("pipe", dp, "tensor"),
            P("pipe", dp),
            P("pipe", dp, None),
            P("pipe", None, dp, "tensor"),
            P("pipe", None, dp, "tensor"),
        ),
        out_specs=(
            P("pipe", dp, "tensor", None),
            P("pipe", dp, "tensor", None),
            P("pipe", dp),
            P("pipe", dp, None, "tensor"),
            P("pipe", dp, "tensor"),
            P("pipe", dp),
            P("pipe", dp, None),
            P("pipe", None, dp, "tensor"),
            P("pipe", None, dp, "tensor"),
        ),
        check_vma=False,
    )
```

```python
import functools
import math

import jax
import jax.numpy as jnp
from jax import lax
from jax.experimental import pallas as pl
from jax.experimental.pallas import tpu as pltpu
from jax.sharding import Mesh
from jax.sharding import PartitionSpec as P

D = 768
DH = 64
E = 4
LEN = 256
HALF = 128
PAD = 88
QKV = 1152
OUT = 384
SMALL = 256
ATTN = QKV + OUT + SMALL
FFH = 1536
MOE = 2 * FFH
QUARTER = 512

norm_eps = 1e-06
f32 = jnp.float32
bf16 = jnp.bfloat16
COLUMN = ("pipe", "core", "tensor")


def column_pairs(target):
    pairs = []
    for p in range(2):
        for c in range(2):
            for t in range(2):
                p2, c2, t2 = target(p, c, t)
                pairs.append((p * 4 + c * 2 + t, p2 * 4 + c2 * 2 + t2))
    return pairs


def column_send(array, target):
    return lax.ppermute(array, COLUMN, column_pairs(target))


def core_swap(array):
    return lax.ppermute(array, "core", [(0, 1), (1, 0)])


def chip_swap(array, k):
    return lax.ppermute(array, ("pipe", "tensor"), [(i, i ^ k) for i in range(4)])


def axis_swap(array, axis, k):
    return lax.ppermute(array, axis, [(i, i ^ k) for i in range(4)])


def gather_axis(block, axis, dim):
    me = lax.axis_index(axis)
    whole = jnp.zeros(block.shape[:dim] + (4,) + block.shape[dim:], block.dtype)
    for k in range(4):
        part = block if k == 0 else axis_swap(block, axis, k)
        whole = lax.dynamic_update_index_in_dim(whole, part, me ^ k, dim)
    return whole


def scatter_axis(whole, axis, dim):
    me = lax.axis_index(axis)
    parts = [lax.dynamic_index_in_dim(whole, me ^ k, dim, keepdims=False) for k in range(4)]
    got = [parts[0]] + [axis_swap(parts[k], axis, k) for k in (1, 2, 3)]
    return sum(part.astype(f32) for part in got).astype(bf16)


def scatter_first(whole, axis):
    return scatter_axis(whole.reshape(4, 4, -1, whole.shape[1]), axis, "xy".index(axis))


def rms_scale(values):
    return lax.rsqrt(jnp.mean(values * values, axis=-1, keepdims=True) + norm_eps)


def norm_back(grad_normed, values, scale_rows, gain):
    normal = values * scale_rows
    weighted = grad_normed * gain
    grad_values = scale_rows * (
        weighted - normal * jnp.mean(weighted * normal, axis=-1, keepdims=True)
    )
    return grad_values, jnp.sum(grad_normed * normal, axis=0)


def matmul(left, right, dims):
    return lax.dot_general(left, right, ((dims[:1], dims[1:]), ((), ())), preferred_element_type=f32)


def pair_sum(partial):
    mine = partial.astype(bf16)
    return mine.astype(f32) + core_swap(mine).astype(f32)


def to_experts(*arrays):
    parts = [
        jnp.stack([rows[k * PAD : (k + 1) * PAD] for rows in arrays]) for k in range(4)
    ]
    parts = [parts[0]] + [chip_swap(parts[k], k) for k in (1, 2, 3)]
    found = [
        jnp.concatenate([part[i] for part in parts], axis=0) for i in range(len(arrays))
    ]
    return found if len(arrays) > 1 else found[0]


PAIR = 2 * DH
SCALE = 1.0 / math.sqrt(DH)


def dot(left, right, dims):
    return lax.dot_general(left, right, ((dims[:1], dims[1:]), ((), ())), preferred_element_type=f32)


def first_head():
    return lax.broadcasted_iota(jnp.int32, (LEN, PAIR), 1) < DH


def head_probs(query, key):
    scores = dot(query, key, (1, 1)) * SCALE
    exponent = jnp.exp(scores - jnp.max(scores, axis=-1, keepdims=True))
    return exponent / jnp.sum(exponent, axis=-1, keepdims=True)


def attend_kernel(
    x_ref, weights_ref, part_ref, normed_ref, packed_ref, context_ref, small_ref, attn_ref, *rest
):
    sems = rest[-1]
    copy = pltpu.make_async_copy(weights_ref.at[:, pl.ds(0, ATTN)], attn_ref, sems.at[0])
    copy.start()
    if len(rest) > 1:
        moe = pltpu.make_async_copy(weights_ref.at[:, pl.ds(ATTN, MOE)], rest[0], sems.at[1])
        moe.start()
    values = x_ref[...]
    scale = lax.rsqrt(jnp.mean(values * values, axis=-1, keepdims=True) + norm_eps)
    copy.wait()
    small = jnp.transpose(attn_ref[:, QKV + OUT : QKV + OUT + 128].astype(f32))[:8]
    small_ref[...] = small
    normed = (values * scale * small[:1]).astype(bf16)
    normed_ref[...] = normed
    packed_ref[...] = dot(normed, attn_ref[:, :QKV], (1, 0)).astype(bf16)
    low = first_head()
    for pair in range(OUT // PAIR):
        at = pair * PAIR
        query = packed_ref[:, at : at + PAIR]
        key = packed_ref[:, OUT + at : OUT + at + PAIR]
        value = packed_ref[:, 2 * OUT + at : 2 * OUT + at + PAIR]
        none = jnp.zeros_like(query)
        parts = []
        for head in range(2):
            mine = low if head == 0 else ~low
            probs = head_probs(jnp.where(mine, query, none), key).astype(bf16)
            parts.append(dot(probs, value, (1, 0)))
        context_ref[:, at : at + PAIR] = jnp.where(low, parts[0], parts[1]).astype(bf16)
    part_ref[...] = dot(context_ref[...], attn_ref[:, QKV : QKV + OUT], (1, 1)).astype(bf16)
    if len(rest) > 1:
        moe.wait()


VMEM = pl.BlockSpec(memory_space=pltpu.VMEM)
HBM = pl.BlockSpec(memory_space=pltpu.HBM)


def attend(inputs, weights, with_experts):
    shape = jax.ShapeDtypeStruct
    moe = (shape((D, MOE), bf16),) if with_experts else ()
    return pl.pallas_call(
        attend_kernel,
        in_specs=[VMEM, HBM],
        out_specs=(VMEM,) * (6 + len(moe)),
        out_shape=(
            shape((LEN, D), bf16),
            shape((LEN, D), bf16),
            shape((LEN, QKV), bf16),
            shape((LEN, OUT), bf16),
            shape((8, D), f32),
            shape((D, ATTN), bf16),
        )
        + moe,
        scratch_shapes=[pltpu.SemaphoreType.DMA((2,))],
        compiler_params=pltpu.CompilerParams(vmem_limit_bytes=24 * 2**20),
        cost_estimate=pl.CostEstimate(
            flops=2 * LEN * D * (QKV + OUT), bytes_accessed=6 * 2**20, transcendentals=6 * LEN * LEN
        ),
        name="attend",
    )(inputs, pltpu.with_memory_space_constraint(weights, pltpu.HBM))


def attend_back_kernel(grad_ref, attn_ref, packed_ref, part_ref, grads_ref, heads_ref):
    heads_ref[...] = dot(grad_ref[...], attn_ref[:, QKV : QKV + OUT], (1, 0)).astype(bf16)
    low = first_head()
    for pair in range(OUT // PAIR):
        at = pair * PAIR
        query = packed_ref[:, at : at + PAIR]
        key = packed_ref[:, OUT + at : OUT + at + PAIR]
        value = packed_ref[:, 2 * OUT + at : 2 * OUT + at + PAIR]
        grad = heads_ref[:, at : at + PAIR]
        none = jnp.zeros_like(query)
        found = []
        for head in range(2):
            mine = low if head == 0 else ~low
            probs = head_probs(jnp.where(mine, query, none), key)
            grad_probs = dot(jnp.where(mine, grad, none), value, (1, 1))
            inner = jnp.sum(grad_probs * probs, axis=-1, keepdims=True)
            grad_scores = (probs * (grad_probs - inner)).astype(bf16)
            found.append(
                (
                    dot(grad_scores, key, (1, 0)) * SCALE,
                    dot(grad_scores, query, (0, 0)) * SCALE,
                    dot(probs.astype(bf16), grad, (0, 0)),
                )
            )
        for j in range(3):
            both = jnp.where(low, found[0][j], found[1][j]).astype(bf16)
            grads_ref[:, j * OUT + at : j * OUT + at + PAIR] = both
    part_ref[...] = dot(grads_ref[...], attn_ref[:, :QKV], (1, 1)).astype(bf16)


def attend_back(grad, attn, packed):
    shape = jax.ShapeDtypeStruct
    return pl.pallas_call(
        attend_back_kernel,
        out_shape=(shape((LEN, D), bf16), shape((LEN, QKV), bf16)),
        scratch_shapes=[pltpu.VMEM((LEN, OUT), bf16)],
        compiler_params=pltpu.CompilerParams(vmem_limit_bytes=24 * 2**20),
        cost_estimate=pl.CostEstimate(
            flops=2 * LEN * D * (QKV + OUT), bytes_accessed=6 * 2**20, transcendentals=6 * LEN * LEN
        ),
        name="attend_back",
    )(grad, attn, packed)


TILE = 256


def expert_grads_kernel(at, filled_ref, hidden_ref, slots_ref, active_ref, *rest):
    out_ref, tiles, sems = rest[-3:]
    copies = []
    for i in range(D // TILE):
        rows = slice(i * TILE, (i + 1) * TILE)
        tiles[rows, :FFH] = dot(filled_ref[:, rows], hidden_ref[...], (0, 0)).astype(bf16)
        tiles[rows, FFH:] = dot(slots_ref[:, rows], active_ref[...], (0, 0)).astype(bf16)
        copy = pltpu.make_async_copy(
            tiles.at[pl.ds(i * TILE, TILE)],
            out_ref.at[pl.ds(i * TILE, TILE), pl.ds(at, MOE)],
            sems.at[i],
        )
        copy.start()
        copies.append(copy)
    for copy in copies:
        copy.wait()


def attend_grads_kernel(at, normed_ref, grads_ref, proj_ref, context_ref, small_ref, *rest):
    out_ref, tiles, sems = rest[-3:]
    tiles[:, :QKV] = dot(normed_ref[...], grads_ref[...], (0, 0)).astype(bf16)
    tiles[:, QKV : QKV + OUT] = dot(proj_ref[...], context_ref[...], (0, 0)).astype(bf16)
    rows = jnp.concatenate([small_ref[...], jnp.zeros((120, D), f32)], axis=0)
    tiles[:, QKV + OUT : QKV + OUT + 128] = jnp.transpose(rows).astype(bf16)
    tiles[:, QKV + OUT + 128 :] = jnp.zeros((D, tiles.shape[1] - QKV - OUT - 128), bf16)
    copy = pltpu.make_async_copy(tiles, out_ref.at[:, pl.ds(at, tiles.shape[1])], sems.at[0])
    copy.start()
    copy.wait()


def grads_into(kernel, name, columns, operands, buffer, width, at):
    count = len(operands)
    if buffer is not None:
        operands = operands + [buffer]
    return pl.pallas_call(
        functools.partial(kernel, at),
        in_specs=[VMEM] * count + [HBM] * (len(operands) - count),
        out_specs=HBM,
        out_shape=pltpu.HBM((D, width), bf16),
        scratch_shapes=[
            pltpu.VMEM((D, columns), bf16),
            pltpu.SemaphoreType.DMA((D // TILE,)),
        ],
        input_output_aliases={} if buffer is None else {count: 0},
        compiler_params=pltpu.CompilerParams(vmem_limit_bytes=24 * 2**20),
        cost_estimate=pl.CostEstimate(
            flops=2 * E * PAD * D * columns, bytes_accessed=9 * 2**20, transcendentals=0
        ),
        name=name,
    )(*operands)


def expert_grads(operands, buffer, width, at):
    return grads_into(expert_grads_kernel, "expert_grads", MOE, operands, buffer, width, at)


def attend_grads(operands, buffer, width, at):
    columns = ATTN if buffer is not None else width
    return grads_into(attend_grads_kernel, "attend_grads", columns, operands, buffer, width, at)


def attention(inputs, weights, onehot, with_experts):
    part, normed, packed, context, small, attn, *moe = attend(inputs, weights, with_experts)
    g_moe, w_router = small[1:2], small[2 : 2 + E].astype(bf16)
    middle = inputs + pair_sum(part)
    scale_mid = rms_scale(middle)
    mixed = (middle * scale_mid * g_moe).astype(bf16)
    logits = matmul(mixed, w_router, (1, 1))
    exponent = jnp.exp(logits - jnp.max(logits, axis=-1, keepdims=True))
    router_probs = exponent / jnp.sum(exponent, axis=-1, keepdims=True)
    gate = jnp.sum(onehot * router_probs, axis=-1, keepdims=True)
    kept = (
        inputs, small, normed, packed, context, middle, scale_mid, mixed, router_probs, gate, attn,
    )
    return (kept, moe[0]) if with_experts else kept


def experts(filled, w_in, w_down):
    hidden = matmul(filled, w_in, (1, 0))
    cdf = 0.5 * (1.0 + lax.erf(hidden * (1.0 / math.sqrt(2.0))))
    activated = (hidden * cdf).astype(bf16)
    slope = cdf + hidden * jnp.exp(-0.5 * hidden * hidden) * (1.0 / math.sqrt(2.0 * math.pi))
    return activated, slope, matmul(activated, w_down, (1, 1)).astype(bf16)


def experts_back(grad_slots, slope, w_in, w_down):
    grad_hidden = (matmul(grad_slots, w_down, (1, 0)) * slope).astype(bf16)
    return grad_hidden, matmul(grad_hidden, w_in, (1, 1)).astype(bf16)


def to_slots(table, rows):
    return matmul(table, rows, (1, 0)).astype(bf16)


def from_slots(table, slots):
    return matmul(table, slots, (0, 0)).astype(bf16)


def mixed_back(grad_out, grad_mixed, combined, onehot, kept):
    inputs, small, normed, packed, context, middle, scale_mid, mixed, router_probs, gate, attn = kept
    grad_gate = jnp.sum(grad_out * combined, axis=-1, keepdims=True)
    grad_logits = router_probs * (onehot - gate) * grad_gate
    grad_w_router = lax.dot_general(
        grad_logits, mixed.astype(f32), (((0,), (0,)), ((), ())), precision=lax.Precision.HIGHEST
    )
    g_moe, w_router = small[1:2], small[2 : 2 + E]
    back_rows = sum(grad_logits[:, e : e + 1] * w_router[e][None, :] for e in range(E))
    grad_norm, grad_g_moe = norm_back(grad_mixed + back_rows, middle, scale_mid, g_moe)
    return grad_out + grad_norm, grad_w_router, grad_g_moe


def attention_back(grad_middle, kept, grad_w_router, grad_g_moe, buffer, width, at):
    inputs, small, normed, packed, context, middle, scale_mid, mixed, router_probs, gate, attn = kept
    proj = grad_middle.astype(bf16)
    part, grads = attend_back(proj, attn, packed)
    grad_normed = pair_sum(part)
    grad_norm, grad_g_attn = norm_back(grad_normed, inputs, rms_scale(inputs), small[:1])
    rows = jnp.concatenate(
        [grad_g_attn[None], grad_g_moe[None], grad_w_router, jnp.zeros((6 - E, D), f32)], axis=0
    )
    buffer = attend_grads([normed, grads, proj, context, rows], buffer, width, at)
    return grad_middle + grad_norm, buffer


def by_layer(p, near, far):
    return jnp.where(p == 0, near, far), jnp.where(p == 0, far, near)


def on_device(tokens, cotangent, routes, g_attn, w_qkv, w_out, g_moe, w_router, w_in, w_down):
    p, c, t = lax.axis_index("pipe"), lax.axis_index("core"), lax.axis_index("tensor")
    chip = p * 2 + t

    def spread(chunk_of):
        got = []
        for k in range(4):
            k1, k0 = k >> 1, k & 1
            got.append(column_send(chunk_of(k), lambda p, c, t: (p ^ k1, t, c ^ k0)))
        layers = []
        for first, second in ((by_layer(p, got[0], got[2])), (by_layer(p, got[1], got[3]))):
            layers.append((first, second))
        return [
            jnp.concatenate(
                [
                    jnp.where(t == 0, layers[0][l], layers[1][l]),
                    jnp.where(t == 0, layers[1][l], layers[0][l]),
                ],
                axis=0,
            )
            for l in range(2)
        ]

    small = jnp.concatenate([g_attn[0][:, None], g_moe[0][:, None], w_router[0]], axis=1)
    small = jnp.pad(small, ((0, 0), (0, SMALL - small.shape[1])))

    def chunk_of(k):
        expert = (p * 2 + c) ^ k
        return jnp.concatenate(
            [
                w_qkv[0].reshape(-1, QKV),
                w_out[0],
                small,
                lax.dynamic_index_in_dim(w_in[0], expert, 0, keepdims=False),
                lax.dynamic_index_in_dim(w_down[0], expert, 0, keepdims=False),
            ],
            axis=1,
        )

    blocks = spread(chunk_of)
    weights = lax.all_gather(blocks[0], ("x", "y"), axis=0, tiled=True)
    late = lax.all_gather(blocks[1][:, ATTN:], ("x", "y"), axis=0, tiled=True)
    quarter = jnp.pad(blocks[1][:, :ATTN], ((0, 0), (0, 4 * QUARTER - ATTN)))
    quarter = lax.dynamic_slice_in_dim(quarter, chip * QUARTER, QUARTER, 1)
    quarter = gather_axis(gather_axis(quarter, "x", 0), "y", 1).reshape(D, QUARTER)

    def to_owner(rows):
        got = [column_send(rows, lambda p, c, t, j=j: (p, t ^ j, c)) for j in range(2)]
        return jnp.where(c == 0, got[0], got[1]), jnp.where(c == 0, got[1], got[0])

    own_routes = routes[0, :, :, 0].astype(bf16)
    far_routes = lax.ppermute(own_routes, "pipe", [(0, 1), (1, 0)])
    route_pair = jnp.stack(by_layer(p, own_routes, far_routes))
    route_rows = lax.dynamic_index_in_dim(route_pair, p, 1, keepdims=False)
    own_tokens = lax.dynamic_index_in_dim(tokens, p, 0, keepdims=False)
    extra = jnp.pad(route_rows.reshape(1, 2 * HALF), ((0, 15), (0, D - 2 * HALF)))
    low_rows, high_rows = to_owner(jnp.concatenate([own_tokens, extra], axis=0))
    inputs = jnp.concatenate([low_rows[:HALF], high_rows[:HALF]], axis=0).astype(f32)
    tables, onehots = [], []
    earlier = (
        lax.broadcasted_iota(jnp.int32, (LEN, LEN), 0)
        < lax.broadcasted_iota(jnp.int32, (LEN, LEN), 1)
    ).astype(bf16)
    for l in range(2):
        cut = slice(l * HALF, (l + 1) * HALF)
        ids = jnp.concatenate([low_rows[HALF, cut], high_rows[HALF, cut]]).astype(jnp.int32)
        picks = (ids[None, :] == jnp.arange(E, dtype=jnp.int32)[:, None]).astype(f32)
        before = matmul(picks.astype(bf16), earlier, (1, 0))
        rank = jnp.sum(before * picks, axis=0).astype(jnp.int32)
        place = (ids ^ chip) * PAD + rank
        tables.append(
            (place[None, :] == jnp.arange(E * PAD, dtype=jnp.int32)[:, None]).astype(bf16)
        )
        onehots.append(picks.T)

    cot_rows = lax.dynamic_index_in_dim(cotangent, p, 0, keepdims=False)
    grad_out = jnp.concatenate(to_owner(cot_rows), axis=0).astype(f32)

    inputs, grad_out, quarter = lax.optimization_barrier((inputs, grad_out, quarter))
    attn_second = jnp.zeros((D, 4 * QUARTER), bf16)
    for k in range(4):
        part = quarter if k == 0 else chip_swap(quarter, k)
        attn_second = lax.dynamic_update_slice_in_dim(attn_second, part, (chip ^ k) * QUARTER, 1)
    in_second, down_second = late[:, :FFH], late[:, FFH:]

    first, moe_weights = attention(inputs, weights, onehots[0], True)
    in_first, down_first = moe_weights[:, :FFH], moe_weights[:, FFH:]
    filled_first = to_experts(to_slots(tables[0], first[7]))
    active_first, slope_first, out_slots = experts(filled_first, in_first, down_first)
    combined_first = pair_sum(from_slots(tables[0], to_experts(out_slots)))
    first_out = (first[5] + first[9] * combined_first).astype(bf16)

    second = attention(first_out.astype(f32), attn_second, onehots[1], False)
    filled, grad_slots = to_experts(
        to_slots(tables[1], second[7]),
        to_slots(tables[1], (second[9] * grad_out).astype(bf16)),
    )
    activated, slope, out_slots = experts(filled, in_second, down_second)
    grad_hidden, grad_filled = experts_back(grad_slots, slope, in_second, down_second)
    width = 2 * MOE + ATTN
    found = to_experts(out_slots, grad_filled)
    buffer = expert_grads([filled, grad_hidden, grad_slots, activated], None, width, 0)
    found, buffer = lax.optimization_barrier((found, buffer))
    sums = pair_sum(jnp.concatenate([from_slots(tables[1], rows) for rows in found], axis=1))
    combined, grad_mixed = sums[:, :D], sums[:, D:]
    second_out = (second[5] + second[9] * combined).astype(bf16)

    def to_home(first, second):
        cut = lambda rows: lax.dynamic_slice_in_dim(rows, c * HALF, HALF, 0)
        near, far = by_layer(p, cut(first), cut(second))
        near = column_send(near, lambda p, c, t: (p, t, c))
        far = column_send(far, lambda p, c, t: (1 - p, t, c))
        return jnp.stack(by_layer(p, near, far))

    def reduce_plane(whole):
        return lax.optimization_barrier(
            lax.psum_scatter(whole, ("x", "y"), scatter_dimension=0, tiled=True)
        )

    grad_mid, g_router, gg_moe = mixed_back(grad_out, grad_mixed, combined, onehots[1], second)
    grad_x, buffer = attention_back(
        grad_mid, second, g_router, gg_moe, buffer, width, MOE
    )
    second_grad = grad_x.astype(bf16)
    grad_out = second_grad.astype(f32)
    grad_slots = to_experts(to_slots(tables[0], (first[9] * grad_out).astype(bf16)))
    grad_hidden, grad_filled = experts_back(grad_slots, slope_first, in_first, down_first)
    grad_filled = to_experts(grad_filled)
    buffer = expert_grads(
        [filled_first, grad_hidden, grad_slots, active_first], buffer, width, MOE + ATTN
    )
    reduced = reduce_plane(buffer)
    grad_filled, buffer = lax.optimization_barrier((grad_filled, buffer))
    grad_mixed = pair_sum(from_slots(tables[0], grad_filled))
    grad_mid, g_router, gg_moe = mixed_back(
        grad_out, grad_mixed, combined_first, onehots[0], first
    )
    grad_x, attn_whole = attention_back(
        grad_mid, first, g_router, gg_moe, None, 4 * QUARTER, 0
    )
    quarters = [
        lax.dynamic_slice_in_dim(attn_whole, (chip ^ k) * QUARTER, QUARTER, 1) for k in range(4)
    ]
    quarters = [quarters[0]] + [chip_swap(quarters[k], k) for k in (1, 2, 3)]
    attn_whole = sum(part.astype(f32) for part in quarters).astype(bf16)
    over_x = scatter_axis(scatter_first(attn_whole[:, : QUARTER // 2], "x"), "y", 0)
    over_y = scatter_axis(scatter_first(attn_whole[:, QUARTER // 2 :], "y"), "x", 0)
    attn_first = jnp.concatenate([over_x, over_y], axis=1)
    first_out, second_out, grad_x = lax.optimization_barrier((first_out, second_out, grad_x))
    hidden_states = to_home(first_out, second_out)
    grad_inputs = to_home(grad_x.astype(bf16), second_grad).astype(f32)

    first_all = jnp.concatenate(
        [reduced[:, MOE + ATTN :], attn_first, jnp.zeros((48, ATTN - QUARTER), bf16)], axis=1
    )
    second_all = reduced[:, : MOE + ATTN]
    attn_sum = jnp.zeros((24, ATTN), f32)
    attn_all = jnp.zeros((24, 4 * QUARTER), bf16)
    moe_all = jnp.zeros((E, 24, MOE), bf16)
    for k in range(4):
        k1, k0 = k >> 1, k & 1
        piece = jnp.where((p ^ k1) == 0, first_all, second_all)
        piece = lax.dynamic_slice_in_dim(piece, (t ^ k0) * 24, 24, 0)
        got = column_send(piece, lambda p, c, t: (p ^ k1, t ^ k0, c))
        source = (p * 2 + c) ^ k
        moe_all = lax.dynamic_update_index_in_dim(moe_all, got[:, :MOE], source, 0)
        attn_sum = attn_sum + got[:, MOE:].astype(f32)
        attn_all = lax.dynamic_update_slice_in_dim(
            attn_all, got[:, MOE : MOE + QUARTER], source * QUARTER, 1
        )
    attn_sum = jnp.where(p == 0, attn_all[:, :ATTN].astype(f32), attn_sum)
    small = attn_sum[:, QKV + OUT :]
    return (
        hidden_states[None],
        grad_inputs[None],
        small[:, 0][None],
        attn_sum[:, :QKV].reshape(24, 3, OUT)[None],
        attn_sum[:, QKV : QKV + OUT][None],
        small[:, 1][None],
        small[:, 2 : 2 + E][None],
        moe_all[:, :, :FFH].astype(f32)[None],
        moe_all[:, :, FFH:].astype(f32)[None],
    )


def solution(mesh):
    grid = Mesh(mesh.devices.reshape(2, 4, 4, 2, 2), ("pipe", "x", "y", "core", "tensor"))
    dp = ("x", "y", "core")
    return jax.shard_map(
        on_device,
        mesh=grid,
        in_specs=(
            P(dp, "tensor", None),
            P(dp, "tensor", None),
            P("pipe", dp, "tensor", None),
            P("pipe", dp),
            P("pipe", dp, None, "tensor"),
            P("pipe", dp, "tensor"),
            P("pipe", dp),
            P("pipe", dp, None),
            P("pipe", None, dp, "tensor"),
            P("pipe", None, dp, "tensor"),
        ),
        out_specs=(
            P("pipe", dp, "tensor", None),
            P("pipe", dp, "tensor", None),
            P("pipe", dp),
            P("pipe", dp, None, "tensor"),
            P("pipe", dp, "tensor"),
            P("pipe", dp),
            P("pipe", dp, None),
            P("pipe", None, dp, "tensor"),
            P("pipe", None, dp, "tensor"),
        ),
        check_vma=False,
    )
```

```python
import functools
import math

import jax
import jax.numpy as jnp
from jax import lax
from jax.experimental import pallas as pl
from jax.experimental.pallas import tpu as pltpu
from jax.sharding import Mesh
from jax.sharding import PartitionSpec as P

D = 768
DH = 64
E = 4
LEN = 256
HALF = 128
PAD = 88
QKV = 1152
OUT = 384
SMALL = 256
ATTN = QKV + OUT + SMALL
FFH = 1536
MOE = 2 * FFH
QUARTER = 512

norm_eps = 1e-06
f32 = jnp.float32
bf16 = jnp.bfloat16
COLUMN = ("pipe", "core", "tensor")


def column_pairs(target):
    pairs = []
    for p in range(2):
        for c in range(2):
            for t in range(2):
                p2, c2, t2 = target(p, c, t)
                pairs.append((p * 4 + c * 2 + t, p2 * 4 + c2 * 2 + t2))
    return pairs


def column_send(array, target):
    return lax.ppermute(array, COLUMN, column_pairs(target))


def core_swap(array):
    return lax.ppermute(array, "core", [(0, 1), (1, 0)])


def chip_swap(array, k):
    return lax.ppermute(array, ("pipe", "tensor"), [(i, i ^ k) for i in range(4)])


def axis_swap(array, axis, k):
    return lax.ppermute(array, axis, [(i, i ^ k) for i in range(4)])


def scatter_axis(whole, axis, dim):
    me = lax.axis_index(axis)
    parts = [lax.dynamic_index_in_dim(whole, me ^ k, dim, keepdims=False) for k in range(4)]
    got = [parts[0]] + [axis_swap(parts[k], axis, k) for k in (1, 2, 3)]
    return sum(part.astype(f32) for part in got).astype(bf16)


def scatter_first(whole, axis):
    return scatter_axis(whole.reshape(4, 4, -1, whole.shape[1]), axis, "xy".index(axis))


def rms_scale(values):
    return lax.rsqrt(jnp.mean(values * values, axis=-1, keepdims=True) + norm_eps)


def norm_back(grad_normed, values, scale_rows, gain):
    normal = values * scale_rows
    weighted = grad_normed * gain
    grad_values = scale_rows * (
        weighted - normal * jnp.mean(weighted * normal, axis=-1, keepdims=True)
    )
    return grad_values, jnp.sum(grad_normed * normal, axis=0)


def matmul(left, right, dims):
    return lax.dot_general(left, right, ((dims[:1], dims[1:]), ((), ())), preferred_element_type=f32)


def pair_sum(partial):
    mine = partial.astype(bf16)
    return mine.astype(f32) + core_swap(mine).astype(f32)


def to_experts(*arrays):
    parts = [
        jnp.stack([rows[k * PAD : (k + 1) * PAD] for rows in arrays]) for k in range(4)
    ]
    parts = [parts[0]] + [chip_swap(parts[k], k) for k in (1, 2, 3)]
    found = [
        jnp.concatenate([part[i] for part in parts], axis=0) for i in range(len(arrays))
    ]
    return found if len(arrays) > 1 else found[0]


PAIR = 2 * DH
SCALE = 1.0 / math.sqrt(DH)


def dot(left, right, dims):
    return lax.dot_general(left, right, ((dims[:1], dims[1:]), ((), ())), preferred_element_type=f32)


def first_head():
    return lax.broadcasted_iota(jnp.int32, (LEN, PAIR), 1) < DH


def head_probs(query, key):
    scores = dot(query, key, (1, 1)) * SCALE
    exponent = jnp.exp(scores - jnp.max(scores, axis=-1, keepdims=True))
    return exponent / jnp.sum(exponent, axis=-1, keepdims=True)


def attend_kernel(
    at, x_ref, weights_ref, part_ref, normed_ref, packed_ref, context_ref, small_ref, attn_ref, *rest
):
    sems = rest[-1]
    copy = pltpu.make_async_copy(weights_ref.at[:, pl.ds(at, ATTN)], attn_ref, sems.at[0])
    copy.start()
    if len(rest) > 1:
        moe = pltpu.make_async_copy(weights_ref.at[:, pl.ds(at + ATTN, MOE)], rest[0], sems.at[1])
        moe.start()
    values = x_ref[...]
    scale = lax.rsqrt(jnp.mean(values * values, axis=-1, keepdims=True) + norm_eps)
    copy.wait()
    small = jnp.transpose(attn_ref[:, QKV + OUT : QKV + OUT + 128].astype(f32))[:8]
    small_ref[...] = small
    normed = (values * scale * small[:1]).astype(bf16)
    normed_ref[...] = normed
    packed_ref[...] = dot(normed, attn_ref[:, :QKV], (1, 0)).astype(bf16)
    low = first_head()
    for pair in range(OUT // PAIR):
        col = pair * PAIR
        query = packed_ref[:, col : col + PAIR]
        key = packed_ref[:, OUT + col : OUT + col + PAIR]
        value = packed_ref[:, 2 * OUT + col : 2 * OUT + col + PAIR]
        none = jnp.zeros_like(query)
        parts = []
        for head in range(2):
            mine = low if head == 0 else ~low
            probs = head_probs(jnp.where(mine, query, none), key).astype(bf16)
            parts.append(dot(probs, value, (1, 0)))
        context_ref[:, col : col + PAIR] = jnp.where(low, parts[0], parts[1]).astype(bf16)
    part_ref[...] = dot(context_ref[...], attn_ref[:, QKV : QKV + OUT], (1, 1)).astype(bf16)
    if len(rest) > 1:
        moe.wait()


VMEM = pl.BlockSpec(memory_space=pltpu.VMEM)
HBM = pl.BlockSpec(memory_space=pltpu.HBM)


def attend(inputs, weights, at, with_experts):
    shape = jax.ShapeDtypeStruct
    moe = (shape((D, MOE), bf16),) if with_experts else ()
    return pl.pallas_call(
        functools.partial(attend_kernel, at),
        in_specs=[VMEM, HBM],
        out_specs=(VMEM,) * (6 + len(moe)),
        out_shape=(
            shape((LEN, D), bf16),
            shape((LEN, D), bf16),
            shape((LEN, QKV), bf16),
            shape((LEN, OUT), bf16),
            shape((8, D), f32),
            shape((D, ATTN), bf16),
        )
        + moe,
        scratch_shapes=[pltpu.SemaphoreType.DMA((2,))],
        compiler_params=pltpu.CompilerParams(vmem_limit_bytes=24 * 2**20),
        cost_estimate=pl.CostEstimate(
            flops=2 * LEN * D * (QKV + OUT), bytes_accessed=6 * 2**20, transcendentals=6 * LEN * LEN
        ),
        name="attend",
    )(inputs, pltpu.with_memory_space_constraint(weights, pltpu.HBM))


def attend_back_kernel(grad_ref, attn_ref, packed_ref, part_ref, grads_ref, heads_ref):
    heads_ref[...] = dot(grad_ref[...], attn_ref[:, QKV : QKV + OUT], (1, 0)).astype(bf16)
    low = first_head()
    for pair in range(OUT // PAIR):
        at = pair * PAIR
        query = packed_ref[:, at : at + PAIR]
        key = packed_ref[:, OUT + at : OUT + at + PAIR]
        value = packed_ref[:, 2 * OUT + at : 2 * OUT + at + PAIR]
        grad = heads_ref[:, at : at + PAIR]
        none = jnp.zeros_like(query)
        found = []
        for head in range(2):
            mine = low if head == 0 else ~low
            probs = head_probs(jnp.where(mine, query, none), key)
            grad_probs = dot(jnp.where(mine, grad, none), value, (1, 1))
            inner = jnp.sum(grad_probs * probs, axis=-1, keepdims=True)
            grad_scores = (probs * (grad_probs - inner)).astype(bf16)
            found.append(
                (
                    dot(grad_scores, key, (1, 0)) * SCALE,
                    dot(grad_scores, query, (0, 0)) * SCALE,
                    dot(probs.astype(bf16), grad, (0, 0)),
                )
            )
        for j in range(3):
            both = jnp.where(low, found[0][j], found[1][j]).astype(bf16)
            grads_ref[:, j * OUT + at : j * OUT + at + PAIR] = both
    part_ref[...] = dot(grads_ref[...], attn_ref[:, :QKV], (1, 1)).astype(bf16)


def attend_back(grad, attn, packed):
    shape = jax.ShapeDtypeStruct
    return pl.pallas_call(
        attend_back_kernel,
        out_shape=(shape((LEN, D), bf16), shape((LEN, QKV), bf16)),
        scratch_shapes=[pltpu.VMEM((LEN, OUT), bf16)],
        compiler_params=pltpu.CompilerParams(vmem_limit_bytes=24 * 2**20),
        cost_estimate=pl.CostEstimate(
            flops=2 * LEN * D * (QKV + OUT), bytes_accessed=6 * 2**20, transcendentals=6 * LEN * LEN
        ),
        name="attend_back",
    )(grad, attn, packed)


TILE = 256


def expert_grads_kernel(at, filled_ref, hidden_ref, slots_ref, active_ref, *rest):
    out_ref, tiles, sems = rest[-3:]
    copies = []
    for i in range(D // TILE):
        rows = slice(i * TILE, (i + 1) * TILE)
        tiles[rows, :FFH] = dot(filled_ref[:, rows], hidden_ref[...], (0, 0)).astype(bf16)
        tiles[rows, FFH:] = dot(slots_ref[:, rows], active_ref[...], (0, 0)).astype(bf16)
        copy = pltpu.make_async_copy(
            tiles.at[pl.ds(i * TILE, TILE)],
            out_ref.at[pl.ds(i * TILE, TILE), pl.ds(at, MOE)],
            sems.at[i],
        )
        copy.start()
        copies.append(copy)
    for copy in copies:
        copy.wait()


def attend_grads_kernel(at, normed_ref, grads_ref, proj_ref, context_ref, small_ref, *rest):
    out_ref, tiles, sems = rest[-3:]
    tiles[:, :QKV] = dot(normed_ref[...], grads_ref[...], (0, 0)).astype(bf16)
    tiles[:, QKV : QKV + OUT] = dot(proj_ref[...], context_ref[...], (0, 0)).astype(bf16)
    rows = jnp.concatenate([small_ref[...], jnp.zeros((120, D), f32)], axis=0)
    tiles[:, QKV + OUT : QKV + OUT + 128] = jnp.transpose(rows).astype(bf16)
    tiles[:, QKV + OUT + 128 :] = jnp.zeros((D, tiles.shape[1] - QKV - OUT - 128), bf16)
    copy = pltpu.make_async_copy(tiles, out_ref.at[:, pl.ds(at, tiles.shape[1])], sems.at[0])
    copy.start()
    copy.wait()


def grads_into(kernel, name, columns, operands, buffer, width, at):
    count = len(operands)
    if buffer is not None:
        operands = operands + [buffer]
    return pl.pallas_call(
        functools.partial(kernel, at),
        in_specs=[VMEM] * count + [HBM] * (len(operands) - count),
        out_specs=HBM,
        out_shape=pltpu.HBM((D, width), bf16),
        scratch_shapes=[
            pltpu.VMEM((D, columns), bf16),
            pltpu.SemaphoreType.DMA((D // TILE,)),
        ],
        input_output_aliases={} if buffer is None else {count: 0},
        compiler_params=pltpu.CompilerParams(vmem_limit_bytes=24 * 2**20),
        cost_estimate=pl.CostEstimate(
            flops=2 * E * PAD * D * columns, bytes_accessed=9 * 2**20, transcendentals=0
        ),
        name=name,
    )(*operands)


def expert_grads(operands, buffer, width, at):
    return grads_into(expert_grads_kernel, "expert_grads", MOE, operands, buffer, width, at)


def attend_grads(operands, buffer, width, at):
    columns = ATTN if buffer is not None else width
    return grads_into(attend_grads_kernel, "attend_grads", columns, operands, buffer, width, at)


def attention(inputs, weights, at, onehot, with_experts):
    part, normed, packed, context, small, attn, *moe = attend(inputs, weights, at, with_experts)
    g_moe, w_router = small[1:2], small[2 : 2 + E].astype(bf16)
    middle = inputs + pair_sum(part)
    scale_mid = rms_scale(middle)
    mixed = (middle * scale_mid * g_moe).astype(bf16)
    logits = matmul(mixed, w_router, (1, 1))
    exponent = jnp.exp(logits - jnp.max(logits, axis=-1, keepdims=True))
    router_probs = exponent / jnp.sum(exponent, axis=-1, keepdims=True)
    gate = jnp.sum(onehot * router_probs, axis=-1, keepdims=True)
    kept = (
        inputs, small, normed, packed, context, middle, scale_mid, mixed, router_probs, gate, attn,
    )
    return (kept, moe[0]) if with_experts else kept


def experts(filled, w_in, w_down):
    hidden = matmul(filled, w_in, (1, 0))
    cdf = 0.5 * (1.0 + lax.erf(hidden * (1.0 / math.sqrt(2.0))))
    activated = (hidden * cdf).astype(bf16)
    slope = cdf + hidden * jnp.exp(-0.5 * hidden * hidden) * (1.0 / math.sqrt(2.0 * math.pi))
    return activated, slope, matmul(activated, w_down, (1, 1)).astype(bf16)


def experts_back(grad_slots, slope, w_in, w_down):
    grad_hidden = (matmul(grad_slots, w_down, (1, 0)) * slope).astype(bf16)
    return grad_hidden, matmul(grad_hidden, w_in, (1, 1)).astype(bf16)


def to_slots(table, rows):
    return matmul(table, rows, (1, 0)).astype(bf16)


def from_slots(table, slots):
    return matmul(table, slots, (0, 0)).astype(bf16)


def mixed_back(grad_out, grad_mixed, combined, onehot, kept):
    inputs, small, normed, packed, context, middle, scale_mid, mixed, router_probs, gate, attn = kept
    grad_gate = jnp.sum(grad_out * combined, axis=-1, keepdims=True)
    grad_logits = router_probs * (onehot - gate) * grad_gate
    grad_w_router = lax.dot_general(
        grad_logits, mixed.astype(f32), (((0,), (0,)), ((), ())), precision=lax.Precision.HIGHEST
    )
    g_moe, w_router = small[1:2], small[2 : 2 + E]
    back_rows = sum(grad_logits[:, e : e + 1] * w_router[e][None, :] for e in range(E))
    grad_norm, grad_g_moe = norm_back(grad_mixed + back_rows, middle, scale_mid, g_moe)
    return grad_out + grad_norm, grad_w_router, grad_g_moe


def attention_back(grad_middle, kept, grad_w_router, grad_g_moe, buffer, width, at):
    inputs, small, normed, packed, context, middle, scale_mid, mixed, router_probs, gate, attn = kept
    proj = grad_middle.astype(bf16)
    part, grads = attend_back(proj, attn, packed)
    grad_normed = pair_sum(part)
    grad_norm, grad_g_attn = norm_back(grad_normed, inputs, rms_scale(inputs), small[:1])
    rows = jnp.concatenate(
        [grad_g_attn[None], grad_g_moe[None], grad_w_router, jnp.zeros((6 - E, D), f32)], axis=0
    )
    buffer = attend_grads([normed, grads, proj, context, rows], buffer, width, at)
    return grad_middle + grad_norm, buffer


def by_layer(p, near, far):
    return jnp.where(p == 0, near, far), jnp.where(p == 0, far, near)


def on_device(tokens, cotangent, routes, g_attn, w_qkv, w_out, g_moe, w_router, w_in, w_down):
    p, c, t = lax.axis_index("pipe"), lax.axis_index("core"), lax.axis_index("tensor")
    chip = p * 2 + t

    def spread(chunk_of):
        got = []
        for k in range(4):
            k1, k0 = k >> 1, k & 1
            got.append(column_send(chunk_of(k), lambda p, c, t: (p ^ k1, t, c ^ k0)))
        layers = []
        for first, second in ((by_layer(p, got[0], got[2])), (by_layer(p, got[1], got[3]))):
            layers.append((first, second))
        return [
            jnp.concatenate(
                [
                    jnp.where(t == 0, layers[0][l], layers[1][l]),
                    jnp.where(t == 0, layers[1][l], layers[0][l]),
                ],
                axis=0,
            )
            for l in range(2)
        ]

    small = jnp.concatenate([g_attn[0][:, None], g_moe[0][:, None], w_router[0]], axis=1)
    small = jnp.pad(small, ((0, 0), (0, SMALL - small.shape[1])))

    def chunk_of(k):
        expert = (p * 2 + c) ^ k
        return jnp.concatenate(
            [
                w_qkv[0].reshape(-1, QKV),
                w_out[0],
                small,
                lax.dynamic_index_in_dim(w_in[0], expert, 0, keepdims=False),
                lax.dynamic_index_in_dim(w_down[0], expert, 0, keepdims=False),
            ],
            axis=1,
        )

    blocks = spread(chunk_of)
    weights = lax.all_gather(
        jnp.concatenate([blocks[0], blocks[1][:, :ATTN]], axis=1), ("x", "y"), axis=0, tiled=True
    )
    late = lax.all_gather(blocks[1][:, ATTN:], ("x", "y"), axis=0, tiled=True)

    def to_owner(rows):
        got = [column_send(rows, lambda p, c, t, j=j: (p, t ^ j, c)) for j in range(2)]
        return jnp.where(c == 0, got[0], got[1]), jnp.where(c == 0, got[1], got[0])

    own_routes = routes[0, :, :, 0].astype(bf16)
    far_routes = lax.ppermute(own_routes, "pipe", [(0, 1), (1, 0)])
    route_pair = jnp.stack(by_layer(p, own_routes, far_routes))
    route_rows = lax.dynamic_index_in_dim(route_pair, p, 1, keepdims=False)
    own_tokens = lax.dynamic_index_in_dim(tokens, p, 0, keepdims=False)
    extra = jnp.pad(route_rows.reshape(1, 2 * HALF), ((0, 15), (0, D - 2 * HALF)))
    low_rows, high_rows = to_owner(jnp.concatenate([own_tokens, extra], axis=0))
    inputs = jnp.concatenate([low_rows[:HALF], high_rows[:HALF]], axis=0).astype(f32)
    tables, onehots = [], []
    earlier = (
        lax.broadcasted_iota(jnp.int32, (LEN, LEN), 0)
        < lax.broadcasted_iota(jnp.int32, (LEN, LEN), 1)
    ).astype(bf16)
    for l in range(2):
        cut = slice(l * HALF, (l + 1) * HALF)
        ids = jnp.concatenate([low_rows[HALF, cut], high_rows[HALF, cut]]).astype(jnp.int32)
        picks = (ids[None, :] == jnp.arange(E, dtype=jnp.int32)[:, None]).astype(f32)
        before = matmul(picks.astype(bf16), earlier, (1, 0))
        rank = jnp.sum(before * picks, axis=0).astype(jnp.int32)
        place = (ids ^ chip) * PAD + rank
        tables.append(
            (place[None, :] == jnp.arange(E * PAD, dtype=jnp.int32)[:, None]).astype(bf16)
        )
        onehots.append(picks.T)

    cot_rows = lax.dynamic_index_in_dim(cotangent, p, 0, keepdims=False)
    grad_out = jnp.concatenate(to_owner(cot_rows), axis=0).astype(f32)

    inputs, grad_out = lax.optimization_barrier((inputs, grad_out))
    in_second, down_second = late[:, :FFH], late[:, FFH:]

    first, moe_weights = attention(inputs, weights, 0, onehots[0], True)
    in_first, down_first = moe_weights[:, :FFH], moe_weights[:, FFH:]
    filled_first = to_experts(to_slots(tables[0], first[7]))
    active_first, slope_first, out_slots = experts(filled_first, in_first, down_first)
    combined_first = pair_sum(from_slots(tables[0], to_experts(out_slots)))
    first_out = (first[5] + first[9] * combined_first).astype(bf16)

    second = attention(
        first_out.astype(f32), weights, ATTN + MOE, onehots[1], False
    )
    filled, grad_slots = to_experts(
        to_slots(tables[1], second[7]),
        to_slots(tables[1], (second[9] * grad_out).astype(bf16)),
    )
    activated, slope, out_slots = experts(filled, in_second, down_second)
    grad_hidden, grad_filled = experts_back(grad_slots, slope, in_second, down_second)
    width = 2 * MOE + ATTN
    found = to_experts(out_slots, grad_filled)
    buffer = expert_grads([filled, grad_hidden, grad_slots, activated], None, width, 0)
    found, buffer = lax.optimization_barrier((found, buffer))
    sums = pair_sum(jnp.concatenate([from_slots(tables[1], rows) for rows in found], axis=1))
    combined, grad_mixed = sums[:, :D], sums[:, D:]
    second_out = (second[5] + second[9] * combined).astype(bf16)

    def to_home(first, second):
        cut = lambda rows: lax.dynamic_slice_in_dim(rows, c * HALF, HALF, 0)
        near, far = by_layer(p, cut(first), cut(second))
        near = column_send(near, lambda p, c, t: (p, t, c))
        far = column_send(far, lambda p, c, t: (1 - p, t, c))
        return jnp.stack(by_layer(p, near, far))

    def reduce_plane(whole):
        return lax.optimization_barrier(
            lax.psum_scatter(whole, ("x", "y"), scatter_dimension=0, tiled=True)
        )

    grad_mid, g_router, gg_moe = mixed_back(grad_out, grad_mixed, combined, onehots[1], second)
    grad_x, buffer = attention_back(
        grad_mid, second, g_router, gg_moe, buffer, width, MOE
    )
    second_grad = grad_x.astype(bf16)
    grad_out = second_grad.astype(f32)
    grad_slots = to_experts(to_slots(tables[0], (first[9] * grad_out).astype(bf16)))
    grad_hidden, grad_filled = experts_back(grad_slots, slope_first, in_first, down_first)
    grad_filled = to_experts(grad_filled)
    buffer = expert_grads(
        [filled_first, grad_hidden, grad_slots, active_first], buffer, width, MOE + ATTN
    )
    reduced = reduce_plane(buffer)
    grad_filled, buffer = lax.optimization_barrier((grad_filled, buffer))
    grad_mixed = pair_sum(from_slots(tables[0], grad_filled))
    grad_mid, g_router, gg_moe = mixed_back(
        grad_out, grad_mixed, combined_first, onehots[0], first
    )
    grad_x, attn_whole = attention_back(
        grad_mid, first, g_router, gg_moe, None, 4 * QUARTER, 0
    )
    quarters = [
        lax.dynamic_slice_in_dim(attn_whole, (chip ^ k) * QUARTER, QUARTER, 1) for k in range(4)
    ]
    quarters = [quarters[0]] + [chip_swap(quarters[k], k) for k in (1, 2, 3)]
    attn_whole = sum(part.astype(f32) for part in quarters).astype(bf16)
    first_out, second_out, grad_x, attn_whole = lax.optimization_barrier(
        (first_out, second_out, grad_x, attn_whole)
    )
    over_x = scatter_axis(scatter_first(attn_whole[:, : QUARTER // 2], "x"), "y", 0)
    over_y = scatter_axis(scatter_first(attn_whole[:, QUARTER // 2 :], "y"), "x", 0)
    attn_first = jnp.concatenate([over_x, over_y], axis=1)
    hidden_states = to_home(first_out, second_out)
    grad_inputs = to_home(grad_x.astype(bf16), second_grad).astype(f32)

    first_all = jnp.concatenate(
        [reduced[:, MOE + ATTN :], attn_first, jnp.zeros((48, ATTN - QUARTER), bf16)], axis=1
    )
    second_all = reduced[:, : MOE + ATTN]
    attn_sum = jnp.zeros((24, ATTN), f32)
    attn_all = jnp.zeros((24, 4 * QUARTER), bf16)
    moe_all = jnp.zeros((E, 24, MOE), bf16)
    for k in range(4):
        k1, k0 = k >> 1, k & 1
        piece = jnp.where((p ^ k1) == 0, first_all, second_all)
        piece = lax.dynamic_slice_in_dim(piece, (t ^ k0) * 24, 24, 0)
        got = column_send(piece, lambda p, c, t: (p ^ k1, t ^ k0, c))
        source = (p * 2 + c) ^ k
        moe_all = lax.dynamic_update_index_in_dim(moe_all, got[:, :MOE], source, 0)
        attn_sum = attn_sum + got[:, MOE:].astype(f32)
        attn_all = lax.dynamic_update_slice_in_dim(
            attn_all, got[:, MOE : MOE + QUARTER], source * QUARTER, 1
        )
    attn_sum = jnp.where(p == 0, attn_all[:, :ATTN].astype(f32), attn_sum)
    small = attn_sum[:, QKV + OUT :]
    return (
        hidden_states[None],
        grad_inputs[None],
        small[:, 0][None],
        attn_sum[:, :QKV].reshape(24, 3, OUT)[None],
        attn_sum[:, QKV : QKV + OUT][None],
        small[:, 1][None],
        small[:, 2 : 2 + E][None],
        moe_all[:, :, :FFH].astype(f32)[None],
        moe_all[:, :, FFH:].astype(f32)[None],
    )


def solution(mesh):
    grid = Mesh(mesh.devices.reshape(2, 4, 4, 2, 2), ("pipe", "x", "y", "core", "tensor"))
    dp = ("x", "y", "core")
    return jax.shard_map(
        on_device,
        mesh=grid,
        in_specs=(
            P(dp, "tensor", None),
            P(dp, "tensor", None),
            P("pipe", dp, "tensor", None),
            P("pipe", dp),
            P("pipe", dp, None, "tensor"),
            P("pipe", dp, "tensor"),
            P("pipe", dp),
            P("pipe", dp, None),
            P("pipe", None, dp, "tensor"),
            P("pipe", None, dp, "tensor"),
        ),
        out_specs=(
            P("pipe", dp, "tensor", None),
            P("pipe", dp, "tensor", None),
            P("pipe", dp),
            P("pipe", dp, None, "tensor"),
            P("pipe", dp, "tensor"),
            P("pipe", dp),
            P("pipe", dp, None),
            P("pipe", None, dp, "tensor"),
            P("pipe", None, dp, "tensor"),
        ),
        check_vma=False,
    )
```

```python
import functools
import math

import jax
import jax.numpy as jnp
from jax import lax
from jax.experimental import pallas as pl
from jax.experimental.pallas import tpu as pltpu
from jax.sharding import Mesh
from jax.sharding import PartitionSpec as P

D = 768
DH = 64
E = 4
LEN = 256
HALF = 128
PAD = 88
QKV = 1152
OUT = 384
SMALL = 256
ATTN = QKV + OUT + SMALL
FFH = 1536
MOE = 2 * FFH
QUARTER = 384

norm_eps = 1e-06
f32 = jnp.float32
bf16 = jnp.bfloat16
COLUMN = ("pipe", "core", "tensor")


def column_pairs(target):
    pairs = []
    for p in range(2):
        for c in range(2):
            for t in range(2):
                p2, c2, t2 = target(p, c, t)
                pairs.append((p * 4 + c * 2 + t, p2 * 4 + c2 * 2 + t2))
    return pairs


def column_send(array, target):
    return lax.ppermute(array, COLUMN, column_pairs(target))


def core_swap(array):
    return lax.ppermute(array, "core", [(0, 1), (1, 0)])


def chip_swap(array, k):
    return lax.ppermute(array, ("pipe", "tensor"), [(i, i ^ k) for i in range(4)])


def axis_swap(array, axis, k):
    return lax.ppermute(array, axis, [(i, i ^ k) for i in range(4)])


def scatter_axis(whole, axis, dim):
    me = lax.axis_index(axis)
    parts = [lax.dynamic_index_in_dim(whole, me ^ k, dim, keepdims=False) for k in range(4)]
    got = [parts[0]] + [axis_swap(parts[k], axis, k) for k in (1, 2, 3)]
    return sum(part.astype(f32) for part in got).astype(bf16)


def scatter_first(whole, axis):
    return scatter_axis(whole.reshape(4, 4, -1, whole.shape[1]), axis, "xy".index(axis))


def rms_scale(values):
    return lax.rsqrt(jnp.mean(values * values, axis=-1, keepdims=True) + norm_eps)


def norm_back(grad_normed, values, scale_rows, gain):
    normal = values * scale_rows
    weighted = grad_normed * gain
    grad_values = scale_rows * (
        weighted - normal * jnp.mean(weighted * normal, axis=-1, keepdims=True)
    )
    return grad_values, jnp.sum(grad_normed * normal, axis=0)


def matmul(left, right, dims):
    return lax.dot_general(left, right, ((dims[:1], dims[1:]), ((), ())), preferred_element_type=f32)


def pair_sum(partial):
    mine = partial.astype(bf16)
    return mine.astype(f32) + core_swap(mine).astype(f32)


def to_experts(*arrays):
    parts = [
        jnp.stack([rows[k * PAD : (k + 1) * PAD] for rows in arrays]) for k in range(4)
    ]
    parts = [parts[0]] + [chip_swap(parts[k], k) for k in (1, 2, 3)]
    found = [
        jnp.concatenate([part[i] for part in parts], axis=0) for i in range(len(arrays))
    ]
    return found if len(arrays) > 1 else found[0]


PAIR = 2 * DH
SCALE = 1.0 / math.sqrt(DH)


def dot(left, right, dims):
    return lax.dot_general(left, right, ((dims[:1], dims[1:]), ((), ())), preferred_element_type=f32)


def first_head():
    return lax.broadcasted_iota(jnp.int32, (LEN, PAIR), 1) < DH


def head_probs(query, key):
    scores = dot(query, key, (1, 1)) * SCALE
    exponent = jnp.exp(scores - jnp.max(scores, axis=-1, keepdims=True))
    return exponent / jnp.sum(exponent, axis=-1, keepdims=True)


def attend_kernel(
    at, x_ref, weights_ref, part_ref, normed_ref, packed_ref, context_ref, small_ref, attn_ref, *rest
):
    sems = rest[-1]
    copy = pltpu.make_async_copy(weights_ref.at[:, pl.ds(at, ATTN)], attn_ref, sems.at[0])
    copy.start()
    if len(rest) > 1:
        moe = pltpu.make_async_copy(weights_ref.at[:, pl.ds(at + ATTN, MOE)], rest[0], sems.at[1])
        moe.start()
    values = x_ref[...]
    scale = lax.rsqrt(jnp.mean(values * values, axis=-1, keepdims=True) + norm_eps)
    copy.wait()
    small = jnp.transpose(attn_ref[:, QKV + OUT : QKV + OUT + 128].astype(f32))[:8]
    small_ref[...] = small
    normed = (values * scale * small[:1]).astype(bf16)
    normed_ref[...] = normed
    packed_ref[...] = dot(normed, attn_ref[:, :QKV], (1, 0)).astype(bf16)
    low = first_head()
    for pair in range(OUT // PAIR):
        col = pair * PAIR
        query = packed_ref[:, col : col + PAIR]
        key = packed_ref[:, OUT + col : OUT + col + PAIR]
        value = packed_ref[:, 2 * OUT + col : 2 * OUT + col + PAIR]
        none = jnp.zeros_like(query)
        parts = []
        for head in range(2):
            mine = low if head == 0 else ~low
            probs = head_probs(jnp.where(mine, query, none), key).astype(bf16)
            parts.append(dot(probs, value, (1, 0)))
        context_ref[:, col : col + PAIR] = jnp.where(low, parts[0], parts[1]).astype(bf16)
    part_ref[...] = dot(context_ref[...], attn_ref[:, QKV : QKV + OUT], (1, 1)).astype(bf16)
    if len(rest) > 1:
        moe.wait()


VMEM = pl.BlockSpec(memory_space=pltpu.VMEM)
HBM = pl.BlockSpec(memory_space=pltpu.HBM)


def attend(inputs, weights, at, with_experts):
    shape = jax.ShapeDtypeStruct
    moe = (shape((D, MOE), bf16),) if with_experts else ()
    return pl.pallas_call(
        functools.partial(attend_kernel, at),
        in_specs=[VMEM, HBM],
        out_specs=(VMEM,) * (6 + len(moe)),
        out_shape=(
            shape((LEN, D), bf16),
            shape((LEN, D), bf16),
            shape((LEN, QKV), bf16),
            shape((LEN, OUT), bf16),
            shape((8, D), f32),
            shape((D, ATTN), bf16),
        )
        + moe,
        scratch_shapes=[pltpu.SemaphoreType.DMA((2,))],
        compiler_params=pltpu.CompilerParams(vmem_limit_bytes=24 * 2**20),
        cost_estimate=pl.CostEstimate(
            flops=2 * LEN * D * (QKV + OUT), bytes_accessed=6 * 2**20, transcendentals=6 * LEN * LEN
        ),
        name="attend",
    )(inputs, pltpu.with_memory_space_constraint(weights, pltpu.HBM))


def attend_back_kernel(grad_ref, attn_ref, packed_ref, part_ref, grads_ref, heads_ref):
    heads_ref[...] = dot(grad_ref[...], attn_ref[:, QKV : QKV + OUT], (1, 0)).astype(bf16)
    low = first_head()
    for pair in range(OUT // PAIR):
        at = pair * PAIR
        query = packed_ref[:, at : at + PAIR]
        key = packed_ref[:, OUT + at : OUT + at + PAIR]
        value = packed_ref[:, 2 * OUT + at : 2 * OUT + at + PAIR]
        grad = heads_ref[:, at : at + PAIR]
        none = jnp.zeros_like(query)
        found = []
        for head in range(2):
            mine = low if head == 0 else ~low
            probs = head_probs(jnp.where(mine, query, none), key)
            grad_probs = dot(jnp.where(mine, grad, none), value, (1, 1))
            inner = jnp.sum(grad_probs * probs, axis=-1, keepdims=True)
            grad_scores = (probs * (grad_probs - inner)).astype(bf16)
            found.append(
                (
                    dot(grad_scores, key, (1, 0)) * SCALE,
                    dot(grad_scores, query, (0, 0)) * SCALE,
                    dot(probs.astype(bf16), grad, (0, 0)),
                )
            )
        for j in range(3):
            both = jnp.where(low, found[0][j], found[1][j]).astype(bf16)
            grads_ref[:, j * OUT + at : j * OUT + at + PAIR] = both
    part_ref[...] = dot(grads_ref[...], attn_ref[:, :QKV], (1, 1)).astype(bf16)


def attend_back(grad, attn, packed):
    shape = jax.ShapeDtypeStruct
    return pl.pallas_call(
        attend_back_kernel,
        out_shape=(shape((LEN, D), bf16), shape((LEN, QKV), bf16)),
        scratch_shapes=[pltpu.VMEM((LEN, OUT), bf16)],
        compiler_params=pltpu.CompilerParams(vmem_limit_bytes=24 * 2**20),
        cost_estimate=pl.CostEstimate(
            flops=2 * LEN * D * (QKV + OUT), bytes_accessed=6 * 2**20, transcendentals=6 * LEN * LEN
        ),
        name="attend_back",
    )(grad, attn, packed)


TILE = 256


def expert_grads_kernel(at, filled_ref, hidden_ref, slots_ref, active_ref, *rest):
    out_ref, tiles, sems = rest[-3:]
    copies = []
    for i in range(D // TILE):
        rows = slice(i * TILE, (i + 1) * TILE)
        tiles[rows, :FFH] = dot(filled_ref[:, rows], hidden_ref[...], (0, 0)).astype(bf16)
        tiles[rows, FFH:] = dot(slots_ref[:, rows], active_ref[...], (0, 0)).astype(bf16)
        copy = pltpu.make_async_copy(
            tiles.at[pl.ds(i * TILE, TILE)],
            out_ref.at[pl.ds(i * TILE, TILE), pl.ds(at, MOE)],
            sems.at[i],
        )
        copy.start()
        copies.append(copy)
    for copy in copies:
        copy.wait()


def attend_grads_kernel(at, normed_ref, grads_ref, proj_ref, context_ref, small_ref, *rest):
    out_ref, tiles, sems = rest[-3:]
    tiles[:, :QKV] = dot(normed_ref[...], grads_ref[...], (0, 0)).astype(bf16)
    tiles[:, QKV : QKV + OUT] = dot(proj_ref[...], context_ref[...], (0, 0)).astype(bf16)
    if tiles.shape[1] > QKV + OUT:
        rows = jnp.concatenate([small_ref[...], jnp.zeros((120, D), f32)], axis=0)
        tiles[:, QKV + OUT : QKV + OUT + 128] = jnp.transpose(rows).astype(bf16)
        tiles[:, QKV + OUT + 128 :] = jnp.zeros((D, tiles.shape[1] - QKV - OUT - 128), bf16)
    copy = pltpu.make_async_copy(tiles, out_ref.at[:, pl.ds(at, tiles.shape[1])], sems.at[0])
    copy.start()
    copy.wait()


def grads_into(kernel, name, columns, operands, buffer, width, at):
    count = len(operands)
    if buffer is not None:
        operands = operands + [buffer]
    return pl.pallas_call(
        functools.partial(kernel, at),
        in_specs=[VMEM] * count + [HBM] * (len(operands) - count),
        out_specs=HBM,
        out_shape=pltpu.HBM((D, width), bf16),
        scratch_shapes=[
            pltpu.VMEM((D, columns), bf16),
            pltpu.SemaphoreType.DMA((D // TILE,)),
        ],
        input_output_aliases={} if buffer is None else {count: 0},
        compiler_params=pltpu.CompilerParams(vmem_limit_bytes=24 * 2**20),
        cost_estimate=pl.CostEstimate(
            flops=2 * E * PAD * D * columns, bytes_accessed=9 * 2**20, transcendentals=0
        ),
        name=name,
    )(*operands)


def expert_grads(operands, buffer, width, at):
    return grads_into(expert_grads_kernel, "expert_grads", MOE, operands, buffer, width, at)


def attend_grads(operands, buffer, width, at):
    columns = ATTN if buffer is not None else width
    return grads_into(attend_grads_kernel, "attend_grads", columns, operands, buffer, width, at)


def attention(inputs, weights, at, onehot, with_experts):
    part, normed, packed, context, small, attn, *moe = attend(inputs, weights, at, with_experts)
    g_moe, w_router = small[1:2], small[2 : 2 + E].astype(bf16)
    middle = inputs + pair_sum(part)
    scale_mid = rms_scale(middle)
    mixed = (middle * scale_mid * g_moe).astype(bf16)
    logits = matmul(mixed, w_router, (1, 1))
    exponent = jnp.exp(logits - jnp.max(logits, axis=-1, keepdims=True))
    router_probs = exponent / jnp.sum(exponent, axis=-1, keepdims=True)
    gate = jnp.sum(onehot * router_probs, axis=-1, keepdims=True)
    kept = (
        inputs, small, normed, packed, context, middle, scale_mid, mixed, router_probs, gate, attn,
    )
    return (kept, moe[0]) if with_experts else kept


def experts(filled, w_in, w_down):
    hidden = matmul(filled, w_in, (1, 0))
    cdf = 0.5 * (1.0 + lax.erf(hidden * (1.0 / math.sqrt(2.0))))
    activated = (hidden * cdf).astype(bf16)
    slope = cdf + hidden * jnp.exp(-0.5 * hidden * hidden) * (1.0 / math.sqrt(2.0 * math.pi))
    return activated, slope, matmul(activated, w_down, (1, 1)).astype(bf16)


def experts_back(grad_slots, slope, w_in, w_down):
    grad_hidden = (matmul(grad_slots, w_down, (1, 0)) * slope).astype(bf16)
    return grad_hidden, matmul(grad_hidden, w_in, (1, 1)).astype(bf16)


def to_slots(table, rows):
    return matmul(table, rows, (1, 0)).astype(bf16)


def from_slots(table, slots):
    return matmul(table, slots, (0, 0)).astype(bf16)


def mixed_back(grad_out, grad_mixed, combined, onehot, kept):
    inputs, small, normed, packed, context, middle, scale_mid, mixed, router_probs, gate, attn = kept
    grad_gate = jnp.sum(grad_out * combined, axis=-1, keepdims=True)
    grad_logits = router_probs * (onehot - gate) * grad_gate
    grad_w_router = lax.dot_general(
        grad_logits, mixed.astype(f32), (((0,), (0,)), ((), ())), precision=lax.Precision.HIGHEST
    )
    g_moe, w_router = small[1:2], small[2 : 2 + E]
    back_rows = sum(grad_logits[:, e : e + 1] * w_router[e][None, :] for e in range(E))
    grad_norm, grad_g_moe = norm_back(grad_mixed + back_rows, middle, scale_mid, g_moe)
    return grad_out + grad_norm, grad_w_router, grad_g_moe


def attention_back(grad_middle, kept, grad_w_router, grad_g_moe, buffer, width, at):
    inputs, small, normed, packed, context, middle, scale_mid, mixed, router_probs, gate, attn = kept
    proj = grad_middle.astype(bf16)
    part, grads = attend_back(proj, attn, packed)
    grad_normed = pair_sum(part)
    grad_norm, grad_g_attn = norm_back(grad_normed, inputs, rms_scale(inputs), small[:1])
    rows = jnp.concatenate(
        [grad_g_attn[None], grad_g_moe[None], grad_w_router, jnp.zeros((6 - E, D), f32)], axis=0
    )
    buffer = attend_grads([normed, grads, proj, context, rows], buffer, width, at)
    return grad_middle + grad_norm, buffer, rows


def by_layer(p, near, far):
    return jnp.where(p == 0, near, far), jnp.where(p == 0, far, near)


def on_device(tokens, cotangent, routes, g_attn, w_qkv, w_out, g_moe, w_router, w_in, w_down):
    p, c, t = lax.axis_index("pipe"), lax.axis_index("core"), lax.axis_index("tensor")
    chip = p * 2 + t

    def spread(chunk_of):
        got = []
        for k in range(4):
            k1, k0 = k >> 1, k & 1
            got.append(column_send(chunk_of(k), lambda p, c, t: (p ^ k1, t, c ^ k0)))
        layers = []
        for first, second in ((by_layer(p, got[0], got[2])), (by_layer(p, got[1], got[3]))):
            layers.append((first, second))
        return [
            jnp.concatenate(
                [
                    jnp.where(t == 0, layers[0][l], layers[1][l]),
                    jnp.where(t == 0, layers[1][l], layers[0][l]),
                ],
                axis=0,
            )
            for l in range(2)
        ]

    small = jnp.concatenate([g_attn[0][:, None], g_moe[0][:, None], w_router[0]], axis=1)
    small = jnp.pad(small, ((0, 0), (0, SMALL - small.shape[1])))

    def chunk_of(k):
        expert = (p * 2 + c) ^ k
        return jnp.concatenate(
            [
                w_qkv[0].reshape(-1, QKV),
                w_out[0],
                small,
                lax.dynamic_index_in_dim(w_in[0], expert, 0, keepdims=False),
                lax.dynamic_index_in_dim(w_down[0], expert, 0, keepdims=False),
            ],
            axis=1,
        )

    blocks = spread(chunk_of)
    weights = lax.all_gather(
        jnp.concatenate([blocks[0], blocks[1][:, :ATTN]], axis=1), ("x", "y"), axis=0, tiled=True
    )
    late = lax.all_gather(blocks[1][:, ATTN:], ("x", "y"), axis=0, tiled=True)

    def to_owner(rows):
        got = [column_send(rows, lambda p, c, t, j=j: (p, t ^ j, c)) for j in range(2)]
        return jnp.where(c == 0, got[0], got[1]), jnp.where(c == 0, got[1], got[0])

    own_routes = routes[0, :, :, 0].astype(bf16)
    far_routes = lax.ppermute(own_routes, "pipe", [(0, 1), (1, 0)])
    route_pair = jnp.stack(by_layer(p, own_routes, far_routes))
    route_rows = lax.dynamic_index_in_dim(route_pair, p, 1, keepdims=False)
    own_tokens = lax.dynamic_index_in_dim(tokens, p, 0, keepdims=False)
    extra = jnp.pad(route_rows.reshape(1, 2 * HALF), ((0, 15), (0, D - 2 * HALF)))
    low_rows, high_rows = to_owner(jnp.concatenate([own_tokens, extra], axis=0))
    inputs = jnp.concatenate([low_rows[:HALF], high_rows[:HALF]], axis=0).astype(f32)
    tables, onehots = [], []
    earlier = (
        lax.broadcasted_iota(jnp.int32, (LEN, LEN), 0)
        < lax.broadcasted_iota(jnp.int32, (LEN, LEN), 1)
    ).astype(bf16)
    for l in range(2):
        cut = slice(l * HALF, (l + 1) * HALF)
        ids = jnp.concatenate([low_rows[HALF, cut], high_rows[HALF, cut]]).astype(jnp.int32)
        picks = (ids[None, :] == jnp.arange(E, dtype=jnp.int32)[:, None]).astype(f32)
        before = matmul(picks.astype(bf16), earlier, (1, 0))
        rank = jnp.sum(before * picks, axis=0).astype(jnp.int32)
        place = (ids ^ chip) * PAD + rank
        tables.append(
            (place[None, :] == jnp.arange(E * PAD, dtype=jnp.int32)[:, None]).astype(bf16)
        )
        onehots.append(picks.T)

    cot_rows = lax.dynamic_index_in_dim(cotangent, p, 0, keepdims=False)
    grad_out = jnp.concatenate(to_owner(cot_rows), axis=0).astype(f32)

    inputs, grad_out = lax.optimization_barrier((inputs, grad_out))
    in_second, down_second = late[:, :FFH], late[:, FFH:]

    first, moe_weights = attention(inputs, weights, 0, onehots[0], True)
    in_first, down_first = moe_weights[:, :FFH], moe_weights[:, FFH:]
    filled_first = to_experts(to_slots(tables[0], first[7]))
    active_first, slope_first, out_slots = experts(filled_first, in_first, down_first)
    combined_first = pair_sum(from_slots(tables[0], to_experts(out_slots)))
    first_out = (first[5] + first[9] * combined_first).astype(bf16)

    second = attention(
        first_out.astype(f32), weights, ATTN + MOE, onehots[1], False
    )
    filled, grad_slots = to_experts(
        to_slots(tables[1], second[7]),
        to_slots(tables[1], (second[9] * grad_out).astype(bf16)),
    )
    activated, slope, out_slots = experts(filled, in_second, down_second)
    grad_hidden, grad_filled = experts_back(grad_slots, slope, in_second, down_second)
    width = 2 * MOE + ATTN
    found = to_experts(out_slots, grad_filled)
    buffer = expert_grads([filled, grad_hidden, grad_slots, activated], None, width, 0)
    found, buffer = lax.optimization_barrier((found, buffer))
    sums = pair_sum(jnp.concatenate([from_slots(tables[1], rows) for rows in found], axis=1))
    combined, grad_mixed = sums[:, :D], sums[:, D:]
    second_out = (second[5] + second[9] * combined).astype(bf16)

    def to_home(first, second):
        cut = lambda rows: lax.dynamic_slice_in_dim(rows, c * HALF, HALF, 0)
        near, far = by_layer(p, cut(first), cut(second))
        near = column_send(near, lambda p, c, t: (p, t, c))
        far = column_send(far, lambda p, c, t: (1 - p, t, c))
        return jnp.stack(by_layer(p, near, far))

    def reduce_plane(whole):
        return lax.optimization_barrier(
            lax.psum_scatter(whole, ("x", "y"), scatter_dimension=0, tiled=True)
        )

    grad_mid, g_router, gg_moe = mixed_back(grad_out, grad_mixed, combined, onehots[1], second)
    grad_x, buffer, _ = attention_back(
        grad_mid, second, g_router, gg_moe, buffer, width, MOE
    )
    second_grad = grad_x.astype(bf16)
    grad_out = second_grad.astype(f32)
    grad_slots = to_experts(to_slots(tables[0], (first[9] * grad_out).astype(bf16)))
    grad_hidden, grad_filled = experts_back(grad_slots, slope_first, in_first, down_first)
    grad_filled = to_experts(grad_filled)
    buffer = expert_grads(
        [filled_first, grad_hidden, grad_slots, active_first], buffer, width, MOE + ATTN
    )
    reduced = reduce_plane(buffer)
    grad_filled, buffer = lax.optimization_barrier((grad_filled, buffer))
    grad_mixed = pair_sum(from_slots(tables[0], grad_filled))
    grad_mid, g_router, gg_moe = mixed_back(
        grad_out, grad_mixed, combined_first, onehots[0], first
    )
    grad_x, attn_whole, small_rows = attention_back(
        grad_mid, first, g_router, gg_moe, None, 4 * QUARTER, 0
    )
    first_out, second_out, grad_x = lax.optimization_barrier((first_out, second_out, grad_x))
    small_rows = small_rows.astype(bf16).reshape(16, QUARTER)
    total = 0.0
    for k in range(4):
        part = lax.dynamic_slice_in_dim(attn_whole, (chip ^ k) * QUARTER, QUARTER, 1)
        part = jnp.concatenate([part, small_rows], axis=0)
        total = total + (part if k == 0 else chip_swap(part, k)).astype(f32)
    small_columns = jnp.pad(total[D:].reshape(8, D).T, ((0, 0), (0, 120)))
    attn_whole = jnp.concatenate([total[:D], small_columns], axis=1).astype(bf16)
    attn_first = scatter_axis(scatter_first(attn_whole, "x"), "y", 0)
    hidden_states = to_home(first_out, second_out)
    grad_inputs = to_home(grad_x.astype(bf16), second_grad).astype(f32)

    spare = jnp.zeros((48, ATTN - attn_first.shape[1]), bf16)
    first_all = jnp.concatenate([reduced[:, MOE + ATTN :], attn_first, spare], axis=1)
    second_all = reduced[:, : MOE + ATTN]
    attn_sum = jnp.zeros((24, ATTN), f32)
    attn_all = jnp.zeros((24, 4 * QUARTER), bf16)
    moe_all = jnp.zeros((E, 24, MOE), bf16)
    for k in range(4):
        k1, k0 = k >> 1, k & 1
        piece = jnp.where((p ^ k1) == 0, first_all, second_all)
        piece = lax.dynamic_slice_in_dim(piece, (t ^ k0) * 24, 24, 0)
        got = column_send(piece, lambda p, c, t: (p ^ k1, t ^ k0, c))
        source = (p * 2 + c) ^ k
        moe_all = lax.dynamic_update_index_in_dim(moe_all, got[:, :MOE], source, 0)
        attn_sum = attn_sum + got[:, MOE:].astype(f32)
        attn_all = lax.dynamic_update_slice_in_dim(
            attn_all, got[:, MOE : MOE + QUARTER], source * QUARTER, 1
        )
        first_small = got[:, MOE + QUARTER : MOE + QUARTER + 128].astype(f32)
    attn_grad = jnp.where(p == 0, attn_all.astype(f32), attn_sum[:, : QKV + OUT])
    small = jnp.where(p == 0, first_small, attn_sum[:, QKV + OUT : QKV + OUT + 128])
    return (
        hidden_states[None],
        grad_inputs[None],
        small[:, 0][None],
        attn_grad[:, :QKV].reshape(24, 3, OUT)[None],
        attn_grad[:, QKV : QKV + OUT][None],
        small[:, 1][None],
        small[:, 2 : 2 + E][None],
        moe_all[:, :, :FFH].astype(f32)[None],
        moe_all[:, :, FFH:].astype(f32)[None],
    )


def solution(mesh):
    grid = Mesh(mesh.devices.reshape(2, 4, 4, 2, 2), ("pipe", "x", "y", "core", "tensor"))
    dp = ("x", "y", "core")
    return jax.shard_map(
        on_device,
        mesh=grid,
        in_specs=(
            P(dp, "tensor", None),
            P(dp, "tensor", None),
            P("pipe", dp, "tensor", None),
            P("pipe", dp),
            P("pipe", dp, None, "tensor"),
            P("pipe", dp, "tensor"),
            P("pipe", dp),
            P("pipe", dp, None),
            P("pipe", None, dp, "tensor"),
            P("pipe", None, dp, "tensor"),
        ),
        out_specs=(
            P("pipe", dp, "tensor", None),
            P("pipe", dp, "tensor", None),
            P("pipe", dp),
            P("pipe", dp, None, "tensor"),
            P("pipe", dp, "tensor"),
            P("pipe", dp),
            P("pipe", dp, None),
            P("pipe", None, dp, "tensor"),
            P("pipe", None, dp, "tensor"),
        ),
        check_vma=False,
    )
```

```python
import functools
import math

import jax
import jax.numpy as jnp
from jax import lax
from jax.experimental import pallas as pl
from jax.experimental.pallas import tpu as pltpu
from jax.sharding import Mesh
from jax.sharding import PartitionSpec as P

D = 768
DH = 64
E = 4
LEN = 256
HALF = 128
PAD = 88
QKV = 1152
OUT = 384
SMALL = 256
ATTN = QKV + OUT + SMALL
SENT = QKV + OUT + 128
FFH = 1536
MOE = 2 * FFH
QUARTER = 384

norm_eps = 1e-06
f32 = jnp.float32
bf16 = jnp.bfloat16
COLUMN = ("pipe", "core", "tensor")


def column_pairs(target):
    pairs = []
    for p in range(2):
        for c in range(2):
            for t in range(2):
                p2, c2, t2 = target(p, c, t)
                pairs.append((p * 4 + c * 2 + t, p2 * 4 + c2 * 2 + t2))
    return pairs


def column_send(array, target):
    return lax.ppermute(array, COLUMN, column_pairs(target))


def core_swap(array):
    return lax.ppermute(array, "core", [(0, 1), (1, 0)])


def chip_swap(array, k):
    return lax.ppermute(array, ("pipe", "tensor"), [(i, i ^ k) for i in range(4)])


def axis_swap(array, axis, k):
    return lax.ppermute(array, axis, [(i, i ^ k) for i in range(4)])


def scatter_axis(whole, axis, dim):
    me = lax.axis_index(axis)
    parts = [lax.dynamic_index_in_dim(whole, me ^ k, dim, keepdims=False) for k in range(4)]
    got = [parts[0]] + [axis_swap(parts[k], axis, k) for k in (1, 2, 3)]
    return sum(part.astype(f32) for part in got).astype(bf16)


def scatter_first(whole, axis):
    return scatter_axis(whole.reshape(4, 4, -1, whole.shape[1]), axis, "xy".index(axis))


def rms_scale(values):
    return lax.rsqrt(jnp.mean(values * values, axis=-1, keepdims=True) + norm_eps)


def norm_back(grad_normed, values, scale_rows, gain):
    normal = values * scale_rows
    weighted = grad_normed * gain
    grad_values = scale_rows * (
        weighted - normal * jnp.mean(weighted * normal, axis=-1, keepdims=True)
    )
    return grad_values, jnp.sum(grad_normed * normal, axis=0)


def matmul(left, right, dims):
    return lax.dot_general(left, right, ((dims[:1], dims[1:]), ((), ())), preferred_element_type=f32)


def pair_sum(partial):
    mine = partial.astype(bf16)
    return mine.astype(f32) + core_swap(mine).astype(f32)


def to_experts(*arrays):
    parts = [
        jnp.stack([rows[k * PAD : (k + 1) * PAD] for rows in arrays]) for k in range(4)
    ]
    parts = [parts[0]] + [chip_swap(parts[k], k) for k in (1, 2, 3)]
    found = [
        jnp.concatenate([part[i] for part in parts], axis=0) for i in range(len(arrays))
    ]
    return found if len(arrays) > 1 else found[0]


PAIR = 2 * DH
SCALE = 1.0 / math.sqrt(DH)


def dot(left, right, dims):
    return lax.dot_general(left, right, ((dims[:1], dims[1:]), ((), ())), preferred_element_type=f32)


def first_head():
    return lax.broadcasted_iota(jnp.int32, (LEN, PAIR), 1) < DH


def head_probs(query, key):
    scores = dot(query, key, (1, 1)) * SCALE
    exponent = jnp.exp(scores - jnp.max(scores, axis=-1, keepdims=True))
    return exponent / jnp.sum(exponent, axis=-1, keepdims=True)


def attend_kernel(
    at, x_ref, weights_ref, part_ref, normed_ref, packed_ref, context_ref, small_ref, *rest
):
    sems = rest[-1]
    attn_ref = rest[-2]
    copy = pltpu.make_async_copy(weights_ref.at[:, pl.ds(at, SENT)], attn_ref, sems.at[0])
    copy.start()
    if len(rest) > 2:
        moe = pltpu.make_async_copy(weights_ref.at[:, pl.ds(at + SENT, MOE)], rest[0], sems.at[1])
        moe.start()
    values = x_ref[...]
    scale = lax.rsqrt(jnp.mean(values * values, axis=-1, keepdims=True) + norm_eps)
    copy.wait()
    small = jnp.transpose(attn_ref[:, QKV + OUT : QKV + OUT + 128].astype(f32))[:8]
    small_ref[...] = small
    normed = (values * scale * small[:1]).astype(bf16)
    normed_ref[...] = normed
    packed_ref[...] = dot(normed, attn_ref[:, :QKV], (1, 0)).astype(bf16)
    low = first_head()
    for pair in range(OUT // PAIR):
        col = pair * PAIR
        query = packed_ref[:, col : col + PAIR]
        key = packed_ref[:, OUT + col : OUT + col + PAIR]
        value = packed_ref[:, 2 * OUT + col : 2 * OUT + col + PAIR]
        none = jnp.zeros_like(query)
        parts = []
        for head in range(2):
            mine = low if head == 0 else ~low
            probs = head_probs(jnp.where(mine, query, none), key).astype(bf16)
            parts.append(dot(probs, value, (1, 0)))
        context_ref[:, col : col + PAIR] = jnp.where(low, parts[0], parts[1]).astype(bf16)
    part_ref[...] = dot(context_ref[...], attn_ref[:, QKV : QKV + OUT], (1, 1)).astype(bf16)
    if len(rest) > 2:
        moe.wait()


VMEM = pl.BlockSpec(memory_space=pltpu.VMEM)
HBM = pl.BlockSpec(memory_space=pltpu.HBM)


def attend(inputs, weights, at, with_experts):
    shape = jax.ShapeDtypeStruct
    return pl.pallas_call(
        functools.partial(attend_kernel, at),
        in_specs=[VMEM, HBM],
        out_specs=(VMEM,) * 6,
        out_shape=(
            shape((LEN, D), bf16),
            shape((LEN, D), bf16),
            shape((LEN, QKV), bf16),
            shape((LEN, OUT), bf16),
            shape((8, D), f32),
            shape((D, MOE if with_experts else SENT), bf16),
        ),
        scratch_shapes=([pltpu.VMEM((D, SENT), bf16)] if with_experts else [])
        + [pltpu.SemaphoreType.DMA((2,))],
        compiler_params=pltpu.CompilerParams(vmem_limit_bytes=24 * 2**20),
        cost_estimate=pl.CostEstimate(
            flops=2 * LEN * D * (QKV + OUT), bytes_accessed=6 * 2**20, transcendentals=6 * LEN * LEN
        ),
        name="attend",
    )(inputs, pltpu.with_memory_space_constraint(weights, pltpu.HBM))


def attend_back_kernel(
    fetched, grad_ref, weights_ref, packed_ref, part_ref, grads_ref, heads_ref, *rest
):
    attn_ref = weights_ref
    if fetched:
        attn_ref, sem = rest
        copy = pltpu.make_async_copy(weights_ref.at[:, pl.ds(0, SENT)], attn_ref, sem)
        copy.start()
        copy.wait()
    heads_ref[...] = dot(grad_ref[...], attn_ref[:, QKV : QKV + OUT], (1, 0)).astype(bf16)
    low = first_head()
    for pair in range(OUT // PAIR):
        at = pair * PAIR
        query = packed_ref[:, at : at + PAIR]
        key = packed_ref[:, OUT + at : OUT + at + PAIR]
        value = packed_ref[:, 2 * OUT + at : 2 * OUT + at + PAIR]
        grad = heads_ref[:, at : at + PAIR]
        none = jnp.zeros_like(query)
        found = []
        for head in range(2):
            mine = low if head == 0 else ~low
            probs = head_probs(jnp.where(mine, query, none), key)
            grad_probs = dot(jnp.where(mine, grad, none), value, (1, 1))
            inner = jnp.sum(grad_probs * probs, axis=-1, keepdims=True)
            grad_scores = (probs * (grad_probs - inner)).astype(bf16)
            found.append(
                (
                    dot(grad_scores, key, (1, 0)) * SCALE,
                    dot(grad_scores, query, (0, 0)) * SCALE,
                    dot(probs.astype(bf16), grad, (0, 0)),
                )
            )
        for j in range(3):
            both = jnp.where(low, found[0][j], found[1][j]).astype(bf16)
            grads_ref[:, j * OUT + at : j * OUT + at + PAIR] = both
    part_ref[...] = dot(grads_ref[...], attn_ref[:, :QKV], (1, 1)).astype(bf16)


def attend_back(grad, attn, packed, fetched):
    shape = jax.ShapeDtypeStruct
    scratch = [pltpu.VMEM((LEN, OUT), bf16)]
    if fetched:
        scratch += [pltpu.VMEM((D, SENT), bf16), pltpu.SemaphoreType.DMA]
        attn = pltpu.with_memory_space_constraint(attn, pltpu.HBM)
    return pl.pallas_call(
        functools.partial(attend_back_kernel, fetched),
        in_specs=[VMEM, HBM if fetched else VMEM, VMEM],
        out_specs=(VMEM, VMEM),
        out_shape=(shape((LEN, D), bf16), shape((LEN, QKV), bf16)),
        scratch_shapes=scratch,
        compiler_params=pltpu.CompilerParams(vmem_limit_bytes=24 * 2**20),
        cost_estimate=pl.CostEstimate(
            flops=2 * LEN * D * (QKV + OUT), bytes_accessed=6 * 2**20, transcendentals=6 * LEN * LEN
        ),
        name="attend_back",
    )(grad, attn, packed)


TILE = 256


def expert_grads_kernel(at, filled_ref, hidden_ref, slots_ref, active_ref, *rest):
    out_ref, tiles, sems = rest[-3:]
    copies = []
    for i in range(D // TILE):
        rows = slice(i * TILE, (i + 1) * TILE)
        tiles[rows, :FFH] = dot(filled_ref[:, rows], hidden_ref[...], (0, 0)).astype(bf16)
        tiles[rows, FFH:] = dot(slots_ref[:, rows], active_ref[...], (0, 0)).astype(bf16)
        copy = pltpu.make_async_copy(
            tiles.at[pl.ds(i * TILE, TILE)],
            out_ref.at[pl.ds(i * TILE, TILE), pl.ds(at, MOE)],
            sems.at[i],
        )
        copy.start()
        copies.append(copy)
    for copy in copies:
        copy.wait()


def attend_grads_kernel(at, normed_ref, grads_ref, proj_ref, context_ref, small_ref, *rest):
    out_ref, tiles, sems = rest[-3:]
    tiles[:, :QKV] = dot(normed_ref[...], grads_ref[...], (0, 0)).astype(bf16)
    tiles[:, QKV : QKV + OUT] = dot(proj_ref[...], context_ref[...], (0, 0)).astype(bf16)
    rows = jnp.concatenate([small_ref[...], jnp.zeros((120, D), f32)], axis=0)
    tiles[:, QKV + OUT : QKV + OUT + 128] = jnp.transpose(rows).astype(bf16)
    tiles[:, QKV + OUT + 128 :] = jnp.zeros((D, SMALL - 128), bf16)
    copy = pltpu.make_async_copy(tiles, out_ref.at[:, pl.ds(at, tiles.shape[1])], sems.at[0])
    copy.start()
    copy.wait()


def grads_into(kernel, name, columns, operands, buffer, width, at):
    count = len(operands)
    if buffer is not None:
        operands = operands + [buffer]
    return pl.pallas_call(
        functools.partial(kernel, at),
        in_specs=[VMEM] * count + [HBM] * (len(operands) - count),
        out_specs=HBM,
        out_shape=pltpu.HBM((D, width), bf16),
        scratch_shapes=[
            pltpu.VMEM((D, columns), bf16),
            pltpu.SemaphoreType.DMA((D // TILE,)),
        ],
        input_output_aliases={} if buffer is None else {count: 0},
        compiler_params=pltpu.CompilerParams(vmem_limit_bytes=24 * 2**20),
        cost_estimate=pl.CostEstimate(
            flops=2 * E * PAD * D * columns, bytes_accessed=9 * 2**20, transcendentals=0
        ),
        name=name,
    )(*operands)


def expert_grads(operands, buffer, width, at):
    return grads_into(expert_grads_kernel, "expert_grads", MOE, operands, buffer, width, at)


def attend_grads(operands, buffer, width, at):
    return grads_into(attend_grads_kernel, "attend_grads", ATTN, operands, buffer, width, at)


def quarter_grads_kernel(normed_ref, grads_ref, proj_ref, context_ref, small_ref, out_ref):
    found = dot(normed_ref[...], grads_ref[...], (0, 0)).astype(bf16)
    for j in range(3):
        out_ref[j, :D] = found[:, j * QUARTER : (j + 1) * QUARTER]
    out_ref[3, :D] = dot(proj_ref[...], context_ref[...], (0, 0)).astype(bf16)
    for j in range(4):
        out_ref[j, D:] = small_ref[...]


def quarter_grads(normed, grads, proj, context, small):
    return pl.pallas_call(
        quarter_grads_kernel,
        in_specs=[VMEM] * 5,
        out_specs=VMEM,
        out_shape=jax.ShapeDtypeStruct((4, D + 16, QUARTER), bf16),
        compiler_params=pltpu.CompilerParams(vmem_limit_bytes=24 * 2**20),
        cost_estimate=pl.CostEstimate(
            flops=2 * LEN * D * (QKV + OUT), bytes_accessed=5 * 2**20, transcendentals=0
        ),
        name="quarter_grads",
    )(normed, grads, proj, context, small)


def attention(inputs, weights, at, onehot, with_experts):
    part, normed, packed, context, small, last = attend(inputs, weights, at, with_experts)
    g_moe, w_router = small[1:2], small[2 : 2 + E].astype(bf16)
    middle = inputs + pair_sum(part)
    scale_mid = rms_scale(middle)
    mixed = (middle * scale_mid * g_moe).astype(bf16)
    logits = matmul(mixed, w_router, (1, 1))
    exponent = jnp.exp(logits - jnp.max(logits, axis=-1, keepdims=True))
    router_probs = exponent / jnp.sum(exponent, axis=-1, keepdims=True)
    gate = jnp.sum(onehot * router_probs, axis=-1, keepdims=True)
    attn = None if with_experts else last
    kept = (
        inputs, small, normed, packed, context, middle, scale_mid, mixed, router_probs, gate, attn,
    )
    return (kept, last) if with_experts else kept


def experts(filled, w_in, w_down):
    hidden = matmul(filled, w_in, (1, 0))
    cdf = 0.5 * (1.0 + lax.erf(hidden * (1.0 / math.sqrt(2.0))))
    activated = (hidden * cdf).astype(bf16)
    slope = cdf + hidden * jnp.exp(-0.5 * hidden * hidden) * (1.0 / math.sqrt(2.0 * math.pi))
    return activated, slope, matmul(activated, w_down, (1, 1)).astype(bf16)


def experts_back(grad_slots, slope, w_in, w_down):
    grad_hidden = (matmul(grad_slots, w_down, (1, 0)) * slope).astype(bf16)
    return grad_hidden, matmul(grad_hidden, w_in, (1, 1)).astype(bf16)


def to_slots(table, rows):
    return matmul(table, rows, (1, 0)).astype(bf16)


def from_slots(table, slots):
    return matmul(table, slots, (0, 0)).astype(bf16)


def mixed_back(grad_out, grad_mixed, combined, onehot, kept):
    inputs, small, normed, packed, context, middle, scale_mid, mixed, router_probs, gate, attn = kept
    grad_gate = jnp.sum(grad_out * combined, axis=-1, keepdims=True)
    grad_logits = router_probs * (onehot - gate) * grad_gate
    grad_w_router = lax.dot_general(
        grad_logits, mixed.astype(f32), (((0,), (0,)), ((), ())), precision=lax.Precision.HIGHEST
    )
    g_moe, w_router = small[1:2], small[2 : 2 + E]
    back_rows = sum(grad_logits[:, e : e + 1] * w_router[e][None, :] for e in range(E))
    grad_norm, grad_g_moe = norm_back(grad_mixed + back_rows, middle, scale_mid, g_moe)
    return grad_out + grad_norm, grad_w_router, grad_g_moe


def attention_back(grad_middle, kept, attn, grad_w_router, grad_g_moe):
    inputs, small, normed, packed, context = kept[:5]
    proj = grad_middle.astype(bf16)
    part, grads = attend_back(proj, kept[-1] if attn is None else attn, packed, attn is not None)
    grad_normed = pair_sum(part)
    grad_norm, grad_g_attn = norm_back(grad_normed, inputs, rms_scale(inputs), small[:1])
    rows = jnp.concatenate(
        [grad_g_attn[None], grad_g_moe[None], grad_w_router, jnp.zeros((6 - E, D), f32)], axis=0
    )
    return grad_middle + grad_norm, [normed, grads, proj, context], rows


def by_layer(p, near, far):
    return jnp.where(p == 0, near, far), jnp.where(p == 0, far, near)


def on_device(tokens, cotangent, routes, g_attn, w_qkv, w_out, g_moe, w_router, w_in, w_down):
    p, c, t = lax.axis_index("pipe"), lax.axis_index("core"), lax.axis_index("tensor")
    chip = p * 2 + t

    def spread(chunk_of):
        got = []
        for k in range(4):
            k1, k0 = k >> 1, k & 1
            got.append(column_send(chunk_of(k), lambda p, c, t: (p ^ k1, t, c ^ k0)))
        layers = []
        for first, second in ((by_layer(p, got[0], got[2])), (by_layer(p, got[1], got[3]))):
            layers.append((first, second))
        return [
            jnp.concatenate(
                [
                    jnp.where(t == 0, layers[0][l], layers[1][l]),
                    jnp.where(t == 0, layers[1][l], layers[0][l]),
                ],
                axis=0,
            )
            for l in range(2)
        ]

    small = jnp.concatenate([g_attn[0][:, None], g_moe[0][:, None], w_router[0]], axis=1)
    small = jnp.pad(small, ((0, 0), (0, 128 - small.shape[1])))

    def chunk_of(k):
        expert = (p * 2 + c) ^ k
        return jnp.concatenate(
            [
                w_qkv[0].reshape(-1, QKV),
                w_out[0],
                small,
                lax.dynamic_index_in_dim(w_in[0], expert, 0, keepdims=False),
                lax.dynamic_index_in_dim(w_down[0], expert, 0, keepdims=False),
            ],
            axis=1,
        )

    blocks = spread(chunk_of)
    weights = lax.all_gather(
        jnp.concatenate([blocks[0], blocks[1][:, :SENT]], axis=1), ("x", "y"), axis=0, tiled=True
    )
    late = lax.all_gather(blocks[1][:, SENT:], ("x", "y"), axis=0, tiled=True)

    def to_owner(rows):
        got = [column_send(rows, lambda p, c, t, j=j: (p, t ^ j, c)) for j in range(2)]
        return jnp.where(c == 0, got[0], got[1]), jnp.where(c == 0, got[1], got[0])

    own_routes = routes[0, :, :, 0].astype(bf16)
    far_routes = lax.ppermute(own_routes, "pipe", [(0, 1), (1, 0)])
    route_pair = jnp.stack(by_layer(p, own_routes, far_routes))
    route_rows = lax.dynamic_index_in_dim(route_pair, p, 1, keepdims=False)
    own_tokens = lax.dynamic_index_in_dim(tokens, p, 0, keepdims=False)
    extra = jnp.pad(route_rows.reshape(1, 2 * HALF), ((0, 15), (0, D - 2 * HALF)))
    low_rows, high_rows = to_owner(jnp.concatenate([own_tokens, extra], axis=0))
    inputs = jnp.concatenate([low_rows[:HALF], high_rows[:HALF]], axis=0).astype(f32)
    tables, onehots = [], []
    earlier = (
        lax.broadcasted_iota(jnp.int32, (LEN, LEN), 0)
        < lax.broadcasted_iota(jnp.int32, (LEN, LEN), 1)
    ).astype(bf16)
    for l in range(2):
        cut = slice(l * HALF, (l + 1) * HALF)
        ids = jnp.concatenate([low_rows[HALF, cut], high_rows[HALF, cut]]).astype(jnp.int32)
        picks = (ids[None, :] == jnp.arange(E, dtype=jnp.int32)[:, None]).astype(f32)
        before = matmul(picks.astype(bf16), earlier, (1, 0))
        rank = jnp.sum(before * picks, axis=0).astype(jnp.int32)
        place = (ids ^ chip) * PAD + rank
        tables.append(
            (place[None, :] == jnp.arange(E * PAD, dtype=jnp.int32)[:, None]).astype(bf16)
        )
        onehots.append(picks.T)

    cot_rows = lax.dynamic_index_in_dim(cotangent, p, 0, keepdims=False)
    grad_out = jnp.concatenate(to_owner(cot_rows), axis=0).astype(f32)

    inputs, grad_out = lax.optimization_barrier((inputs, grad_out))
    in_second, down_second = late[:, :FFH], late[:, FFH:]

    first, moe_weights = attention(inputs, weights, 0, onehots[0], True)
    in_first, down_first = moe_weights[:, :FFH], moe_weights[:, FFH:]
    filled_first = to_experts(to_slots(tables[0], first[7]))
    active_first, slope_first, out_slots = experts(filled_first, in_first, down_first)
    combined_first = pair_sum(from_slots(tables[0], to_experts(out_slots)))
    first_out = (first[5] + first[9] * combined_first).astype(bf16)

    second = attention(
        first_out.astype(f32), weights, SENT + MOE, onehots[1], False
    )
    filled, grad_slots = to_experts(
        to_slots(tables[1], second[7]),
        to_slots(tables[1], (second[9] * grad_out).astype(bf16)),
    )
    activated, slope, out_slots = experts(filled, in_second, down_second)
    grad_hidden, grad_filled = experts_back(grad_slots, slope, in_second, down_second)
    width = 2 * MOE + ATTN
    found = to_experts(out_slots, grad_filled)
    buffer = expert_grads([filled, grad_hidden, grad_slots, activated], None, width, 0)
    found, buffer = lax.optimization_barrier((found, buffer))
    sums = pair_sum(jnp.concatenate([from_slots(tables[1], rows) for rows in found], axis=1))
    combined, grad_mixed = sums[:, :D], sums[:, D:]
    second_out = (second[5] + second[9] * combined).astype(bf16)

    def to_home(first, second):
        cut = lambda rows: lax.dynamic_slice_in_dim(rows, c * HALF, HALF, 0)
        near, far = by_layer(p, cut(first), cut(second))
        near = column_send(near, lambda p, c, t: (p, t, c))
        far = column_send(far, lambda p, c, t: (1 - p, t, c))
        return jnp.stack(by_layer(p, near, far))

    def reduce_plane(whole):
        return lax.optimization_barrier(
            lax.psum_scatter(whole, ("x", "y"), scatter_dimension=0, tiled=True)
        )

    grad_mid, g_router, gg_moe = mixed_back(grad_out, grad_mixed, combined, onehots[1], second)
    grad_x, operands, rows = attention_back(grad_mid, second, None, g_router, gg_moe)
    buffer = attend_grads(operands + [rows], buffer, width, MOE)
    second_grad = grad_x.astype(bf16)
    grad_out = second_grad.astype(f32)
    grad_slots = to_experts(to_slots(tables[0], (first[9] * grad_out).astype(bf16)))
    grad_hidden, grad_filled = experts_back(grad_slots, slope_first, in_first, down_first)
    grad_filled = to_experts(grad_filled)
    buffer = expert_grads(
        [filled_first, grad_hidden, grad_slots, active_first], buffer, width, MOE + ATTN
    )
    reduced = reduce_plane(buffer)
    grad_filled, buffer = lax.optimization_barrier((grad_filled, buffer))
    grad_mixed = pair_sum(from_slots(tables[0], grad_filled))
    grad_mid, g_router, gg_moe = mixed_back(
        grad_out, grad_mixed, combined_first, onehots[0], first
    )
    grad_x, operands, rows = attention_back(grad_mid, first, weights, g_router, gg_moe)
    quarters = quarter_grads(*operands, rows.astype(bf16).reshape(16, QUARTER))
    first_out, second_out, grad_x = lax.optimization_barrier((first_out, second_out, grad_x))
    total = 0.0
    for k in range(4):
        part = lax.dynamic_index_in_dim(quarters, chip ^ k, 0, keepdims=False)
        total = total + (part if k == 0 else chip_swap(part, k)).astype(f32)
    small_columns = jnp.pad(total[D:].reshape(8, D).T, ((0, 0), (0, 120)))
    attn_whole = jnp.concatenate([total[:D], small_columns], axis=1).astype(bf16)
    attn_first = scatter_axis(scatter_first(attn_whole, "x"), "y", 0)
    hidden_states = to_home(first_out, second_out)
    grad_inputs = to_home(grad_x.astype(bf16), second_grad).astype(f32)

    widened = jnp.pad(attn_first, ((0, 0), (0, ATTN - attn_first.shape[1])))
    attn_sum = jnp.zeros((24, ATTN), f32)
    attn_all = jnp.zeros((24, 4 * QUARTER), bf16)
    moe_all = jnp.zeros((E, 24, MOE), bf16)
    for k in range(4):
        k1, k0 = k >> 1, k & 1
        to_first = (p ^ k1) == 0
        piece = jnp.concatenate(
            [
                jnp.where(to_first, reduced[:, MOE + ATTN :], reduced[:, :MOE]),
                jnp.where(to_first, widened, reduced[:, MOE : MOE + ATTN]),
            ],
            axis=1,
        )
        piece = jnp.where(t == k0, piece[:24], piece[24:])
        got = column_send(piece, lambda p, c, t: (p ^ k1, t ^ k0, c))
        source = (p * 2 + c) ^ k
        moe_all = lax.dynamic_update_index_in_dim(moe_all, got[:, :MOE], source, 0)
        attn_sum = attn_sum + got[:, MOE:].astype(f32)
        attn_all = lax.dynamic_update_slice_in_dim(
            attn_all, got[:, MOE : MOE + QUARTER], source * QUARTER, 1
        )
        first_small = got[:, MOE + QUARTER : MOE + QUARTER + 128].astype(f32)
    attn_grad = jnp.where(p == 0, attn_all.astype(f32), attn_sum[:, : QKV + OUT])
    small = jnp.where(p == 0, first_small, attn_sum[:, QKV + OUT : QKV + OUT + 128])
    return (
        hidden_states[None],
        grad_inputs[None],
        small[:, 0][None],
        attn_grad[:, :QKV].reshape(24, 3, OUT)[None],
        attn_grad[:, QKV : QKV + OUT][None],
        small[:, 1][None],
        small[:, 2 : 2 + E][None],
        moe_all[:, :, :FFH].astype(f32)[None],
        moe_all[:, :, FFH:].astype(f32)[None],
    )


def solution(mesh):
    grid = Mesh(mesh.devices.reshape(2, 4, 4, 2, 2), ("pipe", "x", "y", "core", "tensor"))
    dp = ("x", "y", "core")
    return jax.shard_map(
        on_device,
        mesh=grid,
        in_specs=(
            P(dp, "tensor", None),
            P(dp, "tensor", None),
            P("pipe", dp, "tensor", None),
            P("pipe", dp),
            P("pipe", dp, None, "tensor"),
            P("pipe", dp, "tensor"),
            P("pipe", dp),
            P("pipe", dp, None),
            P("pipe", None, dp, "tensor"),
            P("pipe", None, dp, "tensor"),
        ),
        out_specs=(
            P("pipe", dp, "tensor", None),
            P("pipe", dp, "tensor", None),
            P("pipe", dp),
            P("pipe", dp, None, "tensor"),
            P("pipe", dp, "tensor"),
            P("pipe", dp),
            P("pipe", dp, None),
            P("pipe", None, dp, "tensor"),
            P("pipe", None, dp, "tensor"),
        ),
        check_vma=False,
    )
```

```python
import functools
import math

import jax
import jax.numpy as jnp
from jax import lax
from jax.experimental import pallas as pl
from jax.experimental.pallas import tpu as pltpu
from jax.sharding import Mesh
from jax.sharding import PartitionSpec as P

D = 768
DH = 64
E = 4
LEN = 256
HALF = 128
PAD = 88
QKV = 1152
OUT = 384
SMALL = 256
ATTN = QKV + OUT + SMALL
SENT = QKV + OUT + 128
FFH = 1536
MOE = 2 * FFH
QUARTER = 384

norm_eps = 1e-06
f32 = jnp.float32
bf16 = jnp.bfloat16
COLUMN = ("pipe", "core", "tensor")


def column_pairs(target):
    pairs = []
    for p in range(2):
        for c in range(2):
            for t in range(2):
                p2, c2, t2 = target(p, c, t)
                pairs.append((p * 4 + c * 2 + t, p2 * 4 + c2 * 2 + t2))
    return pairs


def column_send(array, target):
    return lax.ppermute(array, COLUMN, column_pairs(target))


def core_swap(array):
    return lax.ppermute(array, "core", [(0, 1), (1, 0)])


def chip_swap(array, k):
    return lax.ppermute(array, ("pipe", "tensor"), [(i, i ^ k) for i in range(4)])


def axis_swap(array, axis, k):
    return lax.ppermute(array, axis, [(i, i ^ k) for i in range(4)])


def scatter_axis(whole, axis, dim):
    me = lax.axis_index(axis)
    parts = [lax.dynamic_index_in_dim(whole, me ^ k, dim, keepdims=False) for k in range(4)]
    got = [parts[0]] + [axis_swap(parts[k], axis, k) for k in (1, 2, 3)]
    return sum(part.astype(f32) for part in got).astype(bf16)


def scatter_first(whole, axis):
    return scatter_axis(whole.reshape(4, 4, -1, whole.shape[1]), axis, "xy".index(axis))


def rms_scale(values):
    return lax.rsqrt(jnp.mean(values * values, axis=-1, keepdims=True) + norm_eps)


def norm_back(grad_normed, values, scale_rows, gain):
    normal = values * scale_rows
    weighted = grad_normed * gain
    grad_values = scale_rows * (
        weighted - normal * jnp.mean(weighted * normal, axis=-1, keepdims=True)
    )
    return grad_values, jnp.sum(grad_normed * normal, axis=0)


def matmul(left, right, dims):
    return lax.dot_general(left, right, ((dims[:1], dims[1:]), ((), ())), preferred_element_type=f32)


def pair_sum(partial):
    mine = partial.astype(bf16)
    return mine.astype(f32) + core_swap(mine).astype(f32)


def to_experts(*arrays):
    parts = [
        jnp.stack([rows[k * PAD : (k + 1) * PAD] for rows in arrays]) for k in range(4)
    ]
    parts = [parts[0]] + [chip_swap(parts[j], 4 - j) for j in (1, 2, 3)]
    found = [
        jnp.concatenate([part[i] for part in parts], axis=0) for i in range(len(arrays))
    ]
    return found if len(arrays) > 1 else found[0]


PAIR = 2 * DH
SCALE = 1.0 / math.sqrt(DH)


def dot(left, right, dims):
    return lax.dot_general(left, right, ((dims[:1], dims[1:]), ((), ())), preferred_element_type=f32)


def first_head():
    return lax.broadcasted_iota(jnp.int32, (LEN, PAIR), 1) < DH


def head_probs(query, key):
    scores = dot(query, key, (1, 1)) * SCALE
    exponent = jnp.exp(scores - jnp.max(scores, axis=-1, keepdims=True))
    return exponent / jnp.sum(exponent, axis=-1, keepdims=True)


def attend_kernel(
    at, x_ref, weights_ref, part_ref, normed_ref, packed_ref, context_ref, small_ref, *rest
):
    sems = rest[-1]
    attn_ref = rest[-2]
    copy = pltpu.make_async_copy(weights_ref.at[:, pl.ds(at, SENT)], attn_ref, sems.at[0])
    copy.start()
    if len(rest) > 2:
        moe = pltpu.make_async_copy(weights_ref.at[:, pl.ds(at + SENT, MOE)], rest[0], sems.at[1])
        moe.start()
    values = x_ref[...]
    scale = lax.rsqrt(jnp.mean(values * values, axis=-1, keepdims=True) + norm_eps)
    copy.wait()
    small = jnp.transpose(attn_ref[:, QKV + OUT : QKV + OUT + 128].astype(f32))[:8]
    small_ref[...] = small
    normed = (values * scale * small[:1]).astype(bf16)
    normed_ref[...] = normed
    packed_ref[...] = dot(normed, attn_ref[:, :QKV], (1, 0)).astype(bf16)
    low = first_head()
    for pair in range(OUT // PAIR):
        col = pair * PAIR
        query = packed_ref[:, col : col + PAIR]
        key = packed_ref[:, OUT + col : OUT + col + PAIR]
        value = packed_ref[:, 2 * OUT + col : 2 * OUT + col + PAIR]
        none = jnp.zeros_like(query)
        parts = []
        for head in range(2):
            mine = low if head == 0 else ~low
            probs = head_probs(jnp.where(mine, query, none), key).astype(bf16)
            parts.append(dot(probs, value, (1, 0)))
        context_ref[:, col : col + PAIR] = jnp.where(low, parts[0], parts[1]).astype(bf16)
    part_ref[...] = dot(context_ref[...], attn_ref[:, QKV : QKV + OUT], (1, 1)).astype(bf16)
    if len(rest) > 2:
        moe.wait()


VMEM = pl.BlockSpec(memory_space=pltpu.VMEM)
HBM = pl.BlockSpec(memory_space=pltpu.HBM)


def attend(inputs, weights, at, with_experts):
    shape = jax.ShapeDtypeStruct
    return pl.pallas_call(
        functools.partial(attend_kernel, at),
        in_specs=[VMEM, HBM],
        out_specs=(VMEM,) * 6,
        out_shape=(
            shape((LEN, D), bf16),
            shape((LEN, D), bf16),
            shape((LEN, QKV), bf16),
            shape((LEN, OUT), bf16),
            shape((8, D), f32),
            shape((D, MOE if with_experts else SENT), bf16),
        ),
        scratch_shapes=([pltpu.VMEM((D, SENT), bf16)] if with_experts else [])
        + [pltpu.SemaphoreType.DMA((2,))],
        compiler_params=pltpu.CompilerParams(vmem_limit_bytes=24 * 2**20),
        cost_estimate=pl.CostEstimate(
            flops=2 * LEN * D * (QKV + OUT), bytes_accessed=6 * 2**20, transcendentals=6 * LEN * LEN
        ),
        name="attend",
    )(inputs, pltpu.with_memory_space_constraint(weights, pltpu.HBM))


def attend_back_kernel(
    fetched, grad_ref, weights_ref, packed_ref, part_ref, grads_ref, heads_ref, *rest
):
    attn_ref = weights_ref
    if fetched:
        attn_ref, sem = rest
        copy = pltpu.make_async_copy(weights_ref.at[:, pl.ds(0, SENT)], attn_ref, sem)
        copy.start()
        copy.wait()
    heads_ref[...] = dot(grad_ref[...], attn_ref[:, QKV : QKV + OUT], (1, 0)).astype(bf16)
    low = first_head()
    for pair in range(OUT // PAIR):
        at = pair * PAIR
        query = packed_ref[:, at : at + PAIR]
        key = packed_ref[:, OUT + at : OUT + at + PAIR]
        value = packed_ref[:, 2 * OUT + at : 2 * OUT + at + PAIR]
        grad = heads_ref[:, at : at + PAIR]
        none = jnp.zeros_like(query)
        found = []
        for head in range(2):
            mine = low if head == 0 else ~low
            probs = head_probs(jnp.where(mine, query, none), key)
            grad_probs = dot(jnp.where(mine, grad, none), value, (1, 1))
            inner = jnp.sum(grad_probs * probs, axis=-1, keepdims=True)
            grad_scores = (probs * (grad_probs - inner)).astype(bf16)
            found.append(
                (
                    dot(grad_scores, key, (1, 0)) * SCALE,
                    dot(grad_scores, query, (0, 0)) * SCALE,
                    dot(probs.astype(bf16), grad, (0, 0)),
                )
            )
        for j in range(3):
            both = jnp.where(low, found[0][j], found[1][j]).astype(bf16)
            grads_ref[:, j * OUT + at : j * OUT + at + PAIR] = both
    part_ref[...] = dot(grads_ref[...], attn_ref[:, :QKV], (1, 1)).astype(bf16)


def attend_back(grad, attn, packed, fetched):
    shape = jax.ShapeDtypeStruct
    scratch = [pltpu.VMEM((LEN, OUT), bf16)]
    if fetched:
        scratch += [pltpu.VMEM((D, SENT), bf16), pltpu.SemaphoreType.DMA]
        attn = pltpu.with_memory_space_constraint(attn, pltpu.HBM)
    return pl.pallas_call(
        functools.partial(attend_back_kernel, fetched),
        in_specs=[VMEM, HBM if fetched else VMEM, VMEM],
        out_specs=(VMEM, VMEM),
        out_shape=(shape((LEN, D), bf16), shape((LEN, QKV), bf16)),
        scratch_shapes=scratch,
        compiler_params=pltpu.CompilerParams(vmem_limit_bytes=24 * 2**20),
        cost_estimate=pl.CostEstimate(
            flops=2 * LEN * D * (QKV + OUT), bytes_accessed=6 * 2**20, transcendentals=6 * LEN * LEN
        ),
        name="attend_back",
    )(grad, attn, packed)


TILE = 256


def expert_grads_kernel(at, filled_ref, hidden_ref, slots_ref, active_ref, *rest):
    out_ref, tiles, sems = rest[-3:]
    copies = []
    for i in range(D // TILE):
        rows = slice(i * TILE, (i + 1) * TILE)
        tiles[rows, :FFH] = dot(filled_ref[:, rows], hidden_ref[...], (0, 0)).astype(bf16)
        tiles[rows, FFH:] = dot(slots_ref[:, rows], active_ref[...], (0, 0)).astype(bf16)
        copy = pltpu.make_async_copy(
            tiles.at[pl.ds(i * TILE, TILE)],
            out_ref.at[pl.ds(i * TILE, TILE), pl.ds(at, MOE)],
            sems.at[i],
        )
        copy.start()
        copies.append(copy)
    for copy in copies:
        copy.wait()


def attend_grads_kernel(at, normed_ref, grads_ref, proj_ref, context_ref, small_ref, *rest):
    out_ref, tiles, sems = rest[-3:]
    tiles[:, :QKV] = dot(normed_ref[...], grads_ref[...], (0, 0)).astype(bf16)
    tiles[:, QKV : QKV + OUT] = dot(proj_ref[...], context_ref[...], (0, 0)).astype(bf16)
    rows = jnp.concatenate([small_ref[...], jnp.zeros((120, D), f32)], axis=0)
    tiles[:, QKV + OUT : QKV + OUT + 128] = jnp.transpose(rows).astype(bf16)
    tiles[:, QKV + OUT + 128 :] = jnp.zeros((D, SMALL - 128), bf16)
    copy = pltpu.make_async_copy(tiles, out_ref.at[:, pl.ds(at, tiles.shape[1])], sems.at[0])
    copy.start()
    copy.wait()


def grads_into(kernel, name, columns, operands, buffer, width, at):
    count = len(operands)
    if buffer is not None:
        operands = operands + [buffer]
    return pl.pallas_call(
        functools.partial(kernel, at),
        in_specs=[VMEM] * count + [HBM] * (len(operands) - count),
        out_specs=HBM,
        out_shape=pltpu.HBM((D, width), bf16),
        scratch_shapes=[
            pltpu.VMEM((D, columns), bf16),
            pltpu.SemaphoreType.DMA((D // TILE,)),
        ],
        input_output_aliases={} if buffer is None else {count: 0},
        compiler_params=pltpu.CompilerParams(vmem_limit_bytes=24 * 2**20),
        cost_estimate=pl.CostEstimate(
            flops=2 * E * PAD * D * columns, bytes_accessed=9 * 2**20, transcendentals=0
        ),
        name=name,
    )(*operands)


def expert_grads(operands, buffer, width, at):
    return grads_into(expert_grads_kernel, "expert_grads", MOE, operands, buffer, width, at)


def attend_grads(operands, buffer, width, at):
    return grads_into(attend_grads_kernel, "attend_grads", ATTN, operands, buffer, width, at)


def quarter_grads_kernel(normed_ref, grads_ref, proj_ref, context_ref, small_ref, out_ref):
    found = dot(normed_ref[...], grads_ref[...], (0, 0)).astype(bf16)
    for j in range(3):
        out_ref[j, :D] = found[:, j * QUARTER : (j + 1) * QUARTER]
    out_ref[3, :D] = dot(proj_ref[...], context_ref[...], (0, 0)).astype(bf16)
    for j in range(4):
        out_ref[j, D:] = small_ref[...]


def quarter_grads(normed, grads, proj, context, small):
    return pl.pallas_call(
        quarter_grads_kernel,
        in_specs=[VMEM] * 5,
        out_specs=VMEM,
        out_shape=jax.ShapeDtypeStruct((4, D + 16, QUARTER), bf16),
        compiler_params=pltpu.CompilerParams(vmem_limit_bytes=24 * 2**20),
        cost_estimate=pl.CostEstimate(
            flops=2 * LEN * D * (QKV + OUT), bytes_accessed=5 * 2**20, transcendentals=0
        ),
        name="quarter_grads",
    )(normed, grads, proj, context, small)


def attention(inputs, weights, at, onehot, with_experts):
    part, normed, packed, context, small, last = attend(inputs, weights, at, with_experts)
    g_moe, w_router = small[1:2], small[2 : 2 + E].astype(bf16)
    middle = inputs + pair_sum(part)
    scale_mid = rms_scale(middle)
    mixed = (middle * scale_mid * g_moe).astype(bf16)
    logits = matmul(mixed, w_router, (1, 1))
    exponent = jnp.exp(logits - jnp.max(logits, axis=-1, keepdims=True))
    router_probs = exponent / jnp.sum(exponent, axis=-1, keepdims=True)
    gate = jnp.sum(onehot * router_probs, axis=-1, keepdims=True)
    attn = None if with_experts else last
    kept = (
        inputs, small, normed, packed, context, middle, scale_mid, mixed, router_probs, gate, attn,
    )
    return (kept, last) if with_experts else kept


def experts(filled, w_in, w_down):
    hidden = matmul(filled, w_in, (1, 0))
    cdf = 0.5 * (1.0 + lax.erf(hidden * (1.0 / math.sqrt(2.0))))
    activated = (hidden * cdf).astype(bf16)
    slope = cdf + hidden * jnp.exp(-0.5 * hidden * hidden) * (1.0 / math.sqrt(2.0 * math.pi))
    return activated, slope, matmul(activated, w_down, (1, 1)).astype(bf16)


def experts_back(grad_slots, slope, w_in, w_down):
    grad_hidden = (matmul(grad_slots, w_down, (1, 0)) * slope).astype(bf16)
    return grad_hidden, matmul(grad_hidden, w_in, (1, 1)).astype(bf16)


def to_slots(table, rows):
    return matmul(table, rows, (1, 0)).astype(bf16)


def from_slots(table, slots):
    return matmul(table, slots, (0, 0)).astype(bf16)


def mixed_back(grad_out, grad_mixed, combined, onehot, kept):
    inputs, small, normed, packed, context, middle, scale_mid, mixed, router_probs, gate, attn = kept
    grad_gate = jnp.sum(grad_out * combined, axis=-1, keepdims=True)
    grad_logits = router_probs * (onehot - gate) * grad_gate
    grad_w_router = lax.dot_general(
        grad_logits, mixed.astype(f32), (((0,), (0,)), ((), ())), precision=lax.Precision.HIGHEST
    )
    g_moe, w_router = small[1:2], small[2 : 2 + E]
    back_rows = sum(grad_logits[:, e : e + 1] * w_router[e][None, :] for e in range(E))
    grad_norm, grad_g_moe = norm_back(grad_mixed + back_rows, middle, scale_mid, g_moe)
    return grad_out + grad_norm, grad_w_router, grad_g_moe


def attention_back(grad_middle, kept, attn, grad_w_router, grad_g_moe):
    inputs, small, normed, packed, context = kept[:5]
    proj = grad_middle.astype(bf16)
    part, grads = attend_back(proj, kept[-1] if attn is None else attn, packed, attn is not None)
    grad_normed = pair_sum(part)
    grad_norm, grad_g_attn = norm_back(grad_normed, inputs, rms_scale(inputs), small[:1])
    rows = jnp.concatenate(
        [grad_g_attn[None], grad_g_moe[None], grad_w_router, jnp.zeros((6 - E, D), f32)], axis=0
    )
    return grad_middle + grad_norm, [normed, grads, proj, context], rows


def by_layer(p, near, far):
    return jnp.where(p == 0, near, far), jnp.where(p == 0, far, near)


def on_device(tokens, cotangent, routes, g_attn, w_qkv, w_out, g_moe, w_router, w_in, w_down):
    p, c, t = lax.axis_index("pipe"), lax.axis_index("core"), lax.axis_index("tensor")
    chip = p * 2 + t

    def spread(chunk_of):
        got = []
        for k in range(4):
            k1, k0 = k >> 1, k & 1
            got.append(column_send(chunk_of(k), lambda p, c, t: (p ^ k1, t, c ^ k0)))
        layers = []
        for first, second in ((by_layer(p, got[0], got[2])), (by_layer(p, got[1], got[3]))):
            layers.append((first, second))
        return [
            jnp.concatenate(
                [
                    jnp.where(t == 0, layers[0][l], layers[1][l]),
                    jnp.where(t == 0, layers[1][l], layers[0][l]),
                ],
                axis=0,
            )
            for l in range(2)
        ]

    small = jnp.concatenate([g_attn[0][:, None], g_moe[0][:, None], w_router[0]], axis=1)
    small = jnp.pad(small, ((0, 0), (0, 128 - small.shape[1])))

    def chunk_of(k):
        expert = (p * 2 + c) ^ k
        return jnp.concatenate(
            [
                w_qkv[0].reshape(-1, QKV),
                w_out[0],
                small,
                lax.dynamic_index_in_dim(w_in[0], expert, 0, keepdims=False),
                lax.dynamic_index_in_dim(w_down[0], expert, 0, keepdims=False),
            ],
            axis=1,
        )

    blocks = spread(chunk_of)
    weights = lax.all_gather(
        jnp.concatenate([blocks[0], blocks[1][:, :SENT]], axis=1), ("x", "y"), axis=0, tiled=True
    )
    late = lax.all_gather(blocks[1][:, SENT:], ("x", "y"), axis=0, tiled=True)

    def to_owner(rows):
        got = [column_send(rows, lambda p, c, t, j=j: (p, t ^ j, c)) for j in range(2)]
        return jnp.where(c == 0, got[0], got[1]), jnp.where(c == 0, got[1], got[0])

    own_routes = routes[0, :, :, 0].astype(bf16)
    far_routes = lax.ppermute(own_routes, "pipe", [(0, 1), (1, 0)])
    route_pair = jnp.stack(by_layer(p, own_routes, far_routes))
    route_rows = lax.dynamic_index_in_dim(route_pair, p, 1, keepdims=False)
    own_tokens = lax.dynamic_index_in_dim(tokens, p, 0, keepdims=False)
    extra = jnp.pad(route_rows.reshape(1, 2 * HALF), ((0, 15), (0, D - 2 * HALF)))
    low_rows, high_rows = to_owner(jnp.concatenate([own_tokens, extra], axis=0))
    inputs = jnp.concatenate([low_rows[:HALF], high_rows[:HALF]], axis=0).astype(f32)
    tables, onehots = [], []
    earlier = (
        lax.broadcasted_iota(jnp.int32, (LEN, LEN), 0)
        < lax.broadcasted_iota(jnp.int32, (LEN, LEN), 1)
    ).astype(bf16)
    for l in range(2):
        cut = slice(l * HALF, (l + 1) * HALF)
        ids = jnp.concatenate([low_rows[HALF, cut], high_rows[HALF, cut]]).astype(jnp.int32)
        picks = (ids[None, :] == jnp.arange(E, dtype=jnp.int32)[:, None]).astype(f32)
        before = matmul(picks.astype(bf16), earlier, (1, 0))
        rank = jnp.sum(before * picks, axis=0).astype(jnp.int32)
        place = (-(ids ^ chip) & 3) * PAD + rank
        tables.append(
            (place[None, :] == jnp.arange(E * PAD, dtype=jnp.int32)[:, None]).astype(bf16)
        )
        onehots.append(picks.T)

    cot_rows = lax.dynamic_index_in_dim(cotangent, p, 0, keepdims=False)
    grad_out = jnp.concatenate(to_owner(cot_rows), axis=0).astype(f32)

    inputs, grad_out = lax.optimization_barrier((inputs, grad_out))
    in_second, down_second = late[:, :FFH], late[:, FFH:]

    first, moe_weights = attention(inputs, weights, 0, onehots[0], True)
    in_first, down_first = moe_weights[:, :FFH], moe_weights[:, FFH:]
    filled_first = to_experts(to_slots(tables[0], first[7]))
    active_first, slope_first, out_slots = experts(filled_first, in_first, down_first)
    combined_first = pair_sum(from_slots(tables[0], to_experts(out_slots)))
    first_out = (first[5] + first[9] * combined_first).astype(bf16)

    second = attention(
        first_out.astype(f32), weights, SENT + MOE, onehots[1], False
    )
    filled, grad_slots = to_experts(
        to_slots(tables[1], second[7]),
        to_slots(tables[1], (second[9] * grad_out).astype(bf16)),
    )
    activated, slope, out_slots = experts(filled, in_second, down_second)
    grad_hidden, grad_filled = experts_back(grad_slots, slope, in_second, down_second)
    width = 2 * MOE + ATTN
    found = to_experts(out_slots, grad_filled)
    buffer = expert_grads([filled, grad_hidden, grad_slots, activated], None, width, 0)
    found, buffer = lax.optimization_barrier((found, buffer))
    sums = pair_sum(jnp.concatenate([from_slots(tables[1], rows) for rows in found], axis=1))
    combined, grad_mixed = sums[:, :D], sums[:, D:]
    second_out = (second[5] + second[9] * combined).astype(bf16)

    def to_home(first, second):
        cut = lambda rows: lax.dynamic_slice_in_dim(rows, c * HALF, HALF, 0)
        near, far = by_layer(p, cut(first), cut(second))
        near = column_send(near, lambda p, c, t: (p, t, c))
        far = column_send(far, lambda p, c, t: (1 - p, t, c))
        return jnp.stack(by_layer(p, near, far))

    def reduce_plane(whole):
        return lax.optimization_barrier(
            lax.psum_scatter(whole, ("x", "y"), scatter_dimension=0, tiled=True)
        )

    grad_mid, g_router, gg_moe = mixed_back(grad_out, grad_mixed, combined, onehots[1], second)
    grad_x, operands, rows = attention_back(grad_mid, second, None, g_router, gg_moe)
    buffer = attend_grads(operands + [rows], buffer, width, MOE)
    second_grad = grad_x.astype(bf16)
    grad_out = second_grad.astype(f32)
    grad_slots = to_experts(to_slots(tables[0], (first[9] * grad_out).astype(bf16)))
    grad_hidden, grad_filled = experts_back(grad_slots, slope_first, in_first, down_first)
    grad_filled = to_experts(grad_filled)
    buffer = expert_grads(
        [filled_first, grad_hidden, grad_slots, active_first], buffer, width, MOE + ATTN
    )
    reduced = reduce_plane(buffer)
    grad_filled, buffer = lax.optimization_barrier((grad_filled, buffer))
    grad_mixed = pair_sum(from_slots(tables[0], grad_filled))
    grad_mid, g_router, gg_moe = mixed_back(
        grad_out, grad_mixed, combined_first, onehots[0], first
    )
    grad_x, operands, rows = attention_back(grad_mid, first, weights, g_router, gg_moe)
    quarters = quarter_grads(*operands, rows.astype(bf16).reshape(16, QUARTER))
    first_out, second_out, grad_x = lax.optimization_barrier((first_out, second_out, grad_x))
    total = 0.0
    for k in range(4):
        part = lax.dynamic_index_in_dim(quarters, chip ^ k, 0, keepdims=False)
        total = total + (part if k == 0 else chip_swap(part, k)).astype(f32)
    small_columns = jnp.pad(total[D:].reshape(8, D).T, ((0, 0), (0, 120)))
    attn_whole = jnp.concatenate([total[:D], small_columns], axis=1).astype(bf16)
    attn_first = scatter_axis(scatter_first(attn_whole, "x"), "y", 0)
    hidden_states = to_home(first_out, second_out)
    grad_inputs = to_home(grad_x.astype(bf16), second_grad).astype(f32)

    widened = jnp.pad(attn_first, ((0, 0), (0, ATTN - attn_first.shape[1])))
    attn_sum = jnp.zeros((24, ATTN), f32)
    attn_all = jnp.zeros((24, 4 * QUARTER), bf16)
    moe_all = jnp.zeros((E, 24, MOE), bf16)
    for k in range(4):
        k1, k0 = k >> 1, k & 1
        to_first = (p ^ k1) == 0
        piece = jnp.concatenate(
            [
                jnp.where(to_first, reduced[:, MOE + ATTN :], reduced[:, :MOE]),
                jnp.where(to_first, widened, reduced[:, MOE : MOE + ATTN]),
            ],
            axis=1,
        )
        piece = jnp.where(t == k0, piece[:24], piece[24:])
        got = column_send(piece, lambda p, c, t: (p ^ k1, t ^ k0, c))
        source = (p * 2 + c) ^ k
        moe_all = lax.dynamic_update_index_in_dim(moe_all, got[:, :MOE], source, 0)
        attn_sum = attn_sum + got[:, MOE:].astype(f32)
        attn_all = lax.dynamic_update_slice_in_dim(
            attn_all, got[:, MOE : MOE + QUARTER], source * QUARTER, 1
        )
        first_small = got[:, MOE + QUARTER : MOE + QUARTER + 128].astype(f32)
    attn_grad = jnp.where(p == 0, attn_all.astype(f32), attn_sum[:, : QKV + OUT])
    small = jnp.where(p == 0, first_small, attn_sum[:, QKV + OUT : QKV + OUT + 128])
    return (
        hidden_states[None],
        grad_inputs[None],
        small[:, 0][None],
        attn_grad[:, :QKV].reshape(24, 3, OUT)[None],
        attn_grad[:, QKV : QKV + OUT][None],
        small[:, 1][None],
        small[:, 2 : 2 + E][None],
        moe_all[:, :, :FFH].astype(f32)[None],
        moe_all[:, :, FFH:].astype(f32)[None],
    )


def solution(mesh):
    grid = Mesh(mesh.devices.reshape(2, 4, 4, 2, 2), ("pipe", "x", "y", "core", "tensor"))
    dp = ("x", "y", "core")
    return jax.shard_map(
        on_device,
        mesh=grid,
        in_specs=(
            P(dp, "tensor", None),
            P(dp, "tensor", None),
            P("pipe", dp, "tensor", None),
            P("pipe", dp),
            P("pipe", dp, None, "tensor"),
            P("pipe", dp, "tensor"),
            P("pipe", dp),
            P("pipe", dp, None),
            P("pipe", None, dp, "tensor"),
            P("pipe", None, dp, "tensor"),
        ),
        out_specs=(
            P("pipe", dp, "tensor", None),
            P("pipe", dp, "tensor", None),
            P("pipe", dp),
            P("pipe", dp, None, "tensor"),
            P("pipe", dp, "tensor"),
            P("pipe", dp),
            P("pipe", dp, None),
            P("pipe", None, dp, "tensor"),
            P("pipe", None, dp, "tensor"),
        ),
        check_vma=False,
    )
```
